512 devices in a mesh: dp: 128 (over z, y, core), tensor: 4 (over x).
Axes of the slice: x: 4, y: 8, z: 8, core: 2. Of those that a mesh axis runs over, the one named last changes fastest.
Arguments:
- head_output: bfloat16 [49152, 1536], P('dp', 'tensor'), may hold values from -6 to 6
- out_weight: bfloat16 [1536, 1536], P('tensor'), may hold values from -0.15625 to 0.15625
- block_cotangent: bfloat16 [49152, 1536], P('dp'), may hold values from -6 to 6
- error_memory: bfloat16 [128, 1536, 1536], P('dp', 'tensor'), may hold values from -96 to 96
- right_factor: float32 [1536, 64], replicated, may hold values from -0.15625 to 0.15625
- gate_table: bfloat16 [64, 1536], replicated, may hold values from -6 to 6
- sample_weight: float32 [64], replicated, may hold values from 0.5 to 2
- time_bins: int32 [384], P('dp'), may hold values from 0 to 63
- token_loss: float32 [49152], P('dp'), as said below
- loss_bins: int32 [49152], P('dp'), may hold values from 0 to 63
Outputs:
- head_grad: bfloat16 [49152, 1536], P('dp', 'tensor')
- left_basis: float32 [1536, 64], P('tensor')
- new_right: float32 [1536, 64], P('tensor')
- gate_grad: float32 [64, 1536], P(None, 'tensor')
- loss_histogram: float32 [64], replicated
The draws below stay inside these ranges and needn't reach their ends.
Inputs may be any that keep to these rules, and one draw needn't show every extreme that they name: `token_loss`: positive losses.
All inputs are finite; a program needn't handle non-finite values.
Results may differ from the reference program's by a relative error of at most 0.0049.
Values sent between devices are 32-bit elements; how exact they have to be, the bound alone decides.
A program may use at most 64 MiB of HBM per device.

```python
import math
import jax
import jax.numpy as jnp
import numpy as np
from jax import lax

D = 1536
RANK = 64
NBINS = 64
TOK_LAT = 128
HA = 1536
TOK_DEV = 384
WORKERS = 128
LATENTS = 384
TOKENS = 49152


def draw_token_loss(key, part):
    key = jax.random.fold_in(key, 11)
    rows = jnp.arange(TOKENS)
    worker = (rows // TOK_DEV).astype(jnp.float32)
    count = max(TOKENS // TOK_DEV - 1, 1)
    ramp = 1.0 + 2.0 * worker / count
    base = jnp.exp(jax.random.uniform(key, (TOKENS,), jnp.float32, -0.7, 0.7))
    return base * ramp


def set_ends(array, key, low, top_value):
    index_at = [jax.random.randint(jax.random.fold_in(key, axis), (), 0, length) for axis, length in enumerate(array.shape)]
    main_axis = array.shape.index(max(array.shape))
    neighbour = index_at[:main_axis] + [(index_at[main_axis] + 1) % array.shape[main_axis]] + index_at[main_axis + 1:]
    return array.at[tuple(index_at)].set(low).at[tuple(neighbour)].set(top_value)


def block_levels(key, shape, cuts, low, top_value):
    loudness, own = 1.0, jax.random.fold_in(key, 6)
    for axis_at, blocks in cuts:
        heights = jnp.exp(jax.random.uniform(jax.random.fold_in(own, axis_at), (blocks,), jnp.float32, low / len(cuts), top_value / len(cuts)))
        loudness = loudness * jnp.repeat(heights, shape[axis_at] // blocks).reshape([-1 if axis == axis_at else 1 for axis in range(len(shape))])
    return loudness


def rank_table(count, skew):
    portions = [(1 << 20) // math.isqrt(grade ** skew) + 1 for grade in range(1, count + 1)]
    spread = 1 + sum(portions) // (1 << 30)
    return np.cumsum(np.array([max(1, weight // spread) for weight in portions]))


def ranked(own_key, extent, number_of, skew):
    listing = rank_table(number_of, skew)
    ticket = jax.random.randint(jax.random.fold_in(own_key, 1), extent, 0, int(listing[number_of - 1]))
    standing = jnp.searchsorted(jnp.asarray(listing, jnp.int32), ticket, side="right")
    return jax.random.permutation(jax.random.fold_in(own_key, 2), number_of)[standing].astype(jnp.int32)


def centred(stream_key, extent, width, limit, split=(), held_as=jnp.bfloat16):
    result = width * jax.random.normal(stream_key, extent, jnp.float32)
    if split:
        result = result * block_levels(stream_key, extent, split, -0.22, 0.18)
    return jnp.clip(result, -limit, limit).astype(held_as)


def setup_inputs(seed: int = 0) -> dict:
    key_list = jax.random.split(jax.random.key(seed), 11)
    head_output = centred(key_list[0], (TOKENS, HA), 1.0, 6.0, ((0, 128), (1, 4)))
    out_weight = centred(key_list[1], (HA, D), HA ** -0.5, 0.15625, ((0, 4),))
    block_cotangent = centred(key_list[2], (TOKENS, D), 1.0, 6.0, ((0, 128),))
    error_memory = centred(key_list[3], (WORKERS, HA, D), 16.0, 96.0, ((0, 128), (1, 4)))
    right_factor = centred(key_list[4], (D, RANK), D ** -0.5, 0.15625, (), jnp.float32)
    gate_table = centred(key_list[5], (NBINS, D), 1.0, 6.0)
    sample_weight = jnp.clip(jnp.exp(jax.random.uniform(key_list[6], (NBINS,), jnp.float32, math.log(0.5), math.log(2.0))), 0.5, 2.0)
    time_bins = set_ends(ranked(key_list[7], (LATENTS,), NBINS, 1), jax.random.fold_in(key_list[7], 3), 0, NBINS - 1).astype(jnp.int32)
    token_loss = draw_token_loss(jax.random.fold_in(key_list[10], 71), 0)
    loss_bins = set_ends(jax.random.randint(key_list[9], (TOKENS,), 0, NBINS), jax.random.fold_in(key_list[9], 1), 0, NBINS - 1).astype(jnp.int32)
    return dict(head_output=head_output, out_weight=out_weight, block_cotangent=block_cotangent, error_memory=error_memory, right_factor=right_factor, gate_table=gate_table, sample_weight=sample_weight, time_bins=time_bins, token_loss=token_loss, loss_bins=loss_bins)


def reference(head_output, out_weight, block_cotangent, error_memory, right_factor, gate_table, sample_weight, time_bins, token_loss, loss_bins):
    highest = lax.Precision.HIGHEST
    lat_weight = sample_weight[time_bins]
    lat_gate = gate_table[time_bins].astype(jnp.float32)
    scaled = lat_weight[:, None] * lat_gate
    cotangent = block_cotangent.astype(jnp.float32).reshape(LATENTS, TOK_LAT, D)
    gated = (cotangent * scaled[:, None, :]).reshape(TOKENS, D).astype(jnp.bfloat16)
    head_grad = jnp.dot(gated.astype(jnp.float32), out_weight.T.astype(jnp.float32), preferred_element_type=jnp.float32).astype(jnp.bfloat16)
    branch = jnp.dot(head_output.astype(jnp.float32), out_weight.astype(jnp.float32), preferred_element_type=jnp.float32)
    products = (cotangent * branch.reshape(LATENTS, TOK_LAT, D)).sum(axis=1)
    lat_gate_grad = lat_weight[:, None] * products
    bin_table = (time_bins[:, None] == jnp.arange(NBINS)[None, :]).astype(jnp.float32)
    gate_grad = jnp.dot(bin_table.T, lat_gate_grad, precision=highest)

    def merged_for(index):
        start = (index * TOK_DEV).astype(jnp.int32)
        rows = lax.dynamic_slice_in_dim(head_output, start, TOK_DEV, 0)
        grads = lax.dynamic_slice_in_dim(gated, start, TOK_DEV, 0)
        local = jnp.dot(rows.T.astype(jnp.float32), grads.astype(jnp.float32), preferred_element_type=jnp.float32)
        return local + error_memory[index].astype(jnp.float32)

    def left_step(total, index):
        return (total + jnp.dot(merged_for(index), right_factor, precision=highest), None)
    workers = jnp.arange(WORKERS, dtype=jnp.int32)
    left, _ = lax.scan(left_step, jnp.zeros((HA, RANK), jnp.float32), workers)
    left = left / WORKERS
    gram = jnp.dot(left.T, left, precision=highest)
    chol = jnp.linalg.cholesky(gram)
    left_basis = jax.scipy.linalg.solve_triangular(chol, left.T, lower=True).T

    def right_step(total, index):
        return (total + jnp.dot(merged_for(index).T, left_basis, precision=highest), None)
    new_right, _ = lax.scan(right_step, jnp.zeros((D, RANK), jnp.float32), workers)
    new_right = new_right / WORKERS
    token_weight = jnp.repeat(lat_weight, TOK_LAT) * token_loss
    token_table = (loss_bins[:, None] == jnp.arange(NBINS)[None, :]).astype(jnp.float32)
    loss_histogram = jnp.dot(token_weight, token_table, precision=highest) * (NBINS / TOKENS)
    return (head_grad, left_basis, new_right, gate_grad, loss_histogram)
```

```python
import functools
import math

import jax
import jax.numpy as jnp
from jax import lax
from jax.experimental import pallas as pl
from jax.experimental.pallas import tpu as pltpu
from jax.sharding import PartitionSpec as P

MESH = pl.DeviceIdType.MESH
F32 = jnp.float32
BF16 = jnp.bfloat16
HIGHEST = lax.Precision.HIGHEST
NN = (((1,), (0,)), ((), ()))
NT = (((1,), (1,)), ((), ()))


def split(x):
    high = x.astype(BF16)
    low = (x - high.astype(F32)).astype(BF16)
    return jnp.concatenate([high, low], axis=0)


def fold(x):
    half = x.shape[0] // 2
    return x[:half] + x[half:]


def eliminate(rows, begin, end):
    groups = len(rows)
    width = rows[0].shape[1]
    sub = lax.broadcasted_iota(jnp.int32, (8, width), 0)
    rows = list(rows)
    for j in range(begin, end):
        g, r = divmod(j, 8)
        cols = [jnp.broadcast_to(rows[i][:, j : j + 1], (8, width)) for i in range(g, groups)]
        pivot = cols[0][r : r + 1]
        scaled = jnp.broadcast_to(rows[g][r : r + 1] / pivot, (8, width))
        for i in range(g, groups):
            factor = cols[i - g]
            if i == g:
                factor = jnp.where(sub > r, factor, 0.0)
            rows[i] = rows[i] - factor * scaled
    return rows


def unscaled_to_inverse(rows, rank):
    out = []
    width = rows[0].shape[1]
    lane = lax.broadcasted_iota(jnp.int32, (8, width), 1)
    sub = lax.broadcasted_iota(jnp.int32, (8, width), 0)
    for g, x in enumerate(rows):
        diag = jnp.sum(jnp.where(lane == sub + 8 * g, x, 0.0), axis=1, keepdims=True)
        out.append(x / jnp.sqrt(diag))
    return jnp.concatenate(out, axis=0)


def main_kernel(
    n, nx, workers,
    tb_ref, sw_ref,
    head_hbm, weight_hbm, cot_hbm, err_hbm, right_hbm, gate_hbm, loss_hbm, bins_hbm,
    left_o, s_o, inv_o, gate_o, grad_o,
    head, weight, cot, err, right, gate, loss, bins, load_sem,
    gated, rstack, scale, grad_v, total, own_s, sib_s,
    l_src, l_in, l_mid, l_all,
    g_src, g_in, g_mid, g_all,
    s_src, s_in, s_x, s_xin, s_mid, s_all,
    t_src, t_in, gram, chol,
    ssem, rsem, out_sem,
):
    rank = right.shape[0]
    tokens, feats = head.shape
    width = cot.shape[1]
    latents, per = loss.shape
    nbins = gate.shape[0]
    share = width // nx
    half = rank // 2
    piece = half // n
    pairs = 2 * n

    index = lax.axis_index("dp")
    x = lax.axis_index("tensor")
    c = lax.rem(index, 2)
    y = lax.rem(index // 2, n)
    z = index // (2 * n)

    def at_z(j, core):
        return ((j * n + y) * 2 + core, x)

    def at_y(j, core):
        return ((z * n + j) * 2 + core, x)

    a = jnp.where(c == 0, z, y)
    b = jnp.where(c == 0, y, z)

    def at_a(j, core):
        return (jnp.where(c == 0, j * n + y, z * n + j) * 2 + core, x)

    def at_b(j):
        return (jnp.where(c == 0, z * n + j, j * n + y) * 2 + c, x)

    sibling = (index + 1 - 2 * c, x)

    barrier = pltpu.get_barrier_semaphore()

    def greet(device):
        pl.semaphore_signal(barrier, inc=1, device_id=device, device_id_type=MESH)

    def greet_ring(k, carry):
        jz = lax.rem(z + k, n)
        jy = lax.rem(y + k, n)
        for core in (0, 1):
            greet(at_z(jz, core))
            greet(at_y(jy, core))
        return carry

    lax.fori_loop(1, n, greet_ring, 0)
    greet(sibling)

    def greet_x(k, carry):
        greet((index, lax.rem(x + k, nx)))
        return carry

    lax.fori_loop(1, nx, greet_x, 0)

    loads = []
    for k, (src, dst) in enumerate(
        (
            (right_hbm, right),
            (gate_hbm, gate),
            (err_hbm.at[0], err),
            (cot_hbm, cot),
            (head_hbm, head),
            (loss_hbm, loss),
            (bins_hbm, bins),
            (weight_hbm, weight),
        )
    ):
        loads.append(pltpu.make_async_copy(src, dst, load_sem.at[k]))
        loads[-1].start()

    def remote(src, dst, phase, device):
        return pltpu.make_async_remote_copy(
            src_ref=src, dst_ref=dst, send_sem=ssem.at[phase], recv_sem=rsem.at[phase],
            device_id=device, device_id_type=MESH,
        )

    def scatter_send(src, dst, phase):
        def step(k, carry):
            jz = lax.rem(z + k, n)
            jy = lax.rem(y + k, n)
            remote(src.at[jz], dst.at[z * 2 + c], phase, at_z(jz, 0)).start()
            remote(src.at[n + jy], dst.at[y * 2 + c], phase, at_y(jy, 1)).start()
            return carry

        lax.fori_loop(1, n, step, 0)

        @pl.when(c == 1)
        def _():
            remote(src.at[z], dst.at[z * 2 + 1], phase, sibling).start()

        @pl.when(c == 0)
        def _():
            remote(src.at[n + y], dst.at[y * 2], phase, sibling).start()

        dst[a * 2 + c] = src[c * n + a]

    def wait_many(ref, count, phase, recv=True):
        part = ref.at[pl.ds(0, count)]
        copy = remote(part, part, phase, sibling)
        if recv:
            copy.wait_recv()
        else:
            copy.wait_send()

    def sum_slots(ref):
        out = ref[0]
        for k in range(1, ref.shape[0]):
            out = out + ref[k]
        return out

    def ring_send(ref, phase):
        def step(k, carry):
            j = lax.rem(b + k, n)
            remote(ref.at[b], ref.at[b], phase, at_b(j)).start()
            return carry

        lax.fori_loop(1, n, step, 0)

    def gather_send(ref, phase):
        mine = c * n + a

        def step(k, carry):
            j = lax.rem(a + k, n)
            for core in (0, 1):
                remote(ref.at[mine], ref.at[mine], phase, at_a(j, core)).start()
            return carry

        remote(ref.at[mine], ref.at[mine], phase, sibling).start()
        lax.fori_loop(1, n, step, 0)

    def x_send(src, dst, phase):
        def step(k, carry):
            j = lax.rem(x + k, nx)
            remote(src.at[j], dst.at[x], phase, (index, j)).start()
            return carry

        lax.fori_loop(1, nx, step, 0)

    loads[0].wait()
    rstack[...] = split(right[...])
    loads[1].wait()
    bin_of = lax.broadcasted_iota(jnp.int32, (8, nbins), 1)
    row_of = lax.broadcasted_iota(jnp.int32, (8, nbins), 0)
    onehot = jnp.zeros((8, nbins), F32)
    weights = []
    for l in range(latents):
        tb = tb_ref[l]
        weights.append(sw_ref[tb])
        onehot = jnp.where((row_of == l) & (bin_of == tb), 1.0, onehot)
    gates = lax.dot_general(onehot.astype(BF16), gate[...], NN, preferred_element_type=F32)
    row8 = lax.broadcasted_iota(jnp.int32, (8, width), 0)
    lat8 = jnp.zeros((8, width), F32)
    for l in range(latents):
        lat8 = jnp.where(row8 == l, weights[l], lat8)
    scale[...] = gates * lat8
    loads[2].wait()
    left = fold(lax.dot_general(rstack[...], err[...], NT, preferred_element_type=F32))
    loads[3].wait()
    for l in range(latents):
        rows = pl.ds(l * per, per)
        gated[rows, :] = (cot[rows, :].astype(F32) * scale[l : l + 1, :]).astype(BF16)
    mixed = fold(lax.dot_general(rstack[...], gated[...], NT, preferred_element_type=F32))
    loads[4].wait()
    left = left + fold(lax.dot_general(split(mixed), head[...], NN, preferred_element_type=F32))
    for k in range(pairs):
        l_src[k] = left[k * piece : (k + 1) * piece]

    pl.semaphore_wait(barrier, 4 * (n - 1) + 1 + (nx - 1))
    scatter_send(l_src, l_in, 0)

    loads[5].wait()
    loads[6].wait()
    bin_row = lax.broadcasted_iota(jnp.int32, (nbins, per), 0)
    hist = jnp.zeros((nbins, per), F32)
    for l in range(latents):
        hist = hist + jnp.where(bin_row == bins[l : l + 1, :], weights[l] * loss[l : l + 1, :], 0.0)
    for k in range(pairs):
        g_src[k, :, share:] = hist[k * piece : (k + 1) * piece]
    loads[7].wait()
    step_w = 128 if share % 256 else 256
    row_s = lax.broadcasted_iota(jnp.int32, (8, step_w), 0)
    for i in range(width // step_w):
        cols = pl.ds(i * step_w, step_w)
        branch = lax.dot_general(head[...], weight[:, cols], NN, preferred_element_type=F32)
        prod = branch * cot[:, cols].astype(F32)
        out = jnp.zeros((8, step_w), F32)
        for l in range(latents):
            row = jnp.sum(prod[l * per : (l + 1) * per], axis=0, keepdims=True) * weights[l]
            out = jnp.where(row_s == l, row, out)
        t, off = divmod(i * step_w, share)
        t_src[t, :, off : off + step_w] = out
    t_in[x] = t_src[x]
    x_send(t_src, t_in, 1)

    wait_many(l_in, pairs - 1, 0)
    l_mid[b] = sum_slots(l_in)
    ring_send(l_mid, 2)

    for l in range(latents):
        rows = pl.ds(l * per, per)
        grad_v[rows, :] = lax.dot_general(
            gated[rows, :], weight[...], NT, preferred_element_type=F32
        ).astype(BF16)
    grad_copy = pltpu.make_async_copy(grad_v, grad_o, out_sem)
    grad_copy.start()

    wait_many(l_mid, n - 1, 2)
    l_all[c * n + a] = sum_slots(l_mid) * (1.0 / workers)
    gather_send(l_all, 3)

    wait_many(t_in, nx - 1, 1)
    lat_sum = sum_slots(t_in)
    bin_s = lax.broadcasted_iota(jnp.int32, (nbins, share), 0)
    spread = jnp.zeros((nbins, share), F32)
    for l in range(latents):
        spread = spread + jnp.where(bin_s == tb_ref[l], lat_sum[l : l + 1, :], 0.0)
    for k in range(pairs):
        g_src[k, :, :share] = spread[k * piece : (k + 1) * piece]

    wait_many(l_all, pairs - 1, 3)
    scatter_send(g_src, g_in, 4)
    left = jnp.concatenate([l_all[k] for k in range(pairs)], axis=0)
    left_o[...] = left
    lstack = split(left)
    mixed = fold(lax.dot_general(lstack, head[...], NT, preferred_element_type=F32))
    mstack = split(mixed)
    for i in range(width // step_w):
        cols = pl.ds(i * step_w, step_w)
        term = lax.dot_general(lstack, err[:, cols], NN, preferred_element_type=F32)
        term = term + lax.dot_general(mstack, gated[:, cols], NN, preferred_element_type=F32)
        term = fold(term)
        own_s[0, :, cols] = term[:half]
        own_s[1, :, cols] = term[half:]
    core_copy = remote(own_s.at[1 - c], sib_s, 5, sibling)
    core_copy.start()
    padded = jnp.concatenate([left, jnp.zeros((128 - rank, share), F32)], axis=0)
    gram[x] = lax.dot_general(left, padded, NT, precision=HIGHEST, preferred_element_type=F32)

    def gram_step(k, carry):
        remote(gram.at[x], gram.at[x], 6, (index, lax.rem(x + k, nx))).start()
        return carry

    lax.fori_loop(1, nx, gram_step, 0)
    core_copy.wait_recv()
    both = own_s[c] + sib_s[...]
    for k in range(n):
        s_src[k] = both[k * piece : (k + 1) * piece]
    s_in[a] = s_src[a]

    def s_step(k, carry):
        j = lax.rem(a + k, n)
        remote(s_src.at[j], s_in.at[a], 7, at_a(j, c)).start()
        return carry

    lax.fori_loop(1, n, s_step, 0)

    wait_many(g_in, pairs - 1, 4)
    g_mid[b] = sum_slots(g_in)
    ring_send(g_mid, 8)

    wait_many(gram, nx - 1, 6)
    whole = sum_slots(gram)
    eye_r = lax.broadcasted_iota(jnp.int32, (rank, 128), 0)
    eye_c = lax.broadcasted_iota(jnp.int32, (rank, 128), 1)
    whole = jnp.where(eye_c == eye_r + rank, 1.0, whole)
    groups = rank // 8

    def put(rows):
        for g in range(groups):
            chol[g] = rows[g]

    def get():
        return [chol[g] for g in range(groups)]

    put(eliminate([whole[8 * g : 8 * g + 8] for g in range(groups)], 0, rank // 4))

    wait_many(s_in, n - 1, 7)
    part = sum_slots(s_in)
    for t in range(nx):
        s_x[t] = part[:, t * share : (t + 1) * share]
    s_xin[x] = s_x[x]
    x_send(s_x, s_xin, 9)
    put(eliminate(get(), rank // 4, rank // 2))

    wait_many(s_xin, nx - 1, 9)
    s_mid[b] = sum_slots(s_xin)
    ring_send(s_mid, 10)
    wait_many(g_mid, n - 1, 8)
    g_all[c * n + a] = sum_slots(g_mid)
    gather_send(g_all, 11)
    put(eliminate(get(), rank // 2, 3 * rank // 4))

    wait_many(s_mid, n - 1, 10)
    s_all[c * n + a] = sum_slots(s_mid)
    gather_send(s_all, 12)
    inv_o[...] = unscaled_to_inverse(eliminate(get(), 3 * rank // 4, rank), rank)
    wait_many(g_all, pairs - 1, 11)
    for k in range(pairs):
        gate_o[k * piece : (k + 1) * piece] = g_all[k]
    wait_many(s_all, pairs - 1, 12)
    for k in range(pairs):
        s_o[k * piece : (k + 1) * piece] = s_all[k]

    wait_many(l_src, pairs - 1, 0, False)
    wait_many(t_src, nx - 1, 1, False)
    wait_many(l_mid, n - 1, 2, False)
    wait_many(l_all, pairs - 1, 3, False)
    wait_many(g_src, pairs - 1, 4, False)
    core_copy.wait_send()
    wait_many(gram, nx - 1, 6, False)
    wait_many(s_src, n - 1, 7, False)
    wait_many(g_mid, n - 1, 8, False)
    wait_many(s_x, nx - 1, 9, False)
    wait_many(s_mid, n - 1, 10, False)
    wait_many(g_all, pairs - 1, 11, False)
    wait_many(s_all, pairs - 1, 12, False)
    grad_copy.wait()


def end_kernel(workers, hist_scale, left, s, inv, gate, grad, basis_o, right_o, gate_o, hist_o, grad_o, sem):
    copy = pltpu.make_async_copy(grad, grad_o, sem)
    copy.start()
    rank, share = left.shape
    inverse = inv[:, rank : 2 * rank]
    basis_o[...] = lax.dot_general(inverse, left[...], NN, precision=HIGHEST, preferred_element_type=F32)
    right_o[...] = lax.dot_general(
        inverse, s[...], NN, precision=HIGHEST, preferred_element_type=F32
    ) * (1.0 / workers)
    gate_o[...] = gate[:, :share]
    hist_o[...] = jnp.sum(gate[:, share:], axis=1, keepdims=True).T * hist_scale
    copy.wait()


def per_device(n, nx, head, weight, cot, err, right, gate, sample, tbins, loss, lbins):
    workers = 2 * n * n
    rank = right.shape[1]
    tokens, feats = head.shape
    width = cot.shape[1]
    latents = tbins.shape[0]
    per = tokens // latents
    nbins = gate.shape[0]
    share = width // nx
    half = rank // 2
    piece = half // n
    pairs = 2 * n
    gwidth = share + per
    vmem = pl.BlockSpec(memory_space=pltpu.VMEM)
    smem = pl.BlockSpec(memory_space=pltpu.SMEM)
    hbm = pl.BlockSpec(memory_space=pl.ANY)
    V = pltpu.VMEM
    DMA = pltpu.SemaphoreType.DMA
    out = jax.ShapeDtypeStruct
    left, s, inv, gsum, grad = pl.pallas_call(
        functools.partial(main_kernel, n, nx, workers),
        out_shape=(
            out((rank, share), F32),
            out((rank, share), F32),
            out((rank, 128), F32),
            out((nbins, gwidth), F32),
            out((tokens, feats), BF16),
        ),
        in_specs=[smem, smem] + [hbm] * 8,
        out_specs=(vmem, vmem, vmem, vmem, hbm),
        scratch_shapes=[
            V(head.shape, BF16),
            V(weight.shape, BF16),
            V(cot.shape, BF16),
            V(err.shape[1:], BF16),
            V((rank, width), F32),
            V(gate.shape, BF16),
            V((latents, per), F32),
            V((latents, per), jnp.int32),
            DMA((8,)),
            V(cot.shape, BF16),
            V((2 * rank, width), BF16),
            V((8, width), F32),
            V((tokens, feats), BF16),
            V((8, 128), F32),
            V((2, half, width), F32),
            V((half, width), F32),
            V((pairs, piece, share), F32),
            V((pairs, piece, share), F32),
            V((n, piece, share), F32),
            V((pairs, piece, share), F32),
            V((pairs, piece, gwidth), F32),
            V((pairs, piece, gwidth), F32),
            V((n, piece, gwidth), F32),
            V((pairs, piece, gwidth), F32),
            V((n, piece, width), F32),
            V((n, piece, width), F32),
            V((nx, piece, share), F32),
            V((nx, piece, share), F32),
            V((n, piece, share), F32),
            V((pairs, piece, share), F32),
            V((nx, 8, share), F32),
            V((nx, 8, share), F32),
            V((nx, rank, 128), F32),
            V((rank // 8, 8, 128), F32),
            DMA((13,)),
            DMA((13,)),
            DMA,
        ],
        compiler_params=pltpu.CompilerParams(
            collective_id=0, has_side_effects=True, vmem_limit_bytes=48 * 1024 * 1024
        ),
        name="main",
    )(
        tbins, sample, head, weight, cot, err, right.T, gate,
        loss.reshape(latents, per), lbins.reshape(latents, per),
    )
    basis, new_right, gate_grad, hist, grad = pl.pallas_call(
        functools.partial(end_kernel, workers, nbins / (tokens * workers)),
        out_shape=(
            out((rank, share), F32),
            out((rank, share), F32),
            out((nbins, share), F32),
            out((1, nbins), F32),
            out((tokens, feats), BF16),
        ),
        in_specs=[vmem, vmem, vmem, vmem, hbm],
        out_specs=(vmem, vmem, vmem, vmem, hbm),
        scratch_shapes=[DMA],
        name="finish",
    )(left, s, inv, gsum, grad)
    return grad, basis.T, new_right.T, gate_grad, hist.reshape(nbins)


def solution(mesh):
    n = math.isqrt(mesh.shape["dp"] // 2)
    assert 2 * n * n == mesh.shape["dp"]
    placed = (
        P("dp", "tensor"),
        P("tensor", None),
        P("dp", None),
        P("dp", "tensor", None),
        P(),
        P(),
        P(),
        P("dp"),
        P("dp"),
        P("dp"),
    )
    return jax.shard_map(
        functools.partial(per_device, n, mesh.shape["tensor"]),
        mesh=mesh,
        in_specs=placed,
        out_specs=(P("dp", "tensor"), P("tensor", None), P("tensor", None), P(None, "tensor"), P()),
        check_vma=False,
    )
```

```python
import functools
import math

import jax
import jax.numpy as jnp
from jax import lax
from jax.experimental import pallas as pl
from jax.experimental.pallas import tpu as pltpu
from jax.sharding import PartitionSpec as P

MESH = pl.DeviceIdType.MESH
F32 = jnp.float32
BF16 = jnp.bfloat16
HIGHEST = lax.Precision.HIGHEST
NN = (((1,), (0,)), ((), ()))
NT = (((1,), (1,)), ((), ()))


def split(x):
    high = x.astype(BF16)
    low = (x - high.astype(F32)).astype(BF16)
    return jnp.concatenate([high, low], axis=0)


def fold(x):
    half = x.shape[0] // 2
    return x[:half] + x[half:]


def eliminate(rows, begin, end):
    groups = len(rows)
    width = rows[0].shape[1]
    sub = lax.broadcasted_iota(jnp.int32, (8, width), 0)
    rows = list(rows)
    for j in range(begin, end):
        g, r = divmod(j, 8)
        cols = [jnp.broadcast_to(rows[i][:, j : j + 1], (8, width)) for i in range(g, groups)]
        pivot = cols[0][r : r + 1]
        scaled = jnp.broadcast_to(rows[g][r : r + 1] / pivot, (8, width))
        for i in range(g, groups):
            factor = cols[i - g]
            if i == g:
                factor = jnp.where(sub > r, factor, 0.0)
            rows[i] = rows[i] - factor * scaled
    return rows


def unscaled_to_inverse(rows, rank):
    out = []
    width = rows[0].shape[1]
    lane = lax.broadcasted_iota(jnp.int32, (8, width), 1)
    sub = lax.broadcasted_iota(jnp.int32, (8, width), 0)
    for g, x in enumerate(rows):
        diag = jnp.sum(jnp.where(lane == sub + 8 * g, x, 0.0), axis=1, keepdims=True)
        out.append(x / jnp.sqrt(diag))
    return jnp.concatenate(out, axis=0)


def main_kernel(
    n, nx, workers,
    tb_hbm, sw_hbm, head_hbm, weight_hbm, cot_hbm, err_hbm, right_hbm, gate_hbm, loss_hbm, bins_hbm,
    left_o, s_o, inv_o, gate_o, grad_o,
    tb_ref, sw_ref, head, weight, cot, err, right, gate, loss, bins, load_sem,
    gated, rstack, scale, own_s, sib_s,
    l_src, l_in, l_mid, l_all,
    g_src, g_in, g_mid, g_all,
    s_src, s_in, s_x, s_xin, s_mid, s_all,
    t_src, t_in, gram, chol,
    ssem, rsem,
):
    rank = right.shape[0]
    tokens, feats = head.shape
    width = cot.shape[1]
    latents, per = loss.shape
    nbins = gate.shape[0]
    share = width // nx
    half = rank // 2
    piece = half // n
    pairs = 2 * n

    index = lax.axis_index("dp")
    x = lax.axis_index("tensor")
    c = lax.rem(index, 2)
    y = lax.rem(index // 2, n)
    z = index // (2 * n)

    def at_z(j, core):
        return ((j * n + y) * 2 + core, x)

    def at_y(j, core):
        return ((z * n + j) * 2 + core, x)

    a = jnp.where(c == 0, z, y)
    b = jnp.where(c == 0, y, z)

    def at_a(j, core):
        return (jnp.where(c == 0, j * n + y, z * n + j) * 2 + core, x)

    def at_b(j):
        return (jnp.where(c == 0, z * n + j, j * n + y) * 2 + c, x)

    sibling = (index + 1 - 2 * c, x)

    barrier = pltpu.get_barrier_semaphore()

    def greet(device):
        pl.semaphore_signal(barrier, inc=1, device_id=device, device_id_type=MESH)

    def greet_ring(k, carry):
        jz = lax.rem(z + k, n)
        jy = lax.rem(y + k, n)
        for core in (0, 1):
            greet(at_z(jz, core))
            greet(at_y(jy, core))
        return carry

    lax.fori_loop(1, n, greet_ring, 0)
    greet(sibling)

    def greet_x(k, carry):
        greet((index, lax.rem(x + k, nx)))
        return carry

    lax.fori_loop(1, nx, greet_x, 0)

    loads = []
    for k, (src, dst) in enumerate(
        (
            (right_hbm, right),
            (err_hbm.at[0], err),
            (tb_hbm, tb_ref),
            (sw_hbm, sw_ref),
            (gate_hbm, gate),
            (cot_hbm, cot),
            (head_hbm, head),
            (loss_hbm, loss),
            (bins_hbm, bins),
            (weight_hbm, weight),
        )
    ):
        loads.append(pltpu.make_async_copy(src, dst, load_sem.at[k]))
        loads[-1].start()

    def remote(src, dst, phase, device):
        return pltpu.make_async_remote_copy(
            src_ref=src, dst_ref=dst, send_sem=ssem.at[phase], recv_sem=rsem.at[phase],
            device_id=device, device_id_type=MESH,
        )

    def scatter_send(src, dst, phase):
        def step(k, carry):
            jz = lax.rem(z + k, n)
            jy = lax.rem(y + k, n)
            remote(src.at[jz], dst.at[z * 2 + c], phase, at_z(jz, 0)).start()
            remote(src.at[n + jy], dst.at[y * 2 + c], phase, at_y(jy, 1)).start()
            return carry

        lax.fori_loop(1, n, step, 0)

        @pl.when(c == 1)
        def _():
            remote(src.at[z], dst.at[z * 2 + 1], phase, sibling).start()

        @pl.when(c == 0)
        def _():
            remote(src.at[n + y], dst.at[y * 2], phase, sibling).start()

        dst[a * 2 + c] = src[c * n + a]

    def wait_many(ref, count, phase, recv=True):
        part = ref.at[pl.ds(0, count)]
        copy = remote(part, part, phase, sibling)
        if recv:
            copy.wait_recv()
        else:
            copy.wait_send()

    def sum_slots(ref):
        out = ref[0]
        for k in range(1, ref.shape[0]):
            out = out + ref[k]
        return out

    def ring_send(ref, phase):
        def step(k, carry):
            j = lax.rem(b + k, n)
            remote(ref.at[b], ref.at[b], phase, at_b(j)).start()
            return carry

        lax.fori_loop(1, n, step, 0)

    def gather_send(ref, phase):
        mine = c * n + a

        def step(k, carry):
            j = lax.rem(a + k, n)
            for core in (0, 1):
                remote(ref.at[mine], ref.at[mine], phase, at_a(j, core)).start()
            return carry

        remote(ref.at[mine], ref.at[mine], phase, sibling).start()
        lax.fori_loop(1, n, step, 0)

    def x_send(src, dst, phase):
        def step(k, carry):
            j = lax.rem(x + k, nx)
            remote(src.at[j], dst.at[x], phase, (index, j)).start()
            return carry

        lax.fori_loop(1, nx, step, 0)

    loads[0].wait()
    rstack[...] = split(right[...])
    loads[1].wait()
    left = fold(lax.dot_general(rstack[...], err[...], NT, preferred_element_type=F32))
    loads[2].wait()
    loads[3].wait()
    loads[4].wait()
    bin_of = lax.broadcasted_iota(jnp.int32, (8, nbins), 1)
    row_of = lax.broadcasted_iota(jnp.int32, (8, nbins), 0)
    onehot = jnp.zeros((8, nbins), F32)
    weights = []
    for l in range(latents):
        tb = tb_ref[l]
        weights.append(sw_ref[tb])
        onehot = jnp.where((row_of == l) & (bin_of == tb), 1.0, onehot)
    gates = lax.dot_general(onehot.astype(BF16), gate[...], NN, preferred_element_type=F32)
    row8 = lax.broadcasted_iota(jnp.int32, (8, width), 0)
    lat8 = jnp.zeros((8, width), F32)
    for l in range(latents):
        lat8 = jnp.where(row8 == l, weights[l], lat8)
    scale[...] = gates * lat8
    loads[5].wait()
    for l in range(latents):
        rows = pl.ds(l * per, per)
        gated[rows, :] = (cot[rows, :].astype(F32) * scale[l : l + 1, :]).astype(BF16)
    mixed = fold(lax.dot_general(rstack[...], gated[...], NT, preferred_element_type=F32))
    loads[6].wait()
    left = left + fold(lax.dot_general(split(mixed), head[...], NN, preferred_element_type=F32))
    for k in range(pairs):
        l_src[k] = left[k * piece : (k + 1) * piece]

    pl.semaphore_wait(barrier, 4 * (n - 1) + 1 + (nx - 1))
    scatter_send(l_src, l_in, 0)

    loads[7].wait()
    loads[8].wait()
    bin_row = lax.broadcasted_iota(jnp.int32, (nbins, per), 0)
    hist = jnp.zeros((nbins, per), F32)
    for l in range(latents):
        hist = hist + jnp.where(bin_row == bins[l : l + 1, :], weights[l] * loss[l : l + 1, :], 0.0)
    for k in range(pairs):
        g_src[k, :, share:] = hist[k * piece : (k + 1) * piece]
    loads[9].wait()
    step_w = 128 if share % 256 else 256
    row_s = lax.broadcasted_iota(jnp.int32, (8, step_w), 0)
    for i in range(width // step_w):
        cols = pl.ds(i * step_w, step_w)
        branch = lax.dot_general(head[...], weight[:, cols], NN, preferred_element_type=F32)
        prod = branch * cot[:, cols].astype(F32)
        out = jnp.zeros((8, step_w), F32)
        for l in range(latents):
            row = jnp.sum(prod[l * per : (l + 1) * per], axis=0, keepdims=True) * weights[l]
            out = jnp.where(row_s == l, row, out)
        t, off = divmod(i * step_w, share)
        t_src[t, :, off : off + step_w] = out
    t_in[x] = t_src[x]
    x_send(t_src, t_in, 1)

    wait_many(l_in, pairs - 1, 0)
    l_mid[b] = sum_slots(l_in)
    ring_send(l_mid, 2)

    for l in range(latents):
        rows = pl.ds(l * per, per)
        grad_o[rows, :] = lax.dot_general(
            gated[rows, :], weight[...], NT, preferred_element_type=F32
        ).astype(BF16)

    wait_many(l_mid, n - 1, 2)
    l_all[c * n + a] = sum_slots(l_mid) * (1.0 / workers)
    gather_send(l_all, 3)

    wait_many(t_in, nx - 1, 1)
    lat_sum = sum_slots(t_in)
    bin_s = lax.broadcasted_iota(jnp.int32, (nbins, share), 0)
    spread = jnp.zeros((nbins, share), F32)
    for l in range(latents):
        spread = spread + jnp.where(bin_s == tb_ref[l], lat_sum[l : l + 1, :], 0.0)
    for k in range(pairs):
        g_src[k, :, :share] = spread[k * piece : (k + 1) * piece]

    wait_many(l_all, pairs - 1, 3)
    scatter_send(g_src, g_in, 4)
    left = jnp.concatenate([l_all[k] for k in range(pairs)], axis=0)
    left_o[...] = left
    lstack = split(left)
    mixed = fold(lax.dot_general(lstack, head[...], NT, preferred_element_type=F32))
    mstack = split(mixed)
    for i in range(width // step_w):
        cols = pl.ds(i * step_w, step_w)
        term = lax.dot_general(lstack, err[:, cols], NN, preferred_element_type=F32)
        term = term + lax.dot_general(mstack, gated[:, cols], NN, preferred_element_type=F32)
        term = fold(term)
        own_s[0, :, cols] = term[:half]
        own_s[1, :, cols] = term[half:]
    core_copy = remote(own_s.at[1 - c], sib_s, 5, sibling)
    core_copy.start()
    padded = jnp.concatenate([left, jnp.zeros((128 - rank, share), F32)], axis=0)
    gram[x] = lax.dot_general(left, padded, NT, precision=HIGHEST, preferred_element_type=F32)

    def gram_step(k, carry):
        remote(gram.at[x], gram.at[x], 6, (index, lax.rem(x + k, nx))).start()
        return carry

    lax.fori_loop(1, nx, gram_step, 0)
    core_copy.wait_recv()
    both = own_s[c] + sib_s[...]
    for k in range(n):
        s_src[k] = both[k * piece : (k + 1) * piece]
    s_in[a] = s_src[a]

    def s_step(k, carry):
        j = lax.rem(a + k, n)
        remote(s_src.at[j], s_in.at[a], 7, at_a(j, c)).start()
        return carry

    lax.fori_loop(1, n, s_step, 0)

    wait_many(g_in, pairs - 1, 4)
    g_mid[b] = sum_slots(g_in)
    ring_send(g_mid, 8)

    wait_many(gram, nx - 1, 6)
    whole = sum_slots(gram)
    eye_r = lax.broadcasted_iota(jnp.int32, (rank, 128), 0)
    eye_c = lax.broadcasted_iota(jnp.int32, (rank, 128), 1)
    whole = jnp.where(eye_c == eye_r + rank, 1.0, whole)
    groups = rank // 8

    def put(rows):
        for g in range(groups):
            chol[g] = rows[g]

    def get():
        return [chol[g] for g in range(groups)]

    put(eliminate([whole[8 * g : 8 * g + 8] for g in range(groups)], 0, rank // 4))

    wait_many(s_in, n - 1, 7)
    part = sum_slots(s_in)
    for t in range(nx):
        s_x[t] = part[:, t * share : (t + 1) * share]
    s_xin[x] = s_x[x]
    x_send(s_x, s_xin, 9)
    put(eliminate(get(), rank // 4, rank // 2))

    wait_many(s_xin, nx - 1, 9)
    s_mid[b] = sum_slots(s_xin)
    ring_send(s_mid, 10)
    wait_many(g_mid, n - 1, 8)
    g_all[c * n + a] = sum_slots(g_mid)
    gather_send(g_all, 11)
    put(eliminate(get(), rank // 2, 3 * rank // 4))

    wait_many(s_mid, n - 1, 10)
    s_all[c * n + a] = sum_slots(s_mid)
    gather_send(s_all, 12)
    inv_o[...] = unscaled_to_inverse(eliminate(get(), 3 * rank // 4, rank), rank)
    wait_many(g_all, pairs - 1, 11)
    for k in range(pairs):
        gate_o[k * piece : (k + 1) * piece] = g_all[k]
    wait_many(s_all, pairs - 1, 12)
    for k in range(pairs):
        s_o[k * piece : (k + 1) * piece] = s_all[k]

    wait_many(l_src, pairs - 1, 0, False)
    wait_many(t_src, nx - 1, 1, False)
    wait_many(l_mid, n - 1, 2, False)
    wait_many(l_all, pairs - 1, 3, False)
    wait_many(g_src, pairs - 1, 4, False)
    core_copy.wait_send()
    wait_many(gram, nx - 1, 6, False)
    wait_many(s_src, n - 1, 7, False)
    wait_many(g_mid, n - 1, 8, False)
    wait_many(s_x, nx - 1, 9, False)
    wait_many(s_mid, n - 1, 10, False)
    wait_many(g_all, pairs - 1, 11, False)
    wait_many(s_all, pairs - 1, 12, False)


def end_kernel(workers, hist_scale, left, s, inv, gate, grad, basis_o, right_o, gate_o, hist_o, grad_o, sem):
    copy = pltpu.make_async_copy(grad, grad_o, sem)
    copy.start()
    rank, share = left.shape
    inverse = inv[:, rank : 2 * rank]
    basis_o[...] = lax.dot_general(inverse, left[...], NN, precision=HIGHEST, preferred_element_type=F32)
    right_o[...] = lax.dot_general(
        inverse, s[...], NN, precision=HIGHEST, preferred_element_type=F32
    ) * (1.0 / workers)
    gate_o[...] = gate[:, :share]
    hist_o[...] = jnp.sum(gate[:, share:], axis=1, keepdims=True).T * hist_scale
    copy.wait()


def per_device(n, nx, head, weight, cot, err, right, gate, sample, tbins, loss, lbins):
    workers = 2 * n * n
    rank = right.shape[1]
    tokens, feats = head.shape
    width = cot.shape[1]
    latents = tbins.shape[0]
    per = tokens // latents
    nbins = gate.shape[0]
    share = width // nx
    half = rank // 2
    piece = half // n
    pairs = 2 * n
    gwidth = share + per
    vmem = pl.BlockSpec(memory_space=pltpu.VMEM)
    hbm = pl.BlockSpec(memory_space=pltpu.HBM)
    V = pltpu.VMEM
    DMA = pltpu.SemaphoreType.DMA
    out = jax.ShapeDtypeStruct
    left, s, inv, gsum, grad = pl.pallas_call(
        functools.partial(main_kernel, n, nx, workers),
        out_shape=(
            out((rank, share), F32),
            out((rank, share), F32),
            out((rank, 128), F32),
            out((nbins, gwidth), F32),
            out((tokens, feats), BF16),
        ),
        in_specs=[hbm] * 10,
        out_specs=(vmem,) * 5,
        scratch_shapes=[
            pltpu.SMEM(tbins.shape, jnp.int32),
            pltpu.SMEM(sample.shape, F32),
            V(head.shape, BF16),
            V(weight.shape, BF16),
            V(cot.shape, BF16),
            V(err.shape[1:], BF16),
            V((rank, width), F32),
            V(gate.shape, BF16),
            V((latents, per), F32),
            V((latents, per), jnp.int32),
            DMA((10,)),
            V(cot.shape, BF16),
            V((2 * rank, width), BF16),
            V((8, width), F32),
            V((2, half, width), F32),
            V((half, width), F32),
            V((pairs, piece, share), F32),
            V((pairs, piece, share), F32),
            V((n, piece, share), F32),
            V((pairs, piece, share), F32),
            V((pairs, piece, gwidth), F32),
            V((pairs, piece, gwidth), F32),
            V((n, piece, gwidth), F32),
            V((pairs, piece, gwidth), F32),
            V((n, piece, width), F32),
            V((n, piece, width), F32),
            V((nx, piece, share), F32),
            V((nx, piece, share), F32),
            V((n, piece, share), F32),
            V((pairs, piece, share), F32),
            V((nx, 8, share), F32),
            V((nx, 8, share), F32),
            V((nx, rank, 128), F32),
            V((rank // 8, 8, 128), F32),
            DMA((13,)),
            DMA((13,)),
        ],
        compiler_params=pltpu.CompilerParams(
            collective_id=0, has_side_effects=True, vmem_limit_bytes=60 * 1024 * 1024
        ),
        name="main",
    )(
        tbins, sample, head, weight, cot, err, right.T, gate,
        loss.reshape(latents, per), lbins.reshape(latents, per),
    )
    basis, new_right, gate_grad, hist, grad = pl.pallas_call(
        functools.partial(end_kernel, workers, nbins / (tokens * workers)),
        out_shape=(
            out((rank, share), F32),
            out((rank, share), F32),
            out((nbins, share), F32),
            out((1, nbins), F32),
            out((tokens, feats), BF16),
        ),
        in_specs=[vmem] * 5,
        out_specs=(vmem, vmem, vmem, vmem, hbm),
        scratch_shapes=[DMA],
        compiler_params=pltpu.CompilerParams(vmem_limit_bytes=60 * 1024 * 1024),
        name="finish",
    )(left, s, inv, gsum, grad)
    return grad, basis.T, new_right.T, gate_grad, hist.reshape(nbins)


def solution(mesh):
    n = math.isqrt(mesh.shape["dp"] // 2)
    assert 2 * n * n == mesh.shape["dp"]
    placed = (
        P("dp", "tensor"),
        P("tensor", None),
        P("dp", None),
        P("dp", "tensor", None),
        P(),
        P(),
        P(),
        P("dp"),
        P("dp"),
        P("dp"),
    )
    return jax.shard_map(
        functools.partial(per_device, n, mesh.shape["tensor"]),
        mesh=mesh,
        in_specs=placed,
        out_specs=(P("dp", "tensor"), P("tensor", None), P("tensor", None), P(None, "tensor"), P()),
        check_vma=False,
    )
```

```python
import functools
import math

import jax
import jax.numpy as jnp
from jax import lax
from jax.experimental import pallas as pl
from jax.experimental.pallas import tpu as pltpu
from jax.sharding import PartitionSpec as P

MESH = pl.DeviceIdType.MESH
F32 = jnp.float32
BF16 = jnp.bfloat16
HIGHEST = lax.Precision.HIGHEST
NN = (((1,), (0,)), ((), ()))
NT = (((1,), (1,)), ((), ()))


def split(x):
    high = x.astype(BF16)
    low = (x - high.astype(F32)).astype(BF16)
    return jnp.concatenate([high, low], axis=0)


def fold(x):
    half = x.shape[0] // 2
    return x[:half] + x[half:]


def eliminate(rows, begin, end):
    groups = len(rows)
    width = rows[0].shape[1]
    sub = lax.broadcasted_iota(jnp.int32, (8, width), 0)
    rows = list(rows)

    def wide(x, j):
        return jnp.broadcast_to(x[:, j : j + 1], (8, width))

    for j in range(begin, end, 2):
        g, r = divmod(j, 8)
        first = [wide(rows[i], j) for i in range(g, groups)]
        second = [wide(rows[i], j + 1) for i in range(g, groups)]
        aa = first[0][r : r + 1]
        ab = first[0][r + 1 : r + 2]
        bb = second[0][r + 1 : r + 2]
        inverse = 1.0 / (aa * bb - ab * ab)
        top = rows[g][r : r + 1]
        low = rows[g][r + 1 : r + 2]
        one = jnp.broadcast_to((bb * inverse) * top - (ab * inverse) * low, (8, width))
        two = jnp.broadcast_to((aa * inverse) * low - (ab * inverse) * top, (8, width))
        for i in range(g, groups):
            change = first[i - g] * one + second[i - g] * two
            if i == g:
                if r == 6:
                    continue
                change = jnp.where(sub > r + 1, change, 0.0)
            rows[i] = rows[i] - change
    return rows


def unscaled_to_inverse(rows):
    out = []
    width = rows[0].shape[1]
    lane = lax.broadcasted_iota(jnp.int32, (8, width), 1)
    sub = lax.broadcasted_iota(jnp.int32, (8, width), 0)
    odd = lax.rem(sub, 2) == 1
    for g, x in enumerate(rows):
        row = sub + 8 * g
        before = jnp.concatenate([x[7:], x[:7]], axis=0)
        over = jnp.sum(jnp.where(lane == row - 1, before, 0.0), axis=1, keepdims=True)
        off = jnp.sum(jnp.where(lane == row - 1, x, 0.0), axis=1, keepdims=True)
        x = jnp.where(odd, x - (off / jnp.where(odd[:, :1], over, 1.0)) * before, x)
        diag = jnp.sum(jnp.where(lane == row, x, 0.0), axis=1, keepdims=True)
        out.append(x / jnp.sqrt(diag))
    return jnp.concatenate(out, axis=0)


def main_kernel(
    n, nx, workers,
    tb_hbm, sw_hbm, head_hbm, weight_hbm, cot_hbm, err_hbm, right_hbm, gate_hbm, loss_hbm, bins_hbm,
    left_o, s_o, inv_o, gate_o, grad_o,
    tb_ref, sw_ref, head, weight, cot, right, gate, loss, bins, load_sem,
    both_g, head_t, rstack, scale, own_s, sib_s,
    l_src, l_in, l_mid, l_all,
    g_src, g_in, g_mid, g_all,
    s_src, s_in, s_x, s_xin, s_mid, s_all,
    t_src, t_in, gram, chol,
    ssem, rsem,
):
    rank = right.shape[0]
    tokens, feats = head.shape
    width = cot.shape[1]
    latents, per = loss.shape
    nbins = gate.shape[0]
    share = width // nx
    half = rank // 2
    piece = half // n
    pairs = 2 * n

    index = lax.axis_index("dp")
    x = lax.axis_index("tensor")
    c = lax.rem(index, 2)
    y = lax.rem(index // 2, n)
    z = index // (2 * n)

    def at_z(j, core):
        return ((j * n + y) * 2 + core, x)

    def at_y(j, core):
        return ((z * n + j) * 2 + core, x)

    a = jnp.where(c == 0, z, y)
    b = jnp.where(c == 0, y, z)

    def at_a(j, core):
        return (jnp.where(c == 0, j * n + y, z * n + j) * 2 + core, x)

    def at_b(j):
        return (jnp.where(c == 0, z * n + j, j * n + y) * 2 + c, x)

    sibling = (index + 1 - 2 * c, x)

    barrier = pltpu.get_barrier_semaphore()

    def greet(device):
        pl.semaphore_signal(barrier, inc=1, device_id=device, device_id_type=MESH)

    def greet_ring(k, carry):
        jz = lax.rem(z + k, n)
        jy = lax.rem(y + k, n)
        for core in (0, 1):
            greet(at_z(jz, core))
            greet(at_y(jy, core))
        return carry

    lax.fori_loop(1, n, greet_ring, 0)
    greet(sibling)

    def greet_x(k, carry):
        greet((index, lax.rem(x + k, nx)))
        return carry

    lax.fori_loop(1, nx, greet_x, 0)

    loads = []
    for k, (src, dst) in enumerate(
        (
            (right_hbm, right),
            (err_hbm.at[0], both_g.at[pl.ds(0, feats)]),
            (tb_hbm, tb_ref),
            (sw_hbm, sw_ref),
            (gate_hbm, gate),
            (cot_hbm, cot),
            (head_hbm, head),
            (loss_hbm, loss),
            (bins_hbm, bins),
            (weight_hbm, weight),
        )
    ):
        loads.append(pltpu.make_async_copy(src, dst, load_sem.at[k]))
        loads[-1].start()

    def remote(src, dst, phase, device):
        return pltpu.make_async_remote_copy(
            src_ref=src, dst_ref=dst, send_sem=ssem.at[phase], recv_sem=rsem.at[phase],
            device_id=device, device_id_type=MESH,
        )

    def scatter_send(src, dst, phase):
        def step(k, carry):
            jz = lax.rem(z + k, n)
            jy = lax.rem(y + k, n)
            remote(src.at[jz], dst.at[z * 2 + c], phase, at_z(jz, 0)).start()
            remote(src.at[n + jy], dst.at[y * 2 + c], phase, at_y(jy, 1)).start()
            return carry

        lax.fori_loop(1, n, step, 0)

        @pl.when(c == 1)
        def _():
            remote(src.at[z], dst.at[z * 2 + 1], phase, sibling).start()

        @pl.when(c == 0)
        def _():
            remote(src.at[n + y], dst.at[y * 2], phase, sibling).start()

        dst[a * 2 + c] = src[c * n + a]

    def wait_many(ref, count, phase, recv=True):
        part = ref.at[pl.ds(0, count)]
        copy = remote(part, part, phase, sibling)
        if recv:
            copy.wait_recv()
        else:
            copy.wait_send()

    def sum_slots(ref):
        out = ref[0]
        for k in range(1, ref.shape[0]):
            out = out + ref[k]
        return out

    def ring_send(ref, phase):
        def step(k, carry):
            j = lax.rem(b + k, n)
            remote(ref.at[b], ref.at[b], phase, at_b(j)).start()
            return carry

        lax.fori_loop(1, n, step, 0)

    def gather_send(ref, phase):
        mine = c * n + a

        def step(k, carry):
            j = lax.rem(a + k, n)
            for core in (0, 1):
                remote(ref.at[mine], ref.at[mine], phase, at_a(j, core)).start()
            return carry

        remote(ref.at[mine], ref.at[mine], phase, sibling).start()
        lax.fori_loop(1, n, step, 0)

    def x_send(src, dst, phase):
        def step(k, carry):
            j = lax.rem(x + k, nx)
            remote(src.at[j], dst.at[x], phase, (index, j)).start()
            return carry

        lax.fori_loop(1, nx, step, 0)

    loads[0].wait()
    rstack[...] = split(right[...])
    loads[1].wait()
    first = lax.dot_general(both_g[:feats], rstack[...], NT, preferred_element_type=F32)
    left = fold(first.T)
    loads[2].wait()
    loads[3].wait()
    loads[4].wait()
    bin_of = lax.broadcasted_iota(jnp.int32, (8, nbins), 1)
    row_of = lax.broadcasted_iota(jnp.int32, (8, nbins), 0)
    onehot = jnp.zeros((8, nbins), F32)
    weights = []
    for l in range(latents):
        tb = tb_ref[l]
        weights.append(sw_ref[tb])
        onehot = jnp.where((row_of == l) & (bin_of == tb), 1.0, onehot)
    gates = lax.dot_general(onehot.astype(BF16), gate[...], NN, preferred_element_type=F32)
    row8 = lax.broadcasted_iota(jnp.int32, (8, width), 0)
    lat8 = jnp.zeros((8, width), F32)
    for l in range(latents):
        lat8 = jnp.where(row8 == l, weights[l], lat8)
    scale[...] = gates * lat8
    loads[5].wait()
    for l in range(latents):
        rows = pl.ds(l * per, per)
        both_g[pl.ds(feats + l * per, per), :] = (cot[rows, :].astype(F32) * scale[l : l + 1, :]).astype(BF16)
    mixed = fold(lax.dot_general(both_g[feats:], rstack[...], NT, preferred_element_type=F32).T)
    loads[6].wait()
    left = left + fold(lax.dot_general(split(mixed), head[...], NN, preferred_element_type=F32))
    for k in range(pairs):
        l_src[k] = left[k * piece : (k + 1) * piece]

    pl.semaphore_wait(barrier, 4 * (n - 1) + 1 + (nx - 1))
    scatter_send(l_src, l_in, 0)

    head_t[...] = head[...].T

    loads[7].wait()
    loads[8].wait()
    bin_row = lax.broadcasted_iota(jnp.int32, (nbins, per), 0)
    hist = jnp.zeros((nbins, per), F32)
    for l in range(latents):
        hist = hist + jnp.where(bin_row == bins[l : l + 1, :], weights[l] * loss[l : l + 1, :], 0.0)
    for k in range(pairs):
        g_src[k, :, share:] = hist[k * piece : (k + 1) * piece]
    loads[9].wait()
    step_w = 128 if share % 256 else 256
    row_s = lax.broadcasted_iota(jnp.int32, (8, step_w), 0)
    for i in range(width // step_w):
        cols = pl.ds(i * step_w, step_w)
        branch = lax.dot_general(head[...], weight[:, cols], NN, preferred_element_type=F32)
        prod = branch * cot[:, cols].astype(F32)
        out = jnp.zeros((8, step_w), F32)
        for l in range(latents):
            row = jnp.sum(prod[l * per : (l + 1) * per], axis=0, keepdims=True) * weights[l]
            out = jnp.where(row_s == l, row, out)
        t, off = divmod(i * step_w, share)
        t_src[t, :, off : off + step_w] = out
    t_in[x] = t_src[x]
    x_send(t_src, t_in, 1)

    wait_many(l_in, pairs - 1, 0)
    l_mid[b] = sum_slots(l_in)
    ring_send(l_mid, 2)

    grad_o[...] = lax.dot_general(
        both_g[feats:], weight[...], NT, preferred_element_type=F32
    ).astype(BF16)

    wait_many(l_mid, n - 1, 2)
    l_all[c * n + a] = sum_slots(l_mid) * (1.0 / workers)
    gather_send(l_all, 3)

    wait_many(t_in, nx - 1, 1)
    lat_sum = sum_slots(t_in)
    bin_s = lax.broadcasted_iota(jnp.int32, (nbins, share), 0)
    spread = jnp.zeros((nbins, share), F32)
    for l in range(latents):
        spread = spread + jnp.where(bin_s == tb_ref[l], lat_sum[l : l + 1, :], 0.0)
    for k in range(pairs):
        g_src[k, :, :share] = spread[k * piece : (k + 1) * piece]

    wait_many(l_all, pairs - 1, 3)
    scatter_send(g_src, g_in, 4)
    left = jnp.concatenate([l_all[k] for k in range(pairs)], axis=0)
    left_o[...] = left
    lstack = split(left)
    mixed = fold(lax.dot_general(lstack, head_t[...], NN, preferred_element_type=F32))
    stack = jnp.concatenate([lstack, split(mixed)], axis=1)
    for i in range(width // share):
        cols = pl.ds(i * share, share)
        term = fold(lax.dot_general(stack, both_g[:, cols], NN, preferred_element_type=F32))
        own_s[0, :, cols] = term[:half]
        own_s[1, :, cols] = term[half:]
        remote(own_s.at[1 - c, :, cols], sib_s.at[:, cols], 5, sibling).start()
    padded = jnp.concatenate([left, jnp.zeros((128 - rank, share), F32)], axis=0)
    gram[x] = lax.dot_general(left, padded, NT, precision=HIGHEST, preferred_element_type=F32)

    def gram_step(k, carry):
        remote(gram.at[x], gram.at[x], 6, (index, lax.rem(x + k, nx))).start()
        return carry

    lax.fori_loop(1, nx, gram_step, 0)
    remote(sib_s, sib_s, 5, sibling).wait_recv()
    both = own_s[c] + sib_s[...]
    for k in range(n):
        s_src[k] = both[k * piece : (k + 1) * piece]
    s_in[a] = s_src[a]

    def s_step(k, carry):
        j = lax.rem(a + k, n)
        remote(s_src.at[j], s_in.at[a], 7, at_a(j, c)).start()
        return carry

    lax.fori_loop(1, n, s_step, 0)

    wait_many(g_in, pairs - 1, 4)
    g_mid[b] = sum_slots(g_in)
    ring_send(g_mid, 8)

    wait_many(gram, nx - 1, 6)
    whole = sum_slots(gram)
    eye_r = lax.broadcasted_iota(jnp.int32, (rank, 128), 0)
    eye_c = lax.broadcasted_iota(jnp.int32, (rank, 128), 1)
    whole = jnp.where(eye_c == eye_r + rank, 1.0, whole)
    groups = rank // 8

    def put(rows):
        for g in range(groups):
            chol[g] = rows[g]

    def get():
        return [chol[g] for g in range(groups)]

    put(eliminate([whole[8 * g : 8 * g + 8] for g in range(groups)], 0, rank // 4))

    wait_many(s_in, n - 1, 7)
    part = sum_slots(s_in)
    for t in range(nx):
        s_x[t] = part[:, t * share : (t + 1) * share]
    s_xin[x] = s_x[x]
    x_send(s_x, s_xin, 9)
    put(eliminate(get(), rank // 4, rank // 2))

    wait_many(s_xin, nx - 1, 9)
    s_mid[b] = sum_slots(s_xin)
    ring_send(s_mid, 10)
    wait_many(g_mid, n - 1, 8)
    g_all[c * n + a] = sum_slots(g_mid)
    gather_send(g_all, 11)
    put(eliminate(get(), rank // 2, 3 * rank // 4))

    wait_many(s_mid, n - 1, 10)
    s_all[c * n + a] = sum_slots(s_mid)
    gather_send(s_all, 12)
    inv_o[...] = unscaled_to_inverse(eliminate(get(), 3 * rank // 4, rank))
    wait_many(g_all, pairs - 1, 11)
    for k in range(pairs):
        gate_o[k * piece : (k + 1) * piece] = g_all[k]
    wait_many(s_all, pairs - 1, 12)
    for k in range(pairs):
        s_o[k * piece : (k + 1) * piece] = s_all[k]

    wait_many(l_src, pairs - 1, 0, False)
    wait_many(t_src, nx - 1, 1, False)
    wait_many(l_mid, n - 1, 2, False)
    wait_many(l_all, pairs - 1, 3, False)
    wait_many(g_src, pairs - 1, 4, False)
    remote(sib_s, sib_s, 5, sibling).wait_send()
    wait_many(gram, nx - 1, 6, False)
    wait_many(s_src, n - 1, 7, False)
    wait_many(g_mid, n - 1, 8, False)
    wait_many(s_x, nx - 1, 9, False)
    wait_many(s_mid, n - 1, 10, False)
    wait_many(g_all, pairs - 1, 11, False)
    wait_many(s_all, pairs - 1, 12, False)


def end_kernel(workers, hist_scale, left, s, inv, gate, grad, basis_o, right_o, gate_o, hist_o, grad_o, sem):
    copy = pltpu.make_async_copy(grad, grad_o, sem)
    copy.start()
    rank, share = left.shape
    inverse = inv[:, rank : 2 * rank]
    basis_o[...] = lax.dot_general(inverse, left[...], NN, precision=HIGHEST, preferred_element_type=F32)
    right_o[...] = lax.dot_general(
        inverse, s[...], NN, precision=HIGHEST, preferred_element_type=F32
    ) * (1.0 / workers)
    gate_o[...] = gate[:, :share]
    hist_o[...] = jnp.sum(gate[:, share:], axis=1, keepdims=True).T * hist_scale
    copy.wait()


def per_device(n, nx, head, weight, cot, err, right, gate, sample, tbins, loss, lbins):
    workers = 2 * n * n
    rank = right.shape[1]
    tokens, feats = head.shape
    width = cot.shape[1]
    latents = tbins.shape[0]
    per = tokens // latents
    nbins = gate.shape[0]
    share = width // nx
    half = rank // 2
    piece = half // n
    pairs = 2 * n
    gwidth = share + per
    vmem = pl.BlockSpec(memory_space=pltpu.VMEM)
    hbm = pl.BlockSpec(memory_space=pltpu.HBM)
    V = pltpu.VMEM
    DMA = pltpu.SemaphoreType.DMA
    out = jax.ShapeDtypeStruct
    left, s, inv, gsum, grad = pl.pallas_call(
        functools.partial(main_kernel, n, nx, workers),
        out_shape=(
            out((rank, share), F32),
            out((rank, share), F32),
            out((rank, 128), F32),
            out((nbins, gwidth), F32),
            out((tokens, feats), BF16),
        ),
        in_specs=[hbm] * 10,
        out_specs=(vmem,) * 5,
        scratch_shapes=[
            pltpu.SMEM(tbins.shape, jnp.int32),
            pltpu.SMEM(sample.shape, F32),
            V(head.shape, BF16),
            V(weight.shape, BF16),
            V(cot.shape, BF16),
            V((rank, width), F32),
            V(gate.shape, BF16),
            V((latents, per), F32),
            V((latents, per), jnp.int32),
            DMA((10,)),
            V((feats + tokens, width), BF16),
            V((feats, tokens), BF16),
            V((2 * rank, width), BF16),
            V((8, width), F32),
            V((2, half, width), F32),
            V((half, width), F32),
            V((pairs, piece, share), F32),
            V((pairs, piece, share), F32),
            V((n, piece, share), F32),
            V((pairs, piece, share), F32),
            V((pairs, piece, gwidth), F32),
            V((pairs, piece, gwidth), F32),
            V((n, piece, gwidth), F32),
            V((pairs, piece, gwidth), F32),
            V((n, piece, width), F32),
            V((n, piece, width), F32),
            V((nx, piece, share), F32),
            V((nx, piece, share), F32),
            V((n, piece, share), F32),
            V((pairs, piece, share), F32),
            V((nx, 8, share), F32),
            V((nx, 8, share), F32),
            V((nx, rank, 128), F32),
            V((rank // 8, 8, 128), F32),
            DMA((13,)),
            DMA((13,)),
        ],
        compiler_params=pltpu.CompilerParams(
            collective_id=0, has_side_effects=True, vmem_limit_bytes=60 * 1024 * 1024
        ),
        name="main",
    )(
        tbins, sample, head, weight, cot, err, right.T, gate,
        loss.reshape(latents, per), lbins.reshape(latents, per),
    )
    basis, new_right, gate_grad, hist, grad = pl.pallas_call(
        functools.partial(end_kernel, workers, nbins / (tokens * workers)),
        out_shape=(
            out((rank, share), F32),
            out((rank, share), F32),
            out((nbins, share), F32),
            out((1, nbins), F32),
            out((tokens, feats), BF16),
        ),
        in_specs=[vmem] * 5,
        out_specs=(vmem, vmem, vmem, vmem, hbm),
        scratch_shapes=[DMA],
        compiler_params=pltpu.CompilerParams(vmem_limit_bytes=60 * 1024 * 1024),
        name="finish",
    )(left, s, inv, gsum, grad)
    return grad, basis.T, new_right.T, gate_grad, hist.reshape(nbins)


def solution(mesh):
    n = math.isqrt(mesh.shape["dp"] // 2)
    assert 2 * n * n == mesh.shape["dp"]
    placed = (
        P("dp", "tensor"),
        P("tensor", None),
        P("dp", None),
        P("dp", "tensor", None),
        P(),
        P(),
        P(),
        P("dp"),
        P("dp"),
        P("dp"),
    )
    return jax.shard_map(
        functools.partial(per_device, n, mesh.shape["tensor"]),
        mesh=mesh,
        in_specs=placed,
        out_specs=(P("dp", "tensor"), P("tensor", None), P("tensor", None), P(None, "tensor"), P()),
        check_vma=False,
    )
```

```python
import functools
import math

import jax
import jax.numpy as jnp
from jax import lax
from jax.experimental import pallas as pl
from jax.experimental.pallas import tpu as pltpu
from jax.sharding import PartitionSpec as P

MESH = pl.DeviceIdType.MESH
F32 = jnp.float32
BF16 = jnp.bfloat16
HIGHEST = lax.Precision.HIGHEST
NN = (((1,), (0,)), ((), ()))
NT = (((1,), (1,)), ((), ()))


def split(x):
    high = x.astype(BF16)
    low = (x - high.astype(F32)).astype(BF16)
    return jnp.concatenate([high, low], axis=0)


def fold(x):
    half = x.shape[0] // 2
    return x[:half] + x[half:]


def eliminate(rows, begin, end):
    groups = len(rows)
    width = rows[0].shape[1]
    sub = lax.broadcasted_iota(jnp.int32, (8, width), 0)
    rows = list(rows)

    def wide(x, j):
        return jnp.broadcast_to(x[:, j : j + 1], (8, width))

    for j in range(begin, end, 2):
        g, r = divmod(j, 8)
        first = [wide(rows[i], j) for i in range(g, groups)]
        second = [wide(rows[i], j + 1) for i in range(g, groups)]
        aa = first[0][r : r + 1]
        ab = first[0][r + 1 : r + 2]
        bb = second[0][r + 1 : r + 2]
        inverse = 1.0 / (aa * bb - ab * ab)
        top = rows[g][r : r + 1]
        low = rows[g][r + 1 : r + 2]
        one = jnp.broadcast_to((bb * inverse) * top - (ab * inverse) * low, (8, width))
        two = jnp.broadcast_to((aa * inverse) * low - (ab * inverse) * top, (8, width))
        for i in range(g, groups):
            change = first[i - g] * one + second[i - g] * two
            if i == g:
                if r == 6:
                    continue
                change = jnp.where(sub > r + 1, change, 0.0)
            rows[i] = rows[i] - change
    return rows


def unscaled_to_inverse(rows):
    out = []
    width = rows[0].shape[1]
    lane = lax.broadcasted_iota(jnp.int32, (8, width), 1)
    sub = lax.broadcasted_iota(jnp.int32, (8, width), 0)
    odd = lax.rem(sub, 2) == 1
    for g, x in enumerate(rows):
        row = sub + 8 * g
        before = jnp.concatenate([x[7:], x[:7]], axis=0)
        over = jnp.sum(jnp.where(lane == row - 1, before, 0.0), axis=1, keepdims=True)
        off = jnp.sum(jnp.where(lane == row - 1, x, 0.0), axis=1, keepdims=True)
        x = jnp.where(odd, x - (off / jnp.where(odd[:, :1], over, 1.0)) * before, x)
        diag = jnp.sum(jnp.where(lane == row, x, 0.0), axis=1, keepdims=True)
        out.append(x / jnp.sqrt(diag))
    return jnp.concatenate(out, axis=0)


def far_first(n):
    return sorted(range(1, n), key=lambda k: -min(k, n - k))


def wrap(value, n):
    return jnp.where(value >= n, value - n, value)


A1, TG, A2, A3, G1, G2, G3, GRAM, XX, C4, C5, PAIR = range(12)


def main_kernel(
    n, nx, workers,
    tb_hbm, sw_hbm, head_hbm, weight_hbm, cot_hbm, err_hbm, right_hbm, gate_hbm, loss_hbm, bins_hbm,
    basis_o, right_o, gate_o, grad_o,
    tb_ref, sw_ref, head, weight, cot, right, gate, loss, bins, load_sem, out_sem,
    both_g, head_t, rstack, scale, own_s, sib_s,
    l_src, l_in, l_mid, l_all,
    g_src, g_in, g_mid, g_all,
    s_src, s_in, s_x, s_xin, s_mid, s_all,
    t_src, t_in, gram, chol, grad_v, gate_v, basis_v, right_v,
    ssem, rsem,
):
    rank = right.shape[0]
    tokens, feats = head.shape
    width = cot.shape[1]
    latents, per = loss.shape
    nbins = gate.shape[0]
    share = width // nx
    half = rank // 2
    piece = half // n
    pairs = 2 * n
    FIRST = PAIR + nx
    order = far_first(n)

    loads = []
    for k, (src, dst) in enumerate(
        (
            (right_hbm, right),
            (err_hbm.at[0], both_g.at[pl.ds(0, feats)]),
            (tb_hbm, tb_ref),
            (sw_hbm, sw_ref),
            (gate_hbm, gate),
            (cot_hbm, cot),
            (head_hbm, head),
            (loss_hbm, loss),
            (bins_hbm, bins),
            (weight_hbm, weight),
        )
    ):
        loads.append(pltpu.make_async_copy(src, dst, load_sem.at[k]))
        loads[-1].start()

    index = lax.axis_index("dp")
    x = lax.axis_index("tensor")
    c = lax.rem(index, 2)
    y = lax.rem(index // 2, n)
    z = index // (2 * n)

    def at_z(j, core):
        return ((j * n + y) * 2 + core, x)

    def at_y(j, core):
        return ((z * n + j) * 2 + core, x)

    a = jnp.where(c == 0, z, y)
    b = jnp.where(c == 0, y, z)

    a_step = jnp.where(c == 0, 2 * n, 2)
    a_base = jnp.where(c == 0, 2 * y, 2 * n * z)
    b_step = jnp.where(c == 0, 2, 2 * n)
    b_base = jnp.where(c == 0, 2 * n * z, 2 * y) + c

    def at_a(j, core):
        return (j * a_step + a_base + core, x)

    def at_b(j):
        return (j * b_step + b_base, x)

    sibling = (index + 1 - 2 * c, x)

    barrier = pltpu.get_barrier_semaphore()

    def greet(device):
        pl.semaphore_signal(barrier, inc=1, device_id=device, device_id_type=MESH)

    for k in order:
        jz = wrap(z + k, n)
        jy = wrap(y + k, n)
        for core in (0, 1):
            greet(at_z(jz, core))
            greet(at_y(jy, core))
    greet(sibling)
    for k in far_first(nx):
        greet((index, wrap(x + k, nx)))

    def remote(src, dst, phase, device):
        return pltpu.make_async_remote_copy(
            src_ref=src, dst_ref=dst, send_sem=ssem.at[phase], recv_sem=rsem.at[phase],
            device_id=device, device_id_type=MESH,
        )

    def scatter_send(src, dst, phase):
        for k in order:
            jz = wrap(z + k, n)
            jy = wrap(y + k, n)
            remote(src.at[jz], dst.at[z * 2 + c], phase, at_z(jz, 0)).start()
            remote(src.at[n + jy], dst.at[y * 2 + c], phase, at_y(jy, 1)).start()

        @pl.when(c == 1)
        def _():
            remote(src.at[z], dst.at[z * 2 + 1], phase, sibling).start()

        @pl.when(c == 0)
        def _():
            remote(src.at[n + y], dst.at[y * 2], phase, sibling).start()

        dst[a * 2 + c] = src[c * n + a]

    def wait_many(ref, count, phase, recv=True):
        part = ref.at[pl.ds(0, count)]
        copy = remote(part, part, phase, sibling)
        if recv:
            copy.wait_recv()
        else:
            copy.wait_send()

    def sum_slots(ref, count):
        out = ref[0]
        for k in range(1, count):
            out = out + ref[k]
        return out

    def ring_send(ref, phase):
        for k in order:
            remote(ref.at[b], ref.at[b], phase, at_b(wrap(b + k, n))).start()

    def gather_send(ref, phase):
        mine = c * n + a
        for k in order:
            j = wrap(a + k, n)
            for core in (0, 1):
                remote(ref.at[mine], ref.at[mine], phase, at_a(j, core)).start()
        remote(ref.at[mine], ref.at[mine], phase, sibling).start()

    loads[0].wait()
    rstack[...] = split(right[...])
    loads[1].wait()
    first = lax.dot_general(both_g[:feats], rstack[...], NT, preferred_element_type=F32)
    left = fold(first.T)
    loads[2].wait()
    loads[3].wait()
    loads[4].wait()
    bin_of = lax.broadcasted_iota(jnp.int32, (8, nbins), 1)
    row_of = lax.broadcasted_iota(jnp.int32, (8, nbins), 0)
    onehot = jnp.zeros((8, nbins), F32)
    weights = []
    for l in range(latents):
        tb = tb_ref[l]
        weights.append(sw_ref[tb])
        onehot = jnp.where((row_of == l) & (bin_of == tb), 1.0, onehot)
    gates = lax.dot_general(onehot.astype(BF16), gate[...], NN, preferred_element_type=F32)
    row8 = lax.broadcasted_iota(jnp.int32, (8, width), 0)
    lat8 = jnp.zeros((8, width), F32)
    for l in range(latents):
        lat8 = jnp.where(row8 == l, weights[l], lat8)
    scale[...] = gates * lat8
    loads[5].wait()
    for l in range(latents):
        rows = pl.ds(l * per, per)
        both_g[pl.ds(feats + l * per, per), :] = (cot[rows, :].astype(F32) * scale[l : l + 1, :]).astype(BF16)
    mixed = fold(lax.dot_general(both_g[feats:], rstack[...], NT, preferred_element_type=F32).T)
    loads[6].wait()
    left = left + fold(lax.dot_general(split(mixed), head[...], NN, preferred_element_type=F32))
    for k in range(pairs):
        l_src[k] = left[k * piece : (k + 1) * piece]

    pl.semaphore_wait(barrier, 4 * (n - 1) + 1 + (nx - 1))
    scatter_send(l_src, l_in, A1)

    loads[9].wait()
    step_w = 128 if share % 256 else 256
    row_s = lax.broadcasted_iota(jnp.int32, (8, step_w), 0)
    for i in range(width // step_w):
        cols = pl.ds(i * step_w, step_w)
        branch = lax.dot_general(head[...], weight[:, cols], NN, preferred_element_type=F32)
        prod = branch * cot[:, cols].astype(F32)
        out = jnp.zeros((8, step_w), F32)
        for l in range(latents):
            row = jnp.sum(prod[l * per : (l + 1) * per], axis=0, keepdims=True) * weights[l]
            out = jnp.where(row_s == l, row, out)
        t, off = divmod(i * step_w, share)
        t_src[t, :, off : off + step_w] = out
    t_in[x] = t_src[x]
    for k in far_first(nx):
        j = wrap(x + k, nx)
        remote(t_src.at[j], t_in.at[x], TG, (index, j)).start()

    wait_many(l_in, pairs - 1, A1)
    l_mid[b] = sum_slots(l_in, pairs)
    ring_send(l_mid, A2)

    head_t[...] = head[...].T
    loads[7].wait()
    loads[8].wait()
    bin_row = lax.broadcasted_iota(jnp.int32, (nbins, per), 0)
    hist = jnp.zeros((nbins, per), F32)
    for l in range(latents):
        hist = hist + jnp.where(bin_row == bins[l : l + 1, :], weights[l] * loss[l : l + 1, :], 0.0)
    wait_many(t_in, nx - 1, TG)
    lat_sum = sum_slots(t_in, nx)
    bin_s = lax.broadcasted_iota(jnp.int32, (nbins, share), 0)
    spread = jnp.zeros((nbins, share), F32)
    for l in range(latents):
        spread = spread + jnp.where(bin_s == tb_ref[l], lat_sum[l : l + 1, :], 0.0)
    for k in range(pairs):
        g_src[k, :, share:] = hist[k * piece : (k + 1) * piece]
        g_src[k, :, :share] = spread[k * piece : (k + 1) * piece]

    wait_many(l_mid, n - 1, A2)
    l_all[c * n + a] = sum_slots(l_mid, n) * (1.0 / workers)
    gather_send(l_all, A3)
    scatter_send(g_src, g_in, G1)

    wait_many(l_all, pairs - 1, A3)
    left = jnp.concatenate([l_all[k] for k in range(pairs)], axis=0)
    lstack = split(left)
    mixed = fold(lax.dot_general(lstack, head_t[...], NN, preferred_element_type=F32))
    stack = jnp.concatenate([lstack, split(mixed)], axis=1)

    parts = far_first(nx) + [0]
    targets = [wrap(x + k, nx) for k in parts]

    def part_start(i):
        cols = pl.ds(pl.multiple_of(targets[i] * share, 128), share)
        term = fold(lax.dot_general(stack, both_g[:, cols], NN, preferred_element_type=F32))
        own_s[i, 0] = term[:half]
        own_s[i, 1] = term[half:]
        remote(own_s.at[i, 1 - c], sib_s.at[i], PAIR + i, sibling).start()

    def part_scatter(i):
        remote(sib_s.at[i], sib_s.at[i], PAIR + i, sibling).wait_recv()
        total = own_s[i, c] + sib_s[i]
        for k in range(n):
            s_src[i, k] = total[k * piece : (k + 1) * piece]
        s_in[i, a] = s_src[i, a]
        for k in order:
            j = wrap(a + k, n)
            remote(s_src.at[i, j], s_in.at[i, a], FIRST + i, at_a(j, c)).start()

    def part_cross(i):
        wait_many(s_in.at[i], n - 1, FIRST + i)
        total = sum_slots(s_in.at[i], n)
        if parts[i]:
            s_x[i] = total
            remote(s_x.at[i], s_xin.at[x], XX, (index, targets[i])).start()
        else:
            s_xin[x] = total

    part_start(0)
    for i in range(1, nx):
        part_start(i)
        part_scatter(i - 1)
    padded = jnp.concatenate([left, jnp.zeros((128 - rank, share), F32)], axis=0)
    gram[x] = lax.dot_general(left, padded, NT, precision=HIGHEST, preferred_element_type=F32)
    part_scatter(nx - 1)
    for k in far_first(nx):
        remote(gram.at[x], gram.at[x], GRAM, (index, wrap(x + k, nx))).start()
    wait_many(g_in, pairs - 1, G1)
    g_mid[b] = sum_slots(g_in, pairs)
    ring_send(g_mid, G2)
    for i in range(nx):
        part_cross(i)

    grad_v[...] = lax.dot_general(
        both_g[feats:], weight[...], NT, preferred_element_type=F32
    ).astype(BF16)
    outs = [pltpu.make_async_copy(grad_v, grad_o, out_sem.at[0])]
    outs[-1].start()

    wait_many(s_xin, nx - 1, XX)
    s_mid[b] = sum_slots(s_xin, nx)
    ring_send(s_mid, C4)

    wait_many(g_mid, n - 1, G2)
    g_all[c * n + a] = sum_slots(g_mid, n)
    gather_send(g_all, G3)
    wait_many(gram, nx - 1, GRAM)
    whole = sum_slots(gram, nx)
    eye_r = lax.broadcasted_iota(jnp.int32, (rank, 128), 0)
    eye_c = lax.broadcasted_iota(jnp.int32, (rank, 128), 1)
    whole = jnp.where(eye_c == eye_r + rank, 1.0, whole)
    groups = rank // 8
    rows = eliminate([whole[8 * g : 8 * g + 8] for g in range(groups)], 0, rank // 2)
    for g in range(groups):
        chol[g] = rows[g]

    wait_many(s_mid, n - 1, C4)
    s_all[c * n + a] = sum_slots(s_mid, n)
    gather_send(s_all, C5)
    rows = eliminate([chol[g] for g in range(groups)], rank // 2, rank)
    inverse = unscaled_to_inverse(rows)[:, rank : 2 * rank]
    basis_v[...] = lax.dot_general(inverse, left, NN, precision=HIGHEST, preferred_element_type=F32)
    outs.append(pltpu.make_async_copy(basis_v, basis_o, out_sem.at[1]))
    outs[-1].start()
    wait_many(g_all, pairs - 1, G3)
    for k in range(pairs):
        gate_v[k * piece : (k + 1) * piece] = g_all[k]
    outs.append(pltpu.make_async_copy(gate_v, gate_o, out_sem.at[2]))
    outs[-1].start()
    wait_many(s_all, pairs - 1, C5)
    s_whole = jnp.concatenate([s_all[k] for k in range(pairs)], axis=0)
    right_v[...] = lax.dot_general(
        inverse, s_whole, NN, precision=HIGHEST, preferred_element_type=F32
    ) * (1.0 / workers)
    outs.append(pltpu.make_async_copy(right_v, right_o, out_sem.at[3]))
    outs[-1].start()

    wait_many(l_src, pairs - 1, A1, False)
    wait_many(t_src, nx - 1, TG, False)
    wait_many(l_mid, n - 1, A2, False)
    wait_many(l_all, pairs - 1, A3, False)
    wait_many(g_src, pairs - 1, G1, False)
    for i in range(nx):
        remote(sib_s.at[i], sib_s.at[i], PAIR + i, sibling).wait_send()
        wait_many(s_src.at[i], n - 1, FIRST + i, False)
    wait_many(gram, nx - 1, GRAM, False)
    wait_many(g_mid, n - 1, G2, False)
    wait_many(s_x, nx - 1, XX, False)
    wait_many(s_mid, n - 1, C4, False)
    wait_many(g_all, pairs - 1, G3, False)
    wait_many(s_all, pairs - 1, C5, False)
    for copy in outs:
        copy.wait()


def end_kernel(hist_scale, basis, right, gate, grad, basis_o, right_o, gate_o, hist_o, grad_o):
    share = basis.shape[1]
    basis_o[...] = basis[...]
    right_o[...] = right[...]
    gate_o[...] = gate[:, :share]
    hist_o[...] = jnp.sum(gate[:, share:], axis=1, keepdims=True).T * hist_scale
    grad_o[...] = grad[...]


def per_device(n, nx, head, weight, cot, err, right, gate, sample, tbins, loss, lbins):
    workers = 2 * n * n
    rank = right.shape[1]
    tokens, feats = head.shape
    width = cot.shape[1]
    latents = tbins.shape[0]
    per = tokens // latents
    nbins = gate.shape[0]
    share = width // nx
    half = rank // 2
    piece = half // n
    pairs = 2 * n
    gwidth = share + per
    vmem = pl.BlockSpec(memory_space=pltpu.VMEM)
    hbm = pl.BlockSpec(memory_space=pltpu.HBM)
    V = pltpu.VMEM
    DMA = pltpu.SemaphoreType.DMA
    out = jax.ShapeDtypeStruct
    basis, new_right, gsum, grad = pl.pallas_call(
        functools.partial(main_kernel, n, nx, workers),
        out_shape=(
            out((rank, share), F32),
            out((rank, share), F32),
            out((nbins, gwidth), F32),
            out((tokens, feats), BF16),
        ),
        in_specs=[hbm] * 10,
        out_specs=(hbm,) * 4,
        scratch_shapes=[
            pltpu.SMEM(tbins.shape, jnp.int32),
            pltpu.SMEM(sample.shape, F32),
            V(head.shape, BF16),
            V(weight.shape, BF16),
            V(cot.shape, BF16),
            V((rank, width), F32),
            V(gate.shape, BF16),
            V((latents, per), F32),
            V((latents, per), jnp.int32),
            DMA((10,)),
            DMA((4,)),
            V((feats + tokens, width), BF16),
            V((feats, tokens), BF16),
            V((2 * rank, width), BF16),
            V((8, width), F32),
            V((nx, 2, half, share), F32),
            V((nx, half, share), F32),
            V((pairs, piece, share), F32),
            V((pairs, piece, share), F32),
            V((n, piece, share), F32),
            V((pairs, piece, share), F32),
            V((pairs, piece, gwidth), F32),
            V((pairs, piece, gwidth), F32),
            V((n, piece, gwidth), F32),
            V((pairs, piece, gwidth), F32),
            V((nx, n, piece, share), F32),
            V((nx, n, piece, share), F32),
            V((nx, piece, share), F32),
            V((nx, piece, share), F32),
            V((n, piece, share), F32),
            V((pairs, piece, share), F32),
            V((nx, 8, share), F32),
            V((nx, 8, share), F32),
            V((nx, rank, 128), F32),
            V((rank // 8, 8, 128), F32),
            V((tokens, feats), BF16),
            V((nbins, gwidth), F32),
            V((rank, share), F32),
            V((rank, share), F32),
            DMA((PAIR + 2 * nx,)),
            DMA((PAIR + 2 * nx,)),
        ],
        compiler_params=pltpu.CompilerParams(
            collective_id=0, has_side_effects=True, vmem_limit_bytes=60 * 1024 * 1024
        ),
        name="main",
    )(
        tbins, sample, head, weight, cot, err, right.T, gate,
        loss.reshape(latents, per), lbins.reshape(latents, per),
    )
    basis, new_right, gate_grad, hist, grad = pl.pallas_call(
        functools.partial(end_kernel, nbins / (tokens * workers)),
        out_shape=(
            out((rank, share), F32),
            out((rank, share), F32),
            out((nbins, share), F32),
            out((1, nbins), F32),
            out((tokens, feats), BF16),
        ),
        in_specs=[vmem] * 4,
        out_specs=(vmem,) * 5,
        compiler_params=pltpu.CompilerParams(vmem_limit_bytes=60 * 1024 * 1024),
        name="finish",
    )(basis, new_right, gsum, grad)
    return grad, basis.T, new_right.T, gate_grad, hist.reshape(nbins)


def solution(mesh):
    n = math.isqrt(mesh.shape["dp"] // 2)
    assert 2 * n * n == mesh.shape["dp"]
    placed = (
        P("dp", "tensor"),
        P("tensor", None),
        P("dp", None),
        P("dp", "tensor", None),
        P(),
        P(),
        P(),
        P("dp"),
        P("dp"),
        P("dp"),
    )
    return jax.shard_map(
        functools.partial(per_device, n, mesh.shape["tensor"]),
        mesh=mesh,
        in_specs=placed,
        out_specs=(P("dp", "tensor"), P("tensor", None), P("tensor", None), P(None, "tensor"), P()),
        check_vma=False,
    )
```

```python
import functools
import math

import jax
import jax.numpy as jnp
from jax import lax
from jax.experimental import pallas as pl
from jax.experimental.pallas import tpu as pltpu
from jax.sharding import PartitionSpec as P

MESH = pl.DeviceIdType.MESH
F32 = jnp.float32
BF16 = jnp.bfloat16
HIGHEST = lax.Precision.HIGHEST
NN = (((1,), (0,)), ((), ()))
NT = (((1,), (1,)), ((), ()))


def split(x):
    high = x.astype(BF16)
    low = (x - high.astype(F32)).astype(BF16)
    return jnp.concatenate([high, low], axis=0)


def fold(x):
    half = x.shape[0] // 2
    return x[:half] + x[half:]


def eliminate(rows, begin, end):
    groups = len(rows)
    width = rows[0].shape[1]
    sub = lax.broadcasted_iota(jnp.int32, (8, width), 0)
    rows = list(rows)

    def wide(x, j):
        return jnp.broadcast_to(x[:, j : j + 1], (8, width))

    for j in range(begin, end, 2):
        g, r = divmod(j, 8)
        first = [wide(rows[i], j) for i in range(g, groups)]
        second = [wide(rows[i], j + 1) for i in range(g, groups)]
        aa = first[0][r : r + 1]
        ab = first[0][r + 1 : r + 2]
        bb = second[0][r + 1 : r + 2]
        inverse = 1.0 / (aa * bb - ab * ab)
        top = rows[g][r : r + 1]
        low = rows[g][r + 1 : r + 2]
        one = jnp.broadcast_to((bb * inverse) * top - (ab * inverse) * low, (8, width))
        two = jnp.broadcast_to((aa * inverse) * low - (ab * inverse) * top, (8, width))
        for i in range(g, groups):
            change = first[i - g] * one + second[i - g] * two
            if i == g:
                if r == 6:
                    continue
                change = jnp.where(sub > r + 1, change, 0.0)
            rows[i] = rows[i] - change
    return rows


def unscaled_to_inverse(rows):
    out = []
    width = rows[0].shape[1]
    lane = lax.broadcasted_iota(jnp.int32, (8, width), 1)
    sub = lax.broadcasted_iota(jnp.int32, (8, width), 0)
    odd = lax.rem(sub, 2) == 1
    for g, x in enumerate(rows):
        row = sub + 8 * g
        before = jnp.concatenate([x[7:], x[:7]], axis=0)
        over = jnp.sum(jnp.where(lane == row - 1, before, 0.0), axis=1, keepdims=True)
        off = jnp.sum(jnp.where(lane == row - 1, x, 0.0), axis=1, keepdims=True)
        x = jnp.where(odd, x - (off / jnp.where(odd[:, :1], over, 1.0)) * before, x)
        diag = jnp.sum(jnp.where(lane == row, x, 0.0), axis=1, keepdims=True)
        out.append(x / jnp.sqrt(diag))
    return jnp.concatenate(out, axis=0)


def far_first(n):
    return sorted(range(1, n), key=lambda k: -min(k, n - k))


def wrap(value, n):
    return jnp.where(value >= n, value - n, value)


A1, TG, A2, A3, G1, G2, G3, GRAM, XX, C4, C5, PAIR = range(12)


def main_kernel(
    n, nx, workers,
    tb_hbm, sw_hbm, head_hbm, weight_hbm, cot_hbm, err_hbm, right_hbm, gate_hbm, loss_hbm, bins_hbm,
    basis_o, right_o, gate_o, grad_o,
    tb_ref, sw_ref, head, weight, cot, right, gate, loss, bins, load_sem, out_sem,
    both_g, head_t, rstack, scale, own_s, sib_s,
    l_src, l_in, l_mid, l_all,
    g_src, g_in, g_mid, g_all,
    s_src, s_in, s_x, s_xin, s_mid, s_all,
    t_src, t_in, gram, chol, grad_v, gate_v, basis_v, right_v,
    ssem, rsem,
):
    rank = right.shape[0]
    tokens, feats = head.shape
    width = cot.shape[1]
    latents, per = loss.shape
    nbins = gate.shape[0]
    share = width // nx
    half = rank // 2
    piece = half // n
    pairs = 2 * n
    FIRST = PAIR + nx
    order = far_first(n)

    loads = []
    for k, (src, dst) in enumerate(
        (
            (right_hbm, right),
            (tb_hbm, tb_ref),
            (sw_hbm, sw_ref),
            (gate_hbm, gate),
            (cot_hbm, cot),
            (err_hbm.at[0], both_g.at[pl.ds(0, feats)]),
            (head_hbm, head),
            (loss_hbm, loss),
            (bins_hbm, bins),
            (weight_hbm, weight),
        )
    ):
        loads.append(pltpu.make_async_copy(src, dst, load_sem.at[k]))
        loads[-1].start()

    index = lax.axis_index("dp")
    x = lax.axis_index("tensor")
    c = lax.rem(index, 2)
    y = lax.rem(index // 2, n)
    z = index // (2 * n)

    def at_z(j, core):
        return ((j * n + y) * 2 + core, x)

    def at_y(j, core):
        return ((z * n + j) * 2 + core, x)

    a = jnp.where(c == 0, z, y)
    b = jnp.where(c == 0, y, z)

    a_step = jnp.where(c == 0, 2 * n, 2)
    a_base = jnp.where(c == 0, 2 * y, 2 * n * z)
    b_step = jnp.where(c == 0, 2, 2 * n)
    b_base = jnp.where(c == 0, 2 * n * z, 2 * y) + c

    def at_a(j, core):
        return (j * a_step + a_base + core, x)

    def at_b(j):
        return (j * b_step + b_base, x)

    sibling = (index + 1 - 2 * c, x)

    barrier = pltpu.get_barrier_semaphore()

    def greet(device):
        pl.semaphore_signal(barrier, inc=1, device_id=device, device_id_type=MESH)

    for k in order:
        jz = wrap(z + k, n)
        jy = wrap(y + k, n)
        for core in (0, 1):
            greet(at_z(jz, core))
            greet(at_y(jy, core))
    greet(sibling)
    for k in far_first(nx):
        greet((index, wrap(x + k, nx)))

    def remote(src, dst, phase, device):
        return pltpu.make_async_remote_copy(
            src_ref=src, dst_ref=dst, send_sem=ssem.at[phase], recv_sem=rsem.at[phase],
            device_id=device, device_id_type=MESH,
        )

    def scatter_send(src, dst, phase):
        for k in order:
            jz = wrap(z + k, n)
            jy = wrap(y + k, n)
            remote(src.at[jz], dst.at[z * 2 + c], phase, at_z(jz, 0)).start()
            remote(src.at[n + jy], dst.at[y * 2 + c], phase, at_y(jy, 1)).start()

        @pl.when(c == 1)
        def _():
            remote(src.at[z], dst.at[z * 2 + 1], phase, sibling).start()

        @pl.when(c == 0)
        def _():
            remote(src.at[n + y], dst.at[y * 2], phase, sibling).start()

        dst[a * 2 + c] = src[c * n + a]

    def wait_many(ref, count, phase, recv=True):
        part = ref.at[pl.ds(0, count)]
        copy = remote(part, part, phase, sibling)
        if recv:
            copy.wait_recv()
        else:
            copy.wait_send()

    def sum_slots(ref, count):
        out = ref[0]
        for k in range(1, count):
            out = out + ref[k]
        return out

    def ring_send(ref, phase):
        for k in order:
            remote(ref.at[b], ref.at[b], phase, at_b(wrap(b + k, n))).start()

    def gather_send(ref, phase):
        mine = c * n + a
        for k in order:
            j = wrap(a + k, n)
            for core in (0, 1):
                remote(ref.at[mine], ref.at[mine], phase, at_a(j, core)).start()
        remote(ref.at[mine], ref.at[mine], phase, sibling).start()

    loads[0].wait()
    rstack[...] = split(right[...])
    for k in (1, 2, 3):
        loads[k].wait()
    bin_of = lax.broadcasted_iota(jnp.int32, (8, nbins), 1)
    row_of = lax.broadcasted_iota(jnp.int32, (8, nbins), 0)
    onehot = jnp.zeros((8, nbins), F32)
    weights = []
    for l in range(latents):
        tb = tb_ref[l]
        weights.append(sw_ref[tb])
        onehot = jnp.where((row_of == l) & (bin_of == tb), 1.0, onehot)
    gates = lax.dot_general(onehot.astype(BF16), gate[...], NN, preferred_element_type=F32)
    row8 = lax.broadcasted_iota(jnp.int32, (8, width), 0)
    lat8 = jnp.zeros((8, width), F32)
    for l in range(latents):
        lat8 = jnp.where(row8 == l, weights[l], lat8)
    scale[...] = gates * lat8
    for k in (4, 5, 6):
        loads[k].wait()
    for l in range(latents):
        rows = pl.ds(l * per, per)
        both_g[pl.ds(feats + l * per, per), :] = (cot[rows, :].astype(F32) * scale[l : l + 1, :]).astype(BF16)
    mixed = fold(lax.dot_general(both_g[feats:], rstack[...], NT, preferred_element_type=F32).T)
    first = lax.dot_general(both_g[:feats], rstack[...], NT, preferred_element_type=F32)
    left = fold(first.T) + fold(lax.dot_general(split(mixed), head[...], NN, preferred_element_type=F32))
    for k in range(pairs):
        l_src[k] = left[k * piece : (k + 1) * piece]

    pl.semaphore_wait(barrier, 4 * (n - 1) + 1 + (nx - 1))
    scatter_send(l_src, l_in, A1)

    loads[9].wait()
    step_w = 128 if share % 256 else 256
    row_s = lax.broadcasted_iota(jnp.int32, (8, step_w), 0)
    for i in range(width // step_w):
        cols = pl.ds(i * step_w, step_w)
        branch = lax.dot_general(head[...], weight[:, cols], NN, preferred_element_type=F32)
        prod = branch * cot[:, cols].astype(F32)
        out = jnp.zeros((8, step_w), F32)
        for l in range(latents):
            row = jnp.sum(prod[l * per : (l + 1) * per], axis=0, keepdims=True) * weights[l]
            out = jnp.where(row_s == l, row, out)
        t, off = divmod(i * step_w, share)
        t_src[t, :, off : off + step_w] = out
    t_in[x] = t_src[x]
    for k in far_first(nx):
        j = wrap(x + k, nx)
        remote(t_src.at[j], t_in.at[x], TG, (index, j)).start()

    wait_many(l_in, pairs - 1, A1)
    l_mid[b] = sum_slots(l_in, pairs)
    ring_send(l_mid, A2)

    head_t[...] = head[...].T
    loads[7].wait()
    loads[8].wait()
    bin_row = lax.broadcasted_iota(jnp.int32, (nbins, per), 0)
    hist = jnp.zeros((nbins, per), F32)
    for l in range(latents):
        hist = hist + jnp.where(bin_row == bins[l : l + 1, :], weights[l] * loss[l : l + 1, :], 0.0)
    wait_many(t_in, nx - 1, TG)
    lat_sum = sum_slots(t_in, nx)
    bin_s = lax.broadcasted_iota(jnp.int32, (nbins, share), 0)
    spread = jnp.zeros((nbins, share), F32)
    for l in range(latents):
        spread = spread + jnp.where(bin_s == tb_ref[l], lat_sum[l : l + 1, :], 0.0)
    for k in range(pairs):
        g_src[k, :, share:] = hist[k * piece : (k + 1) * piece]
        g_src[k, :, :share] = spread[k * piece : (k + 1) * piece]

    wait_many(l_mid, n - 1, A2)
    l_all[c * n + a] = sum_slots(l_mid, n) * (1.0 / workers)
    gather_send(l_all, A3)
    scatter_send(g_src, g_in, G1)

    grad_v[...] = lax.dot_general(
        both_g[feats:], weight[...], NT, preferred_element_type=F32
    ).astype(BF16)
    outs = [pltpu.make_async_copy(grad_v, grad_o, out_sem.at[0])]
    outs[-1].start()

    wait_many(l_all, pairs - 1, A3)
    left = jnp.concatenate([l_all[k] for k in range(pairs)], axis=0)
    lstack = split(left)
    mixed = fold(lax.dot_general(lstack, head_t[...], NN, preferred_element_type=F32))
    stack = jnp.concatenate([lstack, split(mixed)], axis=1)

    parts = far_first(nx) + [0]
    targets = [wrap(x + k, nx) for k in parts]

    def part_start(i):
        cols = pl.ds(pl.multiple_of(targets[i] * share, 128), share)
        term = fold(lax.dot_general(stack, both_g[:, cols], NN, preferred_element_type=F32))
        own_s[i, 0] = term[:half]
        own_s[i, 1] = term[half:]
        remote(own_s.at[i, 1 - c], sib_s.at[i], PAIR + i, sibling).start()

    def part_scatter(i):
        remote(sib_s.at[i], sib_s.at[i], PAIR + i, sibling).wait_recv()
        total = own_s[i, c] + sib_s[i]
        for k in range(n):
            s_src[i, k] = total[k * piece : (k + 1) * piece]
        s_in[i, a] = s_src[i, a]
        for k in order:
            j = wrap(a + k, n)
            remote(s_src.at[i, j], s_in.at[i, a], FIRST + i, at_a(j, c)).start()

    def part_cross(i):
        wait_many(s_in.at[i], n - 1, FIRST + i)
        total = sum_slots(s_in.at[i], n)
        if parts[i]:
            s_x[i] = total
            remote(s_x.at[i], s_xin.at[x], XX, (index, targets[i])).start()
        else:
            s_xin[x] = total

    part_start(0)
    for i in range(1, nx):
        part_start(i)
        part_scatter(i - 1)
    padded = jnp.concatenate([left, jnp.zeros((128 - rank, share), F32)], axis=0)
    gram[x] = lax.dot_general(left, padded, NT, precision=HIGHEST, preferred_element_type=F32)
    part_scatter(nx - 1)
    for k in far_first(nx):
        remote(gram.at[x], gram.at[x], GRAM, (index, wrap(x + k, nx))).start()
    wait_many(g_in, pairs - 1, G1)
    g_mid[b] = sum_slots(g_in, pairs)
    ring_send(g_mid, G2)
    for i in range(nx - 1):
        part_cross(i)
    groups = rank // 8

    def put(rows):
        for g in range(groups):
            chol[g] = rows[g]

    def get():
        return [chol[g] for g in range(groups)]

    wait_many(gram, nx - 1, GRAM)
    whole = sum_slots(gram, nx)
    eye_r = lax.broadcasted_iota(jnp.int32, (rank, 128), 0)
    eye_c = lax.broadcasted_iota(jnp.int32, (rank, 128), 1)
    whole = jnp.where(eye_c == eye_r + rank, 1.0, whole)
    put(eliminate([whole[8 * g : 8 * g + 8] for g in range(groups)], 0, rank // 4))
    part_cross(nx - 1)

    wait_many(s_xin, nx - 1, XX)
    s_mid[b] = sum_slots(s_xin, nx)
    ring_send(s_mid, C4)

    wait_many(g_mid, n - 1, G2)
    g_all[c * n + a] = sum_slots(g_mid, n)
    gather_send(g_all, G3)
    put(eliminate(get(), rank // 4, 5 * rank // 8))

    wait_many(s_mid, n - 1, C4)
    s_all[c * n + a] = sum_slots(s_mid, n)
    gather_send(s_all, C5)
    rows = eliminate(get(), 5 * rank // 8, rank)
    inverse = unscaled_to_inverse(rows)[:, rank : 2 * rank]
    basis_v[...] = lax.dot_general(inverse, left, NN, precision=HIGHEST, preferred_element_type=F32)
    outs.append(pltpu.make_async_copy(basis_v, basis_o, out_sem.at[1]))
    outs[-1].start()
    wait_many(g_all, pairs - 1, G3)
    for k in range(pairs):
        gate_v[k * piece : (k + 1) * piece] = g_all[k]
    outs.append(pltpu.make_async_copy(gate_v, gate_o, out_sem.at[2]))
    outs[-1].start()
    wait_many(s_all, pairs - 1, C5)
    s_whole = jnp.concatenate([s_all[k] for k in range(pairs)], axis=0)
    right_v[...] = lax.dot_general(
        inverse, s_whole, NN, precision=HIGHEST, preferred_element_type=F32
    ) * (1.0 / workers)
    outs.append(pltpu.make_async_copy(right_v, right_o, out_sem.at[3]))
    outs[-1].start()

    wait_many(l_src, pairs - 1, A1, False)
    wait_many(t_src, nx - 1, TG, False)
    wait_many(l_mid, n - 1, A2, False)
    wait_many(l_all, pairs - 1, A3, False)
    wait_many(g_src, pairs - 1, G1, False)
    for i in range(nx):
        remote(sib_s.at[i], sib_s.at[i], PAIR + i, sibling).wait_send()
        wait_many(s_src.at[i], n - 1, FIRST + i, False)
    wait_many(gram, nx - 1, GRAM, False)
    wait_many(g_mid, n - 1, G2, False)
    wait_many(s_x, nx - 1, XX, False)
    wait_many(s_mid, n - 1, C4, False)
    wait_many(g_all, pairs - 1, G3, False)
    wait_many(s_all, pairs - 1, C5, False)
    for copy in outs:
        copy.wait()


def end_kernel(hist_scale, basis, right, gate, grad, basis_o, right_o, gate_o, hist_o, grad_o):
    share = basis.shape[1]
    basis_o[...] = basis[...]
    right_o[...] = right[...]
    gate_o[...] = gate[:, :share]
    hist_o[...] = jnp.sum(gate[:, share:], axis=1, keepdims=True).T * hist_scale
    grad_o[...] = grad[...]


def per_device(n, nx, head, weight, cot, err, right, gate, sample, tbins, loss, lbins):
    workers = 2 * n * n
    rank = right.shape[1]
    tokens, feats = head.shape
    width = cot.shape[1]
    latents = tbins.shape[0]
    per = tokens // latents
    nbins = gate.shape[0]
    share = width // nx
    half = rank // 2
    piece = half // n
    pairs = 2 * n
    gwidth = share + per
    vmem = pl.BlockSpec(memory_space=pltpu.VMEM)
    hbm = pl.BlockSpec(memory_space=pltpu.HBM)
    V = pltpu.VMEM
    DMA = pltpu.SemaphoreType.DMA
    out = jax.ShapeDtypeStruct
    basis, new_right, gsum, grad = pl.pallas_call(
        functools.partial(main_kernel, n, nx, workers),
        out_shape=(
            out((rank, share), F32),
            out((rank, share), F32),
            out((nbins, gwidth), F32),
            out((tokens, feats), BF16),
        ),
        in_specs=[hbm] * 10,
        out_specs=(hbm,) * 4,
        scratch_shapes=[
            pltpu.SMEM(tbins.shape, jnp.int32),
            pltpu.SMEM(sample.shape, F32),
            V(head.shape, BF16),
            V(weight.shape, BF16),
            V(cot.shape, BF16),
            V((rank, width), F32),
            V(gate.shape, BF16),
            V((latents, per), F32),
            V((latents, per), jnp.int32),
            DMA((10,)),
            DMA((4,)),
            V((feats + tokens, width), BF16),
            V((feats, tokens), BF16),
            V((2 * rank, width), BF16),
            V((8, width), F32),
            V((nx, 2, half, share), F32),
            V((nx, half, share), F32),
            V((pairs, piece, share), F32),
            V((pairs, piece, share), F32),
            V((n, piece, share), F32),
            V((pairs, piece, share), F32),
            V((pairs, piece, gwidth), F32),
            V((pairs, piece, gwidth), F32),
            V((n, piece, gwidth), F32),
            V((pairs, piece, gwidth), F32),
            V((nx, n, piece, share), F32),
            V((nx, n, piece, share), F32),
            V((nx, piece, share), F32),
            V((nx, piece, share), F32),
            V((n, piece, share), F32),
            V((pairs, piece, share), F32),
            V((nx, 8, share), F32),
            V((nx, 8, share), F32),
            V((nx, rank, 128), F32),
            V((rank // 8, 8, 128), F32),
            V((tokens, feats), BF16),
            V((nbins, gwidth), F32),
            V((rank, share), F32),
            V((rank, share), F32),
            DMA((PAIR + 2 * nx,)),
            DMA((PAIR + 2 * nx,)),
        ],
        compiler_params=pltpu.CompilerParams(
            collective_id=0, has_side_effects=True, vmem_limit_bytes=60 * 1024 * 1024
        ),
        name="main",
    )(
        tbins, sample, head, weight, cot, err, right.T, gate,
        loss.reshape(latents, per), lbins.reshape(latents, per),
    )
    basis, new_right, gate_grad, hist, grad = pl.pallas_call(
        functools.partial(end_kernel, nbins / (tokens * workers)),
        out_shape=(
            out((rank, share), F32),
            out((rank, share), F32),
            out((nbins, share), F32),
            out((1, nbins), F32),
            out((tokens, feats), BF16),
        ),
        in_specs=[vmem] * 4,
        out_specs=(vmem,) * 5,
        compiler_params=pltpu.CompilerParams(vmem_limit_bytes=60 * 1024 * 1024),
        name="finish",
    )(basis, new_right, gsum, grad)
    return grad, basis.T, new_right.T, gate_grad, hist.reshape(nbins)


def solution(mesh):
    n = math.isqrt(mesh.shape["dp"] // 2)
    assert 2 * n * n == mesh.shape["dp"]
    placed = (
        P("dp", "tensor"),
        P("tensor", None),
        P("dp", None),
        P("dp", "tensor", None),
        P(),
        P(),
        P(),
        P("dp"),
        P("dp"),
        P("dp"),
    )
    return jax.shard_map(
        functools.partial(per_device, n, mesh.shape["tensor"]),
        mesh=mesh,
        in_specs=placed,
        out_specs=(P("dp", "tensor"), P("tensor", None), P("tensor", None), P(None, "tensor"), P()),
        check_vma=False,
    )
```

```python
import functools
import math

import jax
import jax.numpy as jnp
from jax import lax
from jax.experimental import pallas as pl
from jax.experimental.pallas import tpu as pltpu
from jax.sharding import PartitionSpec as P

MESH = pl.DeviceIdType.MESH
F32 = jnp.float32
BF16 = jnp.bfloat16
HIGHEST = lax.Precision.HIGHEST
NN = (((1,), (0,)), ((), ()))
NT = (((1,), (1,)), ((), ()))


def split(x):
    high = x.astype(BF16)
    low = (x - high.astype(F32)).astype(BF16)
    return jnp.concatenate([high, low], axis=0)


def fold(x):
    half = x.shape[0] // 2
    return x[:half] + x[half:]


def eliminate(rows, begin, end):
    groups = len(rows)
    width = rows[0].shape[1]
    sub = lax.broadcasted_iota(jnp.int32, (8, width), 0)
    rows = list(rows)

    def wide(x, j):
        return jnp.broadcast_to(x[:, j : j + 1], (8, width))

    for j in range(begin, end, 2):
        g, r = divmod(j, 8)
        first = [wide(rows[i], j) for i in range(g, groups)]
        second = [wide(rows[i], j + 1) for i in range(g, groups)]
        aa = first[0][r : r + 1]
        ab = first[0][r + 1 : r + 2]
        bb = second[0][r + 1 : r + 2]
        inverse = 1.0 / (aa * bb - ab * ab)
        top = rows[g][r : r + 1]
        low = rows[g][r + 1 : r + 2]
        one = jnp.broadcast_to((bb * inverse) * top - (ab * inverse) * low, (8, width))
        two = jnp.broadcast_to((aa * inverse) * low - (ab * inverse) * top, (8, width))
        for i in range(g, groups):
            change = first[i - g] * one + second[i - g] * two
            if i == g:
                if r == 6:
                    continue
                change = jnp.where(sub > r + 1, change, 0.0)
            rows[i] = rows[i] - change
    return rows


def unscaled_to_inverse(rows):
    out = []
    width = rows[0].shape[1]
    lane = lax.broadcasted_iota(jnp.int32, (8, width), 1)
    sub = lax.broadcasted_iota(jnp.int32, (8, width), 0)
    odd = lax.rem(sub, 2) == 1
    for g, x in enumerate(rows):
        row = sub + 8 * g
        before = jnp.concatenate([x[7:], x[:7]], axis=0)
        over = jnp.sum(jnp.where(lane == row - 1, before, 0.0), axis=1, keepdims=True)
        off = jnp.sum(jnp.where(lane == row - 1, x, 0.0), axis=1, keepdims=True)
        x = jnp.where(odd, x - (off / jnp.where(odd[:, :1], over, 1.0)) * before, x)
        diag = jnp.sum(jnp.where(lane == row, x, 0.0), axis=1, keepdims=True)
        out.append(x / jnp.sqrt(diag))
    return jnp.concatenate(out, axis=0)


def far_first(n):
    return sorted(range(1, n), key=lambda k: -min(k, n - k))


def wrap(value, n):
    return jnp.where(value >= n, value - n, value)


A1, TG, A2, A3, G1, G2, G3, GRAM, XX, C4, C5, PAIR = range(12)


def main_kernel(
    n, nx, workers, hist_scale,
    tb_hbm, sw_hbm, head_hbm, weight_hbm, cot_hbm, err_hbm, right_hbm, gate_hbm, loss_hbm, bins_hbm,
    right_o, basis_o, gate_o, hist_o, grad_o,
    tb_ref, sw_ref, head, weight, cot, right, gate, loss, bins, load_sem,
    both_g, head_t, rstack, scale, own_s, sib_s,
    l_src, l_in, l_mid, l_all,
    g_src, g_in, g_mid, g_all,
    s_src, s_in, s_x, s_xin, s_mid, s_all,
    t_src, t_in, gram, chol,
    ssem, rsem,
):
    rank = right.shape[0]
    tokens, feats = head.shape
    width = cot.shape[1]
    latents, per = loss.shape
    nbins = gate.shape[0]
    share = width // nx
    half = rank // 2
    piece = half // n
    pairs = 2 * n
    FIRST = PAIR + nx
    order = far_first(n)

    loads = []
    for k, (src, dst) in enumerate(
        (
            (right_hbm, right),
            (tb_hbm, tb_ref),
            (sw_hbm, sw_ref),
            (gate_hbm, gate),
            (cot_hbm, cot),
            (err_hbm.at[0], both_g.at[pl.ds(0, feats)]),
            (head_hbm, head),
            (loss_hbm, loss),
            (bins_hbm, bins),
            (weight_hbm, weight),
        )
    ):
        loads.append(pltpu.make_async_copy(src, dst, load_sem.at[k]))
        loads[-1].start()

    index = lax.axis_index("dp")
    x = lax.axis_index("tensor")
    c = lax.rem(index, 2)
    y = lax.rem(index // 2, n)
    z = index // (2 * n)

    def at_z(j, core):
        return ((j * n + y) * 2 + core, x)

    def at_y(j, core):
        return ((z * n + j) * 2 + core, x)

    a = jnp.where(c == 0, z, y)
    b = jnp.where(c == 0, y, z)

    a_step = jnp.where(c == 0, 2 * n, 2)
    a_base = jnp.where(c == 0, 2 * y, 2 * n * z)
    b_step = jnp.where(c == 0, 2, 2 * n)
    b_base = jnp.where(c == 0, 2 * n * z, 2 * y) + c

    def at_a(j, core):
        return (j * a_step + a_base + core, x)

    def at_b(j):
        return (j * b_step + b_base, x)

    sibling = (index + 1 - 2 * c, x)

    barrier = pltpu.get_barrier_semaphore()

    def greet(device):
        pl.semaphore_signal(barrier, inc=1, device_id=device, device_id_type=MESH)

    for k in order:
        jz = wrap(z + k, n)
        jy = wrap(y + k, n)
        for core in (0, 1):
            greet(at_z(jz, core))
            greet(at_y(jy, core))
    greet(sibling)
    for k in far_first(nx):
        greet((index, wrap(x + k, nx)))

    def remote(src, dst, phase, device):
        return pltpu.make_async_remote_copy(
            src_ref=src, dst_ref=dst, send_sem=ssem.at[phase], recv_sem=rsem.at[phase],
            device_id=device, device_id_type=MESH,
        )

    def scatter_send(src, dst, phase):
        for k in order:
            jz = wrap(z + k, n)
            jy = wrap(y + k, n)
            remote(src.at[jz], dst.at[z * 2 + c], phase, at_z(jz, 0)).start()
            remote(src.at[n + jy], dst.at[y * 2 + c], phase, at_y(jy, 1)).start()

        @pl.when(c == 1)
        def _():
            remote(src.at[z], dst.at[z * 2 + 1], phase, sibling).start()

        @pl.when(c == 0)
        def _():
            remote(src.at[n + y], dst.at[y * 2], phase, sibling).start()

        dst[a * 2 + c] = src[c * n + a]

    def wait_many(ref, count, phase, recv=True):
        part = ref.at[pl.ds(0, count)]
        copy = remote(part, part, phase, sibling)
        if recv:
            copy.wait_recv()
        else:
            copy.wait_send()

    def sum_slots(ref, count):
        out = ref[0]
        for k in range(1, count):
            out = out + ref[k]
        return out

    def ring_send(ref, phase):
        for k in order:
            remote(ref.at[b], ref.at[b], phase, at_b(wrap(b + k, n))).start()

    def gather_send(ref, phase):
        mine = c * n + a
        for k in order:
            j = wrap(a + k, n)
            for core in (0, 1):
                remote(ref.at[mine], ref.at[mine], phase, at_a(j, core)).start()
        remote(ref.at[mine], ref.at[mine], phase, sibling).start()

    loads[0].wait()
    rstack[...] = split(right[...])
    for k in (1, 2, 3):
        loads[k].wait()
    bin_of = lax.broadcasted_iota(jnp.int32, (8, nbins), 1)
    row_of = lax.broadcasted_iota(jnp.int32, (8, nbins), 0)
    onehot = jnp.zeros((8, nbins), F32)
    weights = []
    for l in range(latents):
        tb = tb_ref[l]
        weights.append(sw_ref[tb])
        onehot = jnp.where((row_of == l) & (bin_of == tb), 1.0, onehot)
    gates = lax.dot_general(onehot.astype(BF16), gate[...], NN, preferred_element_type=F32)
    row8 = lax.broadcasted_iota(jnp.int32, (8, width), 0)
    lat8 = jnp.zeros((8, width), F32)
    for l in range(latents):
        lat8 = jnp.where(row8 == l, weights[l], lat8)
    scale[...] = gates * lat8
    for k in (4, 5, 6):
        loads[k].wait()
    for l in range(latents):
        rows = pl.ds(l * per, per)
        both_g[pl.ds(feats + l * per, per), :] = (cot[rows, :].astype(F32) * scale[l : l + 1, :]).astype(BF16)
    mixed = fold(lax.dot_general(both_g[feats:], rstack[...], NT, preferred_element_type=F32).T)
    first = lax.dot_general(both_g[:feats], rstack[...], NT, preferred_element_type=F32)
    left = fold(first.T) + fold(lax.dot_general(split(mixed), head[...], NN, preferred_element_type=F32))
    for k in range(pairs):
        l_src[k] = left[k * piece : (k + 1) * piece]

    pl.semaphore_wait(barrier, 4 * (n - 1) + 1 + (nx - 1))
    scatter_send(l_src, l_in, A1)

    loads[9].wait()
    step_w = 128 if share % 256 else 256
    row_s = lax.broadcasted_iota(jnp.int32, (8, step_w), 0)
    for i in range(width // step_w):
        cols = pl.ds(i * step_w, step_w)
        branch = lax.dot_general(head[...], weight[:, cols], NN, preferred_element_type=F32)
        prod = branch * cot[:, cols].astype(F32)
        out = jnp.zeros((8, step_w), F32)
        for l in range(latents):
            row = jnp.sum(prod[l * per : (l + 1) * per], axis=0, keepdims=True) * weights[l]
            out = jnp.where(row_s == l, row, out)
        t, off = divmod(i * step_w, share)
        t_src[t, :, off : off + step_w] = out
    t_in[x] = t_src[x]
    for k in far_first(nx):
        j = wrap(x + k, nx)
        remote(t_src.at[j], t_in.at[x], TG, (index, j)).start()

    wait_many(l_in, pairs - 1, A1)
    l_mid[b] = sum_slots(l_in, pairs)
    ring_send(l_mid, A2)

    head_t[...] = head[...].T
    loads[7].wait()
    loads[8].wait()
    bin_row = lax.broadcasted_iota(jnp.int32, (nbins, per), 0)
    hist = jnp.zeros((nbins, per), F32)
    for l in range(latents):
        hist = hist + jnp.where(bin_row == bins[l : l + 1, :], weights[l] * loss[l : l + 1, :], 0.0)
    wait_many(t_in, nx - 1, TG)
    lat_sum = sum_slots(t_in, nx)
    bin_s = lax.broadcasted_iota(jnp.int32, (nbins, share), 0)
    spread = jnp.zeros((nbins, share), F32)
    for l in range(latents):
        spread = spread + jnp.where(bin_s == tb_ref[l], lat_sum[l : l + 1, :], 0.0)
    for k in range(pairs):
        g_src[k, :, share:] = hist[k * piece : (k + 1) * piece]
        g_src[k, :, :share] = spread[k * piece : (k + 1) * piece]
    scatter_send(g_src, g_in, G1)

    wait_many(l_mid, n - 1, A2)
    l_all[c * n + a] = sum_slots(l_mid, n) * (1.0 / workers)
    gather_send(l_all, A3)

    grad_o[...] = lax.dot_general(
        both_g[feats:], weight[...], NT, preferred_element_type=F32
    ).astype(BF16)
    wait_many(g_in, pairs - 1, G1)
    g_mid[b] = sum_slots(g_in, pairs)
    ring_send(g_mid, G2)

    wait_many(l_all, pairs - 1, A3)
    left = jnp.concatenate([l_all[k] for k in range(pairs)], axis=0)
    lstack = split(left)
    mixed = fold(lax.dot_general(lstack, head_t[...], NN, preferred_element_type=F32))
    stack = jnp.concatenate([lstack, split(mixed)], axis=1)

    parts = far_first(nx) + [0]
    targets = [wrap(x + k, nx) for k in parts]

    def part_start(i):
        cols = pl.ds(pl.multiple_of(targets[i] * share, 128), share)
        term = fold(lax.dot_general(stack, both_g[:, cols], NN, preferred_element_type=F32))
        own_s[i, 0] = term[:half]
        own_s[i, 1] = term[half:]
        remote(own_s.at[i, 1 - c], sib_s.at[i], PAIR + i, sibling).start()

    def part_scatter(i):
        remote(sib_s.at[i], sib_s.at[i], PAIR + i, sibling).wait_recv()
        total = own_s[i, c] + sib_s[i]
        for k in range(n):
            s_src[i, k] = total[k * piece : (k + 1) * piece]
        s_in[i, a] = s_src[i, a]
        for k in order:
            j = wrap(a + k, n)
            remote(s_src.at[i, j], s_in.at[i, a], FIRST + i, at_a(j, c)).start()

    def part_cross(i):
        wait_many(s_in.at[i], n - 1, FIRST + i)
        total = sum_slots(s_in.at[i], n)
        if parts[i]:
            s_x[i] = total
            remote(s_x.at[i], s_xin.at[x], XX, (index, targets[i])).start()
        else:
            s_xin[x] = total

    lead = min(nx, 3)
    for i in range(lead):
        part_start(i)
    for i in range(lead, nx):
        part_scatter(i - lead)
        part_start(i)
    padded = jnp.concatenate([left, jnp.zeros((128 - rank, share), F32)], axis=0)
    gram[x] = lax.dot_general(left, padded, NT, precision=HIGHEST, preferred_element_type=F32)
    for i in range(nx - lead, nx):
        part_scatter(i)
    for k in far_first(nx):
        remote(gram.at[x], gram.at[x], GRAM, (index, wrap(x + k, nx))).start()
    wait_many(g_mid, n - 1, G2)
    g_all[c * n + a] = sum_slots(g_mid, n)
    gather_send(g_all, G3)
    for i in range(nx - 1):
        part_cross(i)
    groups = rank // 8

    def put(rows):
        for g in range(groups):
            chol[g] = rows[g]

    def get():
        return [chol[g] for g in range(groups)]

    wait_many(gram, nx - 1, GRAM)
    whole = sum_slots(gram, nx)
    eye_r = lax.broadcasted_iota(jnp.int32, (rank, 128), 0)
    eye_c = lax.broadcasted_iota(jnp.int32, (rank, 128), 1)
    whole = jnp.where(eye_c == eye_r + rank, 1.0, whole)
    put(eliminate([whole[8 * g : 8 * g + 8] for g in range(groups)], 0, rank // 4))
    part_cross(nx - 1)

    wait_many(s_xin, nx - 1, XX)
    s_mid[b] = sum_slots(s_xin, nx)
    ring_send(s_mid, C4)

    put(eliminate(get(), rank // 4, 5 * rank // 8))

    wait_many(s_mid, n - 1, C4)
    s_all[c * n + a] = sum_slots(s_mid, n)
    gather_send(s_all, C5)
    rows = eliminate(get(), 5 * rank // 8, rank)
    inverse = unscaled_to_inverse(rows)[:, rank : 2 * rank]
    basis_o[...] = lax.dot_general(inverse, left, NN, precision=HIGHEST, preferred_element_type=F32)
    wait_many(g_all, pairs - 1, G3)
    gates = jnp.concatenate([g_all[k] for k in range(pairs)], axis=0)
    gate_o[...] = gates[:, :share]
    hist_o[...] = jnp.sum(gates[:, share:], axis=1, keepdims=True).T * hist_scale
    wait_many(s_all, pairs - 1, C5)
    s_whole = jnp.concatenate([s_all[k] for k in range(pairs)], axis=0)
    right_o[...] = lax.dot_general(
        inverse, s_whole, NN, precision=HIGHEST, preferred_element_type=F32
    ) * (1.0 / workers)

    wait_many(l_src, pairs - 1, A1, False)
    wait_many(t_src, nx - 1, TG, False)
    wait_many(l_mid, n - 1, A2, False)
    wait_many(l_all, pairs - 1, A3, False)
    wait_many(g_src, pairs - 1, G1, False)
    for i in range(nx):
        remote(sib_s.at[i], sib_s.at[i], PAIR + i, sibling).wait_send()
        wait_many(s_src.at[i], n - 1, FIRST + i, False)
    wait_many(gram, nx - 1, GRAM, False)
    wait_many(g_mid, n - 1, G2, False)
    wait_many(s_x, nx - 1, XX, False)
    wait_many(s_mid, n - 1, C4, False)
    wait_many(g_all, pairs - 1, G3, False)
    wait_many(s_all, pairs - 1, C5, False)


def end_kernel(*refs):
    count = len(refs) // 2
    sem = refs[-1]
    copies = [pltpu.make_async_copy(refs[k], refs[count + k], sem.at[k]) for k in range(count)]
    for copy in copies:
        copy.start()
    for copy in copies:
        copy.wait()


def per_device(n, nx, head, weight, cot, err, right, gate, sample, tbins, loss, lbins):
    workers = 2 * n * n
    rank = right.shape[1]
    tokens, feats = head.shape
    width = cot.shape[1]
    latents = tbins.shape[0]
    per = tokens // latents
    nbins = gate.shape[0]
    share = width // nx
    half = rank // 2
    piece = half // n
    pairs = 2 * n
    gwidth = share + per
    vmem = pl.BlockSpec(memory_space=pltpu.VMEM)
    hbm = pl.BlockSpec(memory_space=pltpu.HBM)
    V = pltpu.VMEM
    DMA = pltpu.SemaphoreType.DMA
    out = jax.ShapeDtypeStruct
    operands = (
        tbins, sample, head, weight, cot, err, right.T, gate,
        loss.reshape(latents, per), lbins.reshape(latents, per),
    )
    kinds = (
        ((rank, share), F32),
        ((rank, share), F32),
        ((nbins, share), F32),
        ((1, nbins), F32),
        ((tokens, feats), BF16),
    )
    results = pl.pallas_call(
        functools.partial(main_kernel, n, nx, workers, nbins / (tokens * workers)),
        out_shape=tuple(V(shape, dtype) for shape, dtype in kinds),
        in_specs=[hbm] * 10,
        out_specs=(vmem,) * 5,
        scratch_shapes=[
            pltpu.SMEM(tbins.shape, jnp.int32),
            pltpu.SMEM(sample.shape, F32),
            V(head.shape, BF16),
            V(weight.shape, BF16),
            V(cot.shape, BF16),
            V((rank, width), F32),
            V(gate.shape, BF16),
            V((latents, per), F32),
            V((latents, per), jnp.int32),
            DMA((10,)),
            V((feats + tokens, width), BF16),
            V((feats, tokens), BF16),
            V((2 * rank, width), BF16),
            V((8, width), F32),
            V((nx, 2, half, share), F32),
            V((nx, half, share), F32),
            V((pairs, piece, share), F32),
            V((pairs, piece, share), F32),
            V((n, piece, share), F32),
            V((pairs, piece, share), F32),
            V((pairs, piece, gwidth), F32),
            V((pairs, piece, gwidth), F32),
            V((n, piece, gwidth), F32),
            V((pairs, piece, gwidth), F32),
            V((nx, n, piece, share), F32),
            V((nx, n, piece, share), F32),
            V((nx, piece, share), F32),
            V((nx, piece, share), F32),
            V((n, piece, share), F32),
            V((pairs, piece, share), F32),
            V((nx, 8, share), F32),
            V((nx, 8, share), F32),
            V((nx, rank, 128), F32),
            V((rank // 8, 8, 128), F32),
            DMA((PAIR + 2 * nx,)),
            DMA((PAIR + 2 * nx,)),
        ],
        compiler_params=pltpu.CompilerParams(
            collective_id=0, has_side_effects=True, vmem_limit_bytes=32 * 1024 * 1024
        ),
        name="main",
    )(*[pltpu.with_memory_space_constraint(v, pltpu.HBM) for v in operands])
    new_right, basis, gate_grad, hist, grad = pl.pallas_call(
        end_kernel,
        out_shape=tuple(out(shape, dtype) for shape, dtype in kinds),
        in_specs=[vmem] * 5,
        out_specs=(hbm,) * 5,
        scratch_shapes=[DMA((5,))],
        compiler_params=pltpu.CompilerParams(vmem_limit_bytes=8 * 1024 * 1024),
        name="finish",
    )(*results)
    return grad, basis.T, new_right.T, gate_grad, hist.reshape(nbins)


def solution(mesh):
    n = math.isqrt(mesh.shape["dp"] // 2)
    assert 2 * n * n == mesh.shape["dp"]
    placed = (
        P("dp", "tensor"),
        P("tensor", None),
        P("dp", None),
        P("dp", "tensor", None),
        P(),
        P(),
        P(),
        P("dp"),
        P("dp"),
        P("dp"),
    )
    return jax.shard_map(
        functools.partial(per_device, n, mesh.shape["tensor"]),
        mesh=mesh,
        in_specs=placed,
        out_specs=(P("dp", "tensor"), P("tensor", None), P("tensor", None), P(None, "tensor"), P()),
        check_vma=False,
    )
```

```python
import functools
import math

import jax
import jax.numpy as jnp
from jax import lax
from jax.experimental import pallas as pl
from jax.experimental.pallas import tpu as pltpu
from jax.sharding import PartitionSpec as P

MESH = pl.DeviceIdType.MESH
F32 = jnp.float32
BF16 = jnp.bfloat16
HIGHEST = lax.Precision.HIGHEST
NN = (((1,), (0,)), ((), ()))
NT = (((1,), (1,)), ((), ()))


def split(x):
    high = x.astype(BF16)
    low = (x - high.astype(F32)).astype(BF16)
    return jnp.concatenate([high, low], axis=0)


def fold(x):
    half = x.shape[0] // 2
    return x[:half] + x[half:]


def eliminate(ref, begin, end):
    groups, _, width = ref.shape
    sub = lax.broadcasted_iota(jnp.int32, (8, width), 0)

    def wide(x, j):
        return jnp.broadcast_to(x[:, j : j + 1], (8, width))

    def block(k, carry):
        own = ref[k]
        rows = [ref[g] for g in range(groups)]
        for r in range(0, 8, 2):
            first, second = wide(own, r), wide(own, r + 1)
            aa = first[r : r + 1]
            ab = first[r + 1 : r + 2]
            bb = second[r + 1 : r + 2]
            inverse = 1.0 / (aa * bb - ab * ab)
            top = own[r : r + 1]
            low = own[r + 1 : r + 2]
            one = jnp.broadcast_to((bb * inverse) * top - (ab * inverse) * low, (8, width))
            two = jnp.broadcast_to((aa * inverse) * low - (ab * inverse) * top, (8, width))
            if r < 6:
                own = own - jnp.where(sub > r + 1, first * one + second * two, 0.0)
            for g in range(groups):
                change = wide(rows[g], r) * one + wide(rows[g], r + 1) * two
                rows[g] = rows[g] - jnp.where(g > k, change, 0.0)
        for g in range(groups):
            ref[g] = pltpu.roll(jnp.where(g == k, own, rows[g]), width - 8, 1)
        return carry

    lax.fori_loop(begin, end, block, 0)


def unscaled_to_inverse(rows, rank):
    out = []
    width = rows[0].shape[1]
    lane = lax.broadcasted_iota(jnp.int32, (8, width), 1)
    sub = lax.broadcasted_iota(jnp.int32, (8, width), 0)
    odd = lax.rem(sub, 2) == 1
    for g, x in enumerate(rows):
        row = sub + (8 * g + rank)
        before = jnp.concatenate([x[7:], x[:7]], axis=0)
        over = jnp.sum(jnp.where(lane == row - 1, before, 0.0), axis=1, keepdims=True)
        off = jnp.sum(jnp.where(lane == row - 1, x, 0.0), axis=1, keepdims=True)
        x = jnp.where(odd, x - (off / jnp.where(odd[:, :1], over, 1.0)) * before, x)
        diag = jnp.sum(jnp.where(lane == row, x, 0.0), axis=1, keepdims=True)
        out.append(x / jnp.sqrt(diag))
    return jnp.concatenate(out, axis=0)


def far_first(i, n):
    return n // 2 + ((i + 1) // 2) * (1 - 2 * (i % 2))


def each(count, step):
    def body(i, carry):
        step(i)
        return carry

    lax.fori_loop(0, count, body, 0)


def wrap(value, n):
    return jnp.where(value >= n, value - n, value)


A1, TG, A2, A3, G1, G2, G3, GRAM, XX, C4, C5, PAIR = range(12)


def main_kernel(
    n, nx, workers, hist_scale,
    tb_hbm, sw_hbm, head_hbm, weight_hbm, cot_hbm, err_hbm, right_hbm, gate_hbm, loss_hbm, bins_hbm,
    right_o, basis_o, gate_o, hist_o, grad_o,
    tb_ref, sw_ref, head, weight, cot, right, gate, loss, bins, load_sem,
    both_g, head_t, rstack, scale, left_v, stack_v, own_s, sib_s,
    l_src, l_in, l_mid, l_all,
    g_src, g_in, g_mid, g_all,
    s_src, s_in, s_x, s_xin, s_mid, s_all,
    t_src, t_in, gram, chol,
    ssem, rsem,
):
    rank = right.shape[0]
    tokens, feats = head.shape
    width = cot.shape[1]
    latents, per = loss.shape
    nbins = gate.shape[0]
    share = width // nx
    half = rank // 2
    piece = half // n
    pairs = 2 * n
    FIRST = PAIR + nx

    loads = []
    for k, (src, dst) in enumerate(
        (
            (right_hbm, right),
            (tb_hbm, tb_ref),
            (sw_hbm, sw_ref),
            (gate_hbm, gate),
            (cot_hbm, cot),
            (err_hbm.at[0], both_g.at[pl.ds(0, feats)]),
            (head_hbm, head),
            (loss_hbm, loss),
            (bins_hbm, bins),
            (weight_hbm, weight),
        )
    ):
        loads.append(pltpu.make_async_copy(src, dst, load_sem.at[k]))
        loads[-1].start()

    index = lax.axis_index("dp")
    x = lax.axis_index("tensor")
    c = lax.rem(index, 2)
    y = lax.rem(index // 2, n)
    z = index // (2 * n)

    def at_z(j, core):
        return ((j * n + y) * 2 + core, x)

    def at_y(j, core):
        return ((z * n + j) * 2 + core, x)

    a = jnp.where(c == 0, z, y)
    b = jnp.where(c == 0, y, z)

    a_step = jnp.where(c == 0, 2 * n, 2)
    a_base = jnp.where(c == 0, 2 * y, 2 * n * z)
    b_step = jnp.where(c == 0, 2, 2 * n)
    b_base = jnp.where(c == 0, 2 * n * z, 2 * y) + c

    def at_a(j, core):
        return (j * a_step + a_base + core, x)

    def at_b(j):
        return (j * b_step + b_base, x)

    sibling = (index + 1 - 2 * c, x)

    barrier = pltpu.get_barrier_semaphore()

    def greet(device):
        pl.semaphore_signal(barrier, inc=1, device_id=device, device_id_type=MESH)

    @functools.partial(each, n - 1)
    def _(i):
        k = far_first(i, n)
        jz = wrap(z + k, n)
        jy = wrap(y + k, n)
        for core in (0, 1):
            greet(at_z(jz, core))
            greet(at_y(jy, core))

    greet(sibling)

    @functools.partial(each, nx - 1)
    def _(i):
        greet((index, wrap(x + far_first(i, nx), nx)))

    def remote(src, dst, phase, device):
        return pltpu.make_async_remote_copy(
            src_ref=src, dst_ref=dst, send_sem=ssem.at[phase], recv_sem=rsem.at[phase],
            device_id=device, device_id_type=MESH,
        )

    def scatter_send(src, dst, phase):
        @functools.partial(each, n - 1)
        def _(i):
            k = far_first(i, n)
            jz = wrap(z + k, n)
            jy = wrap(y + k, n)
            remote(src.at[jz], dst.at[z * 2 + c], phase, at_z(jz, 0)).start()
            remote(src.at[n + jy], dst.at[y * 2 + c], phase, at_y(jy, 1)).start()

        @pl.when(c == 1)
        def _():
            remote(src.at[z], dst.at[z * 2 + 1], phase, sibling).start()

        @pl.when(c == 0)
        def _():
            remote(src.at[n + y], dst.at[y * 2], phase, sibling).start()

        dst[a * 2 + c] = src[c * n + a]

    def wait_many(ref, count, phase, recv=True):
        part = ref.at[pl.ds(0, count)]
        copy = remote(part, part, phase, sibling)
        if recv:
            copy.wait_recv()
        else:
            copy.wait_send()

    def sum_slots(ref, count):
        out = ref[0]
        for k in range(1, count):
            out = out + ref[k]
        return out

    def ring_send(ref, phase):
        @functools.partial(each, n - 1)
        def _(i):
            remote(ref.at[b], ref.at[b], phase, at_b(wrap(b + far_first(i, n), n))).start()

    def gather_send(ref, phase):
        mine = c * n + a

        @functools.partial(each, n - 1)
        def _(i):
            j = wrap(a + far_first(i, n), n)
            for core in (0, 1):
                remote(ref.at[mine], ref.at[mine], phase, at_a(j, core)).start()

        remote(ref.at[mine], ref.at[mine], phase, sibling).start()

    loads[0].wait()
    rstack[...] = split(right[...])
    for k in (1, 2, 3):
        loads[k].wait()
    bin_of = lax.broadcasted_iota(jnp.int32, (8, nbins), 1)
    row_of = lax.broadcasted_iota(jnp.int32, (8, nbins), 0)
    onehot = jnp.zeros((8, nbins), F32)
    weights = []
    for l in range(latents):
        tb = tb_ref[l]
        weights.append(sw_ref[tb])
        onehot = jnp.where((row_of == l) & (bin_of == tb), 1.0, onehot)
    gates = lax.dot_general(onehot.astype(BF16), gate[...], NN, preferred_element_type=F32)
    row8 = lax.broadcasted_iota(jnp.int32, (8, width), 0)
    lat8 = jnp.zeros((8, width), F32)
    for l in range(latents):
        lat8 = jnp.where(row8 == l, weights[l], lat8)
    scale[...] = gates * lat8
    for k in (4, 5, 6):
        loads[k].wait()

    @functools.partial(each, feats // 128)
    def _(i):
        rows = pl.ds(pl.multiple_of(i * 128, 128), 128)
        term = lax.dot_general(both_g[rows, :], rstack[...], NT, preferred_element_type=F32)
        left_v[:, rows] = fold(term.T)

    @functools.partial(each, latents)
    def _(l):
        rows = pl.ds(pl.multiple_of(l * per, per), per)
        part = (cot[rows, :].astype(F32) * scale[pl.ds(l, 1), :]).astype(BF16)
        both_g[pl.ds(pl.multiple_of(feats + l * per, per), per), :] = part
        mixed = fold(lax.dot_general(part, rstack[...], NT, preferred_element_type=F32).T)
        left_v[...] += fold(lax.dot_general(split(mixed), head[rows, :], NN, preferred_element_type=F32))

    left = left_v[...]
    for k in range(pairs):
        l_src[k] = left[k * piece : (k + 1) * piece]

    pl.semaphore_wait(barrier, 4 * (n - 1) + 1 + (nx - 1))
    scatter_send(l_src, l_in, A1)

    loads[9].wait()
    row_s = lax.broadcasted_iota(jnp.int32, (8, share), 0)

    @functools.partial(each, nx)
    def _(t):
        cols = pl.ds(pl.multiple_of(t * share, 128), share)
        out = jnp.zeros((8, share), F32)
        for l in range(latents):
            rows = pl.ds(l * per, per)
            branch = lax.dot_general(head[rows, :], weight[:, cols], NN, preferred_element_type=F32)
            row = jnp.sum(branch * cot[rows, cols].astype(F32), axis=0, keepdims=True) * weights[l]
            out = jnp.where(row_s == l, row, out)
        t_src[t] = out

    t_in[x] = t_src[x]

    @functools.partial(each, nx - 1)
    def _(i):
        j = wrap(x + far_first(i, nx), nx)
        remote(t_src.at[j], t_in.at[x], TG, (index, j)).start()

    wait_many(l_in, pairs - 1, A1)
    l_mid[b] = sum_slots(l_in, pairs)
    ring_send(l_mid, A2)

    head_t[...] = head[...].T
    loads[7].wait()
    loads[8].wait()
    bin_row = lax.broadcasted_iota(jnp.int32, (nbins, per), 0)
    hist = jnp.zeros((nbins, per), F32)
    for l in range(latents):
        hist = hist + jnp.where(bin_row == bins[l : l + 1, :], weights[l] * loss[l : l + 1, :], 0.0)
    wait_many(t_in, nx - 1, TG)
    lat_sum = sum_slots(t_in, nx)
    bin_s = lax.broadcasted_iota(jnp.int32, (nbins, share), 0)
    spread = jnp.zeros((nbins, share), F32)
    for l in range(latents):
        spread = spread + jnp.where(bin_s == tb_ref[l], lat_sum[l : l + 1, :], 0.0)
    for k in range(pairs):
        g_src[k, :, share:] = hist[k * piece : (k + 1) * piece]
        g_src[k, :, :share] = spread[k * piece : (k + 1) * piece]
    scatter_send(g_src, g_in, G1)

    wait_many(l_mid, n - 1, A2)
    l_all[c * n + a] = sum_slots(l_mid, n) * (1.0 / workers)
    gather_send(l_all, A3)

    @functools.partial(each, latents)
    def _(l):
        grad_o[pl.ds(pl.multiple_of(l * per, per), per), :] = lax.dot_general(
            both_g[pl.ds(pl.multiple_of(feats + l * per, per), per), :], weight[...], NT, preferred_element_type=F32
        ).astype(BF16)

    wait_many(g_in, pairs - 1, G1)
    g_mid[b] = sum_slots(g_in, pairs)
    ring_send(g_mid, G2)

    wait_many(l_all, pairs - 1, A3)
    left = jnp.concatenate([l_all[k] for k in range(pairs)], axis=0)
    lstack = split(left)
    mixed = fold(lax.dot_general(lstack, head_t[...], NN, preferred_element_type=F32))
    stack = jnp.concatenate([lstack, split(mixed)], axis=1)

    stack_v[...] = stack

    def target(i):
        return wrap(x + far_first(i, nx), nx)

    def part_start(i):
        cols = pl.ds(pl.multiple_of(target(i) * share, 128), share)
        term = fold(lax.dot_general(stack_v[...], both_g[:, cols], NN, preferred_element_type=F32))
        own_s[i, 0] = term[:half]
        own_s[i, 1] = term[half:]
        remote(own_s.at[i, 1 - c], sib_s.at[i], PAIR + i, sibling).start()

    def part_scatter(i):
        remote(sib_s.at[i], sib_s.at[i], PAIR + i, sibling).wait_recv()
        total = own_s[i, c] + sib_s[i]
        for k in range(n):
            s_src[i, k] = total[k * piece : (k + 1) * piece]
        s_in[i, a] = s_src[i, a]

        @functools.partial(each, n - 1)
        def _(k):
            j = wrap(a + far_first(k, n), n)
            remote(s_src.at[i, j], s_in.at[i, a], FIRST + i, at_a(j, c)).start()

    def part_sum(i):
        wait_many(s_in.at[i], n - 1, FIRST + i)
        total = s_in[i, 0]
        for k in range(1, n):
            total = total + s_in[i, k]
        return total

    lead = min(nx, 2)

    @functools.partial(each, nx + lead)
    def _(i):
        @pl.when(i < nx)
        def _():
            part_start(i)

        @pl.when(i >= lead)
        def _():
            part_scatter(i - lead)

    padded = jnp.concatenate([left, jnp.zeros((128 - rank, share), F32)], axis=0)
    gram[x] = lax.dot_general(left, padded, NT, precision=HIGHEST, preferred_element_type=F32)

    @functools.partial(each, nx - 1)
    def _(i):
        remote(gram.at[x], gram.at[x], GRAM, (index, target(i))).start()

    wait_many(g_mid, n - 1, G2)
    g_all[c * n + a] = sum_slots(g_mid, n)
    gather_send(g_all, G3)

    @functools.partial(each, nx - 1)
    def _(i):
        s_x[i] = part_sum(i)
        remote(s_x.at[i], s_xin.at[x], XX, (index, target(i))).start()

    groups = rank // 8
    wait_many(gram, nx - 1, GRAM)
    whole = sum_slots(gram, nx)
    eye_r = lax.broadcasted_iota(jnp.int32, (rank, 128), 0)
    eye_c = lax.broadcasted_iota(jnp.int32, (rank, 128), 1)
    whole = jnp.where(eye_c == eye_r + rank, 1.0, whole)
    for g in range(groups):
        chol[g] = whole[8 * g : 8 * g + 8]
    eliminate(chol, 0, groups // 4)
    s_xin[x] = part_sum(nx - 1)

    wait_many(s_xin, nx - 1, XX)
    s_mid[b] = sum_slots(s_xin, nx)
    ring_send(s_mid, C4)

    eliminate(chol, groups // 4, 5 * groups // 8)

    wait_many(s_mid, n - 1, C4)
    s_all[c * n + a] = sum_slots(s_mid, n)
    gather_send(s_all, C5)
    eliminate(chol, 5 * groups // 8, groups)
    inverse = unscaled_to_inverse([chol[g] for g in range(groups)], rank)[:, :rank]
    basis_o[...] = lax.dot_general(inverse, left, NN, precision=HIGHEST, preferred_element_type=F32)
    wait_many(g_all, pairs - 1, G3)
    gates = jnp.concatenate([g_all[k] for k in range(pairs)], axis=0)
    gate_o[...] = gates[:, :share]
    hist_o[...] = jnp.sum(gates[:, share:], axis=1, keepdims=True).T * hist_scale
    wait_many(s_all, pairs - 1, C5)
    s_whole = jnp.concatenate([s_all[k] for k in range(pairs)], axis=0)
    right_o[...] = lax.dot_general(
        inverse, s_whole, NN, precision=HIGHEST, preferred_element_type=F32
    ) * (1.0 / workers)

    wait_many(l_src, pairs - 1, A1, False)
    wait_many(t_src, nx - 1, TG, False)
    wait_many(l_mid, n - 1, A2, False)
    wait_many(l_all, pairs - 1, A3, False)
    wait_many(g_src, pairs - 1, G1, False)

    @functools.partial(each, nx)
    def _(i):
        remote(sib_s.at[i], sib_s.at[i], PAIR + i, sibling).wait_send()
        wait_many(s_src.at[i], n - 1, FIRST + i, False)

    wait_many(gram, nx - 1, GRAM, False)
    wait_many(g_mid, n - 1, G2, False)
    wait_many(s_x, nx - 1, XX, False)
    wait_many(s_mid, n - 1, C4, False)
    wait_many(g_all, pairs - 1, G3, False)
    wait_many(s_all, pairs - 1, C5, False)


def end_kernel(*refs):
    count = len(refs) // 2
    sem = refs[-1]
    copies = [pltpu.make_async_copy(refs[k], refs[count + k], sem.at[k]) for k in range(count)]
    for copy in copies:
        copy.start()
    for copy in copies:
        copy.wait()


def per_device(n, nx, head, weight, cot, err, right, gate, sample, tbins, loss, lbins):
    workers = 2 * n * n
    rank = right.shape[1]
    tokens, feats = head.shape
    width = cot.shape[1]
    latents = tbins.shape[0]
    per = tokens // latents
    nbins = gate.shape[0]
    share = width // nx
    half = rank // 2
    piece = half // n
    pairs = 2 * n
    gwidth = share + per
    vmem = pl.BlockSpec(memory_space=pltpu.VMEM)
    hbm = pl.BlockSpec(memory_space=pltpu.HBM)
    V = pltpu.VMEM
    DMA = pltpu.SemaphoreType.DMA
    out = jax.ShapeDtypeStruct
    operands = (
        tbins, sample, head, weight, cot, err, right.T, gate,
        loss.reshape(latents, per), lbins.reshape(latents, per),
    )
    kinds = (
        ((rank, share), F32),
        ((rank, share), F32),
        ((nbins, share), F32),
        ((1, nbins), F32),
        ((tokens, feats), BF16),
    )
    results = pl.pallas_call(
        functools.partial(main_kernel, n, nx, workers, nbins / (tokens * workers)),
        out_shape=tuple(V(shape, dtype) for shape, dtype in kinds),
        in_specs=[hbm] * 10,
        out_specs=(vmem,) * 5,
        scratch_shapes=[
            pltpu.SMEM(tbins.shape, jnp.int32),
            pltpu.SMEM(sample.shape, F32),
            V(head.shape, BF16),
            V(weight.shape, BF16),
            V(cot.shape, BF16),
            V((rank, width), F32),
            V(gate.shape, BF16),
            V((latents, per), F32),
            V((latents, per), jnp.int32),
            DMA((10,)),
            V((feats + tokens, width), BF16),
            V((feats, tokens), BF16),
            V((2 * rank, width), BF16),
            V((8, width), F32),
            V((rank, share), F32),
            V((2 * rank, feats + tokens), BF16),
            V((nx, 2, half, share), F32),
            V((nx, half, share), F32),
            V((pairs, piece, share), F32),
            V((pairs, piece, share), F32),
            V((n, piece, share), F32),
            V((pairs, piece, share), F32),
            V((pairs, piece, gwidth), F32),
            V((pairs, piece, gwidth), F32),
            V((n, piece, gwidth), F32),
            V((pairs, piece, gwidth), F32),
            V((nx, n, piece, share), F32),
            V((nx, n, piece, share), F32),
            V((nx, piece, share), F32),
            V((nx, piece, share), F32),
            V((n, piece, share), F32),
            V((pairs, piece, share), F32),
            V((nx, 8, share), F32),
            V((nx, 8, share), F32),
            V((nx, rank, 128), F32),
            V((rank // 8, 8, 128), F32),
            DMA((PAIR + 2 * nx,)),
            DMA((PAIR + 2 * nx,)),
        ],
        compiler_params=pltpu.CompilerParams(
            collective_id=0, has_side_effects=True, vmem_limit_bytes=32 * 1024 * 1024
        ),
        name="main",
    )(*[pltpu.with_memory_space_constraint(v, pltpu.HBM) for v in operands])
    new_right, basis, gate_grad, hist, grad = pl.pallas_call(
        end_kernel,
        out_shape=tuple(out(shape, dtype) for shape, dtype in kinds),
        in_specs=[vmem] * 5,
        out_specs=(hbm,) * 5,
        scratch_shapes=[DMA((5,))],
        compiler_params=pltpu.CompilerParams(vmem_limit_bytes=8 * 1024 * 1024),
        name="finish",
    )(*results)
    return grad, basis.T, new_right.T, gate_grad, hist.reshape(nbins)


def solution(mesh):
    n = math.isqrt(mesh.shape["dp"] // 2)
    assert 2 * n * n == mesh.shape["dp"]
    placed = (
        P("dp", "tensor"),
        P("tensor", None),
        P("dp", None),
        P("dp", "tensor", None),
        P(),
        P(),
        P(),
        P("dp"),
        P("dp"),
        P("dp"),
    )
    return jax.shard_map(
        functools.partial(per_device, n, mesh.shape["tensor"]),
        mesh=mesh,
        in_specs=placed,
        out_specs=(P("dp", "tensor"), P("tensor", None), P("tensor", None), P(None, "tensor"), P()),
        check_vma=False,
    )
```

```python
import functools
import math

import jax
import jax.numpy as jnp
from jax import lax
from jax.experimental import pallas as pl
from jax.experimental.pallas import tpu as pltpu
from jax.sharding import PartitionSpec as P

MESH = pl.DeviceIdType.MESH
F32 = jnp.float32
BF16 = jnp.bfloat16
HIGHEST = lax.Precision.HIGHEST
NN = (((1,), (0,)), ((), ()))
NT = (((1,), (1,)), ((), ()))


def split(x):
    high = x.astype(BF16)
    low = (x - high.astype(F32)).astype(BF16)
    return jnp.concatenate([high, low], axis=0)


def fold(x):
    half = x.shape[0] // 2
    return x[:half] + x[half:]


def eliminate(ref, begin, end):
    groups, _, width = ref.shape
    sub = lax.broadcasted_iota(jnp.int32, (8, width), 0)

    def wide(x, j):
        return jnp.broadcast_to(x[:, j : j + 1], (8, width))

    def block(k, carry):
        own = ref[k]
        rows = [ref[g] for g in range(groups)]
        for r in range(0, 8, 2):
            first, second = wide(own, r), wide(own, r + 1)
            aa = first[r : r + 1]
            ab = first[r + 1 : r + 2]
            bb = second[r + 1 : r + 2]
            inverse = 1.0 / (aa * bb - ab * ab)
            top = own[r : r + 1]
            low = own[r + 1 : r + 2]
            one = jnp.broadcast_to((bb * inverse) * top - (ab * inverse) * low, (8, width))
            two = jnp.broadcast_to((aa * inverse) * low - (ab * inverse) * top, (8, width))
            if r < 6:
                own = own - jnp.where(sub > r + 1, first * one + second * two, 0.0)
            for g in range(groups):
                change = wide(rows[g], r) * one + wide(rows[g], r + 1) * two
                rows[g] = rows[g] - jnp.where(g > k, change, 0.0)
        for g in range(groups):
            ref[g] = pltpu.roll(jnp.where(g == k, own, rows[g]), width - 8, 1)
        return carry

    lax.fori_loop(begin, end, block, 0)


def unscaled_to_inverse(rows, rank):
    out = []
    width = rows[0].shape[1]
    lane = lax.broadcasted_iota(jnp.int32, (8, width), 1)
    sub = lax.broadcasted_iota(jnp.int32, (8, width), 0)
    odd = lax.rem(sub, 2) == 1
    for g, x in enumerate(rows):
        row = sub + (8 * g + rank)
        before = jnp.concatenate([x[7:], x[:7]], axis=0)
        over = jnp.sum(jnp.where(lane == row - 1, before, 0.0), axis=1, keepdims=True)
        off = jnp.sum(jnp.where(lane == row - 1, x, 0.0), axis=1, keepdims=True)
        x = jnp.where(odd, x - (off / jnp.where(odd[:, :1], over, 1.0)) * before, x)
        diag = jnp.sum(jnp.where(lane == row, x, 0.0), axis=1, keepdims=True)
        out.append(x / jnp.sqrt(diag))
    return jnp.concatenate(out, axis=0)


def far_first(i, n):
    return n // 2 + ((i + 1) // 2) * (1 - 2 * (i % 2))


def each(count, step):
    def body(i, carry):
        step(i)
        return carry

    lax.fori_loop(0, count, body, 0)


def wrap(value, n):
    return jnp.where(value >= n, value - n, value)


A1, TG, A2, A3, G1, G2, G3, GRAM, XX, C4, C5, PAIR = range(12)


def main_kernel(
    n, nx, workers, hist_scale,
    tb_hbm, sw_hbm, head_hbm, weight_hbm, cot_hbm, err_hbm, right_hbm, gate_hbm, loss_hbm, bins_hbm,
    right_o, basis_o, gate_o, hist_o, grad_o,
    tb_ref, sw_ref, head, weight, cot, right, gate, loss, bins, load_sem,
    both_g, head_t, rstack, scale, left_v, stack_v, own_s, sib_s,
    l_src, l_in, l_mid, l_all,
    g_src, g_in, g_mid, g_all,
    s_src, s_in, s_x, s_xin, s_mid, s_all,
    t_src, t_in, gram, chol,
    ssem, rsem,
):
    rank = right.shape[0]
    tokens, feats = head.shape
    width = cot.shape[1]
    latents, per = loss.shape
    nbins = gate.shape[0]
    share = width // nx
    half = rank // 2
    piece = half // n
    pairs = 2 * n
    parts = nx // 2
    FIRST = PAIR + parts

    wanted = [(right_hbm, right), (tb_hbm, tb_ref), (sw_hbm, sw_ref), (gate_hbm, gate)]
    for i in range(feats // 128):
        rows = pl.ds(i * 128, 128)
        wanted.append((err_hbm.at[0, rows], both_g.at[rows]))
    for l in range(latents):
        rows = pl.ds(l * per, per)
        wanted.append((cot_hbm.at[rows], cot.at[rows]))
    wanted += [(head_hbm, head), (loss_hbm, loss), (bins_hbm, bins), (weight_hbm, weight)]
    loads = []
    for k, (src, dst) in enumerate(wanted):
        loads.append(pltpu.make_async_copy(src, dst, load_sem.at[k]))
        loads[-1].start()
    e_load = 4
    c_load = e_load + feats // 128
    h_load = c_load + latents

    index = lax.axis_index("dp")
    x = lax.axis_index("tensor")
    c = lax.rem(index, 2)
    y = lax.rem(index // 2, n)
    z = index // (2 * n)

    def at_z(j, core):
        return ((j * n + y) * 2 + core, x)

    def at_y(j, core):
        return ((z * n + j) * 2 + core, x)

    a = jnp.where(c == 0, z, y)
    b = jnp.where(c == 0, y, z)

    a_step = jnp.where(c == 0, 2 * n, 2)
    a_base = jnp.where(c == 0, 2 * y, 2 * n * z)
    b_step = jnp.where(c == 0, 2, 2 * n)
    b_base = jnp.where(c == 0, 2 * n * z, 2 * y) + c

    def at_a(j, core):
        return (j * a_step + a_base + core, x)

    def at_b(j):
        return (j * b_step + b_base, x)

    sibling = (index + 1 - 2 * c, x)

    barrier = pltpu.get_barrier_semaphore()

    def greet(device):
        pl.semaphore_signal(barrier, inc=1, device_id=device, device_id_type=MESH)

    @functools.partial(each, n - 1)
    def _(i):
        k = far_first(i, n)
        jz = wrap(z + k, n)
        jy = wrap(y + k, n)
        for core in (0, 1):
            greet(at_z(jz, core))
            greet(at_y(jy, core))

    greet(sibling)

    @functools.partial(each, nx - 1)
    def _(i):
        greet((index, wrap(x + far_first(i, nx), nx)))

    def remote(src, dst, phase, device):
        return pltpu.make_async_remote_copy(
            src_ref=src, dst_ref=dst, send_sem=ssem.at[phase], recv_sem=rsem.at[phase],
            device_id=device, device_id_type=MESH,
        )

    def scatter_send(src, dst, phase):
        @functools.partial(each, n - 1)
        def _(i):
            k = far_first(i, n)
            jz = wrap(z + k, n)
            jy = wrap(y + k, n)
            remote(src.at[jz], dst.at[z * 2 + c], phase, at_z(jz, 0)).start()
            remote(src.at[n + jy], dst.at[y * 2 + c], phase, at_y(jy, 1)).start()

        @pl.when(c == 1)
        def _():
            remote(src.at[z], dst.at[z * 2 + 1], phase, sibling).start()

        @pl.when(c == 0)
        def _():
            remote(src.at[n + y], dst.at[y * 2], phase, sibling).start()

        dst[a * 2 + c] = src[c * n + a]

    def wait_many(ref, count, phase, recv=True):
        part = ref.at[pl.ds(0, count)]
        copy = remote(part, part, phase, sibling)
        if recv:
            copy.wait_recv()
        else:
            copy.wait_send()

    def sum_slots(ref, count):
        out = ref[0]
        for k in range(1, count):
            out = out + ref[k]
        return out

    def ring_send(ref, phase):
        @functools.partial(each, n - 1)
        def _(i):
            remote(ref.at[b], ref.at[b], phase, at_b(wrap(b + far_first(i, n), n))).start()

    def gather_send(ref, phase):
        mine = c * n + a

        @functools.partial(each, n - 1)
        def _(i):
            j = wrap(a + far_first(i, n), n)
            for core in (0, 1):
                remote(ref.at[mine], ref.at[mine], phase, at_a(j, core)).start()

        remote(ref.at[mine], ref.at[mine], phase, sibling).start()

    loads[0].wait()
    rstack[...] = split(right[...])

    @functools.partial(each, feats // 128)
    def _(i):
        rows = pl.ds(pl.multiple_of(i * 128, 128), 128)
        pltpu.make_async_copy(err_hbm.at[0, rows], both_g.at[rows], load_sem.at[e_load + i]).wait()
        term = lax.dot_general(both_g[rows, :], rstack[...], NT, preferred_element_type=F32)
        left_v[:, rows] = fold(term.T)

    for k in (1, 2, 3):
        loads[k].wait()
    bin_of = lax.broadcasted_iota(jnp.int32, (8, nbins), 1)
    row_of = lax.broadcasted_iota(jnp.int32, (8, nbins), 0)
    onehot = jnp.zeros((8, nbins), F32)
    weights = []
    for l in range(latents):
        tb = tb_ref[l]
        weights.append(sw_ref[tb])
        onehot = jnp.where((row_of == l) & (bin_of == tb), 1.0, onehot)
    gates = lax.dot_general(onehot.astype(BF16), gate[...], NN, preferred_element_type=F32)
    row8 = lax.broadcasted_iota(jnp.int32, (8, width), 0)
    lat8 = jnp.zeros((8, width), F32)
    for l in range(latents):
        lat8 = jnp.where(row8 == l, weights[l], lat8)
    scale[...] = gates * lat8
    loads[h_load].wait()

    @functools.partial(each, latents)
    def _(l):
        rows = pl.ds(pl.multiple_of(l * per, per), per)
        pltpu.make_async_copy(cot_hbm.at[rows], cot.at[rows], load_sem.at[c_load + l]).wait()
        part = (cot[rows, :].astype(F32) * scale[pl.ds(l, 1), :]).astype(BF16)
        both_g[pl.ds(pl.multiple_of(feats + l * per, per), per), :] = part
        mixed = fold(lax.dot_general(part, rstack[...], NT, preferred_element_type=F32).T)
        left_v[...] += fold(lax.dot_general(split(mixed), head[rows, :], NN, preferred_element_type=F32))

    left = left_v[...]
    for k in range(pairs):
        l_src[k] = left[k * piece : (k + 1) * piece]

    pl.semaphore_wait(barrier, 4 * (n - 1) + 1 + (nx - 1))
    scatter_send(l_src, l_in, A1)

    loads[h_load + 3].wait()
    row_s = lax.broadcasted_iota(jnp.int32, (8, share), 0)

    @functools.partial(each, nx)
    def _(t):
        cols = pl.ds(pl.multiple_of(t * share, 128), share)
        out = jnp.zeros((8, share), F32)
        for l in range(latents):
            rows = pl.ds(l * per, per)
            branch = lax.dot_general(head[rows, :], weight[:, cols], NN, preferred_element_type=F32)
            row = jnp.sum(branch * cot[rows, cols].astype(F32), axis=0, keepdims=True) * weights[l]
            out = jnp.where(row_s == l, row, out)
        t_src[t] = out

    t_in[x] = t_src[x]

    @functools.partial(each, nx - 1)
    def _(i):
        j = wrap(x + far_first(i, nx), nx)
        remote(t_src.at[j], t_in.at[x], TG, (index, j)).start()

    wait_many(l_in, pairs - 1, A1)
    l_mid[b] = sum_slots(l_in, pairs)
    ring_send(l_mid, A2)

    head_t[...] = head[...].T
    loads[h_load + 1].wait()
    loads[h_load + 2].wait()
    bin_row = lax.broadcasted_iota(jnp.int32, (nbins, per), 0)
    hist = jnp.zeros((nbins, per), F32)
    for l in range(latents):
        hist = hist + jnp.where(bin_row == bins[l : l + 1, :], weights[l] * loss[l : l + 1, :], 0.0)
    wait_many(t_in, nx - 1, TG)
    lat_sum = sum_slots(t_in, nx)
    bin_s = lax.broadcasted_iota(jnp.int32, (nbins, share), 0)
    spread = jnp.zeros((nbins, share), F32)
    for l in range(latents):
        spread = spread + jnp.where(bin_s == tb_ref[l], lat_sum[l : l + 1, :], 0.0)
    for k in range(pairs):
        g_src[k, :, share:] = hist[k * piece : (k + 1) * piece]
        g_src[k, :, :share] = spread[k * piece : (k + 1) * piece]
    scatter_send(g_src, g_in, G1)

    wait_many(l_mid, n - 1, A2)
    l_all[c * n + a] = sum_slots(l_mid, n) * (1.0 / workers)
    gather_send(l_all, A3)

    @functools.partial(each, latents)
    def _(l):
        grad_o[pl.ds(pl.multiple_of(l * per, per), per), :] = lax.dot_general(
            both_g[pl.ds(pl.multiple_of(feats + l * per, per), per), :], weight[...], NT, preferred_element_type=F32
        ).astype(BF16)

    wait_many(g_in, pairs - 1, G1)
    g_mid[b] = sum_slots(g_in, pairs)
    ring_send(g_mid, G2)

    wait_many(l_all, pairs - 1, A3)
    left = jnp.concatenate([l_all[k] for k in range(pairs)], axis=0)
    lstack = split(left)
    mixed = fold(lax.dot_general(lstack, head_t[...], NN, preferred_element_type=F32))
    stack = jnp.concatenate([lstack, split(mixed)], axis=1)

    stack_v[...] = stack

    def target(i):
        return wrap(x + far_first(i, nx), nx)

    def part_start(i):
        for q in (0, 1):
            cols = pl.ds(pl.multiple_of(target(2 * i + q) * share, 128), share)
            term = fold(lax.dot_general(stack_v[...], both_g[:, cols], NN, preferred_element_type=F32))
            own_s[i, 0, q] = term[:half]
            own_s[i, 1, q] = term[half:]
        remote(own_s.at[i, 1 - c], sib_s.at[i], PAIR + i, sibling).start()

    def part_scatter(i):
        remote(sib_s.at[i], sib_s.at[i], PAIR + i, sibling).wait_recv()
        total = own_s[i, c] + sib_s[i]
        for q in (0, 1):
            for k in range(n):
                s_src[i, k, q] = total[q, k * piece : (k + 1) * piece]
        s_in[i, a] = s_src[i, a]

        @functools.partial(each, n - 1)
        def _(k):
            j = wrap(a + far_first(k, n), n)
            remote(s_src.at[i, j], s_in.at[i, a], FIRST + i, at_a(j, c)).start()

    def part_sum(i):
        wait_many(s_in.at[i], n - 1, FIRST + i)
        total = s_in[i, 0]
        for k in range(1, n):
            total = total + s_in[i, k]
        return total

    @functools.partial(each, parts + 1)
    def _(i):
        @pl.when(i < parts)
        def _():
            part_start(i)

        @pl.when(i >= 1)
        def _():
            part_scatter(i - 1)

    padded = jnp.concatenate([left, jnp.zeros((128 - rank, share), F32)], axis=0)
    gram[x] = lax.dot_general(left, padded, NT, precision=HIGHEST, preferred_element_type=F32)

    @functools.partial(each, nx - 1)
    def _(i):
        remote(gram.at[x], gram.at[x], GRAM, (index, target(i))).start()

    wait_many(g_mid, n - 1, G2)
    g_all[c * n + a] = sum_slots(g_mid, n)
    gather_send(g_all, G3)

    def cross(i, total):
        s_x[i] = total
        remote(s_x.at[i], s_xin.at[x], XX, (index, target(i))).start()

    @functools.partial(each, parts - 1)
    def _(i):
        total = part_sum(i)
        cross(2 * i, total[0])
        cross(2 * i + 1, total[1])

    groups = rank // 8
    wait_many(gram, nx - 1, GRAM)
    whole = sum_slots(gram, nx)
    eye_r = lax.broadcasted_iota(jnp.int32, (rank, 128), 0)
    eye_c = lax.broadcasted_iota(jnp.int32, (rank, 128), 1)
    whole = jnp.where(eye_c == eye_r + rank, 1.0, whole)
    for g in range(groups):
        chol[g] = whole[8 * g : 8 * g + 8]
    eliminate(chol, 0, groups // 4)
    total = part_sum(parts - 1)
    cross(nx - 2, total[0])
    s_xin[x] = total[1]

    wait_many(s_xin, nx - 1, XX)
    s_mid[b] = sum_slots(s_xin, nx)
    ring_send(s_mid, C4)

    eliminate(chol, groups // 4, 5 * groups // 8)

    wait_many(s_mid, n - 1, C4)
    s_all[c * n + a] = sum_slots(s_mid, n)
    gather_send(s_all, C5)
    eliminate(chol, 5 * groups // 8, groups)
    inverse = unscaled_to_inverse([chol[g] for g in range(groups)], rank)[:, :rank]
    basis_o[...] = lax.dot_general(inverse, left, NN, precision=HIGHEST, preferred_element_type=F32)
    wait_many(g_all, pairs - 1, G3)
    gates = jnp.concatenate([g_all[k] for k in range(pairs)], axis=0)
    gate_o[...] = gates[:, :share]
    hist_o[...] = jnp.sum(gates[:, share:], axis=1, keepdims=True).T * hist_scale
    wait_many(s_all, pairs - 1, C5)
    s_whole = jnp.concatenate([s_all[k] for k in range(pairs)], axis=0)
    right_o[...] = lax.dot_general(
        inverse, s_whole, NN, precision=HIGHEST, preferred_element_type=F32
    ) * (1.0 / workers)

    wait_many(l_src, pairs - 1, A1, False)
    wait_many(t_src, nx - 1, TG, False)
    wait_many(l_mid, n - 1, A2, False)
    wait_many(l_all, pairs - 1, A3, False)
    wait_many(g_src, pairs - 1, G1, False)

    @functools.partial(each, parts)
    def _(i):
        remote(sib_s.at[i], sib_s.at[i], PAIR + i, sibling).wait_send()
        wait_many(s_src.at[i], n - 1, FIRST + i, False)

    wait_many(gram, nx - 1, GRAM, False)
    wait_many(g_mid, n - 1, G2, False)
    wait_many(s_x, nx - 1, XX, False)
    wait_many(s_mid, n - 1, C4, False)
    wait_many(g_all, pairs - 1, G3, False)
    wait_many(s_all, pairs - 1, C5, False)


def end_kernel(*refs):
    count = len(refs) // 2
    sem = refs[-1]
    copies = [pltpu.make_async_copy(refs[k], refs[count + k], sem.at[k]) for k in range(count)]
    for copy in copies:
        copy.start()
    for copy in copies:
        copy.wait()


def per_device(n, nx, head, weight, cot, err, right, gate, sample, tbins, loss, lbins):
    workers = 2 * n * n
    rank = right.shape[1]
    tokens, feats = head.shape
    width = cot.shape[1]
    latents = tbins.shape[0]
    per = tokens // latents
    nbins = gate.shape[0]
    share = width // nx
    half = rank // 2
    piece = half // n
    pairs = 2 * n
    gwidth = share + per
    parts = nx // 2
    vmem = pl.BlockSpec(memory_space=pltpu.VMEM)
    hbm = pl.BlockSpec(memory_space=pltpu.HBM)
    V = pltpu.VMEM
    DMA = pltpu.SemaphoreType.DMA
    out = jax.ShapeDtypeStruct
    operands = (
        tbins, sample, head, weight, cot, err, right.T, gate,
        loss.reshape(latents, per), lbins.reshape(latents, per),
    )
    kinds = (
        ((rank, share), F32),
        ((rank, share), F32),
        ((nbins, share), F32),
        ((1, nbins), F32),
        ((tokens, feats), BF16),
    )
    results = pl.pallas_call(
        functools.partial(main_kernel, n, nx, workers, nbins / (tokens * workers)),
        out_shape=tuple(V(shape, dtype) for shape, dtype in kinds),
        in_specs=[hbm] * 10,
        out_specs=(vmem,) * 5,
        scratch_shapes=[
            pltpu.SMEM(tbins.shape, jnp.int32),
            pltpu.SMEM(sample.shape, F32),
            V(head.shape, BF16),
            V(weight.shape, BF16),
            V(cot.shape, BF16),
            V((rank, width), F32),
            V(gate.shape, BF16),
            V((latents, per), F32),
            V((latents, per), jnp.int32),
            DMA((8 + feats // 128 + latents,)),
            V((feats + tokens, width), BF16),
            V((feats, tokens), BF16),
            V((2 * rank, width), BF16),
            V((8, width), F32),
            V((rank, share), F32),
            V((2 * rank, feats + tokens), BF16),
            V((parts, 2, 2, half, share), F32),
            V((parts, 2, half, share), F32),
            V((pairs, piece, share), F32),
            V((pairs, piece, share), F32),
            V((n, piece, share), F32),
            V((pairs, piece, share), F32),
            V((pairs, piece, gwidth), F32),
            V((pairs, piece, gwidth), F32),
            V((n, piece, gwidth), F32),
            V((pairs, piece, gwidth), F32),
            V((parts, n, 2, piece, share), F32),
            V((parts, n, 2, piece, share), F32),
            V((nx, piece, share), F32),
            V((nx, piece, share), F32),
            V((n, piece, share), F32),
            V((pairs, piece, share), F32),
            V((nx, 8, share), F32),
            V((nx, 8, share), F32),
            V((nx, rank, 128), F32),
            V((rank // 8, 8, 128), F32),
            DMA((PAIR + 2 * parts,)),
            DMA((PAIR + 2 * parts,)),
        ],
        compiler_params=pltpu.CompilerParams(
            collective_id=0, has_side_effects=True, vmem_limit_bytes=32 * 1024 * 1024
        ),
        name="main",
    )(*[pltpu.with_memory_space_constraint(v, pltpu.HBM) for v in operands])
    new_right, basis, gate_grad, hist, grad = pl.pallas_call(
        end_kernel,
        out_shape=tuple(out(shape, dtype) for shape, dtype in kinds),
        in_specs=[vmem] * 5,
        out_specs=(hbm,) * 5,
        scratch_shapes=[DMA((5,))],
        compiler_params=pltpu.CompilerParams(vmem_limit_bytes=8 * 1024 * 1024),
        name="finish",
    )(*results)
    return grad, basis.T, new_right.T, gate_grad, hist.reshape(nbins)


def solution(mesh):
    n = math.isqrt(mesh.shape["dp"] // 2)
    assert 2 * n * n == mesh.shape["dp"]
    placed = (
        P("dp", "tensor"),
        P("tensor", None),
        P("dp", None),
        P("dp", "tensor", None),
        P(),
        P(),
        P(),
        P("dp"),
        P("dp"),
        P("dp"),
    )
    return jax.shard_map(
        functools.partial(per_device, n, mesh.shape["tensor"]),
        mesh=mesh,
        in_specs=placed,
        out_specs=(P("dp", "tensor"), P("tensor", None), P("tensor", None), P(None, "tensor"), P()),
        check_vma=False,
    )
```

```python
import functools
import math

import jax
import jax.numpy as jnp
from jax import lax
from jax.experimental import pallas as pl
from jax.experimental.pallas import tpu as pltpu
from jax.sharding import PartitionSpec as P

MESH = pl.DeviceIdType.MESH
F32 = jnp.float32
BF16 = jnp.bfloat16
HIGHEST = lax.Precision.HIGHEST
NN = (((1,), (0,)), ((), ()))
NT = (((1,), (1,)), ((), ()))


def split(x):
    high = x.astype(BF16)
    low = (x - high.astype(F32)).astype(BF16)
    return jnp.concatenate([high, low], axis=0)


def fold(x):
    half = x.shape[0] // 2
    return x[:half] + x[half:]


def eliminate(ref, begin, end):
    groups, _, width = ref.shape
    sub = lax.broadcasted_iota(jnp.int32, (8, width), 0)

    def wide(x, j):
        return jnp.broadcast_to(x[:, j : j + 1], (8, width))

    def block(k, carry):
        own = ref[k]
        rows = [ref[g] for g in range(groups)]
        for r in range(0, 8, 2):
            first, second = wide(own, r), wide(own, r + 1)
            aa = first[r : r + 1]
            ab = first[r + 1 : r + 2]
            bb = second[r + 1 : r + 2]
            inverse = 1.0 / (aa * bb - ab * ab)
            top = own[r : r + 1]
            low = own[r + 1 : r + 2]
            one = jnp.broadcast_to((bb * inverse) * top - (ab * inverse) * low, (8, width))
            two = jnp.broadcast_to((aa * inverse) * low - (ab * inverse) * top, (8, width))
            if r < 6:
                own = own - jnp.where(sub > r + 1, first * one + second * two, 0.0)
            for g in range(groups):
                change = wide(rows[g], r) * one + wide(rows[g], r + 1) * two
                rows[g] = rows[g] - jnp.where(g > k, change, 0.0)
        for g in range(groups):
            ref[g] = pltpu.roll(jnp.where(g == k, own, rows[g]), width - 8, 1)
        return carry

    lax.fori_loop(begin, end, block, 0)


def unscaled_to_inverse(rows, rank):
    out = []
    width = rows[0].shape[1]
    lane = lax.broadcasted_iota(jnp.int32, (8, width), 1)
    sub = lax.broadcasted_iota(jnp.int32, (8, width), 0)
    odd = lax.rem(sub, 2) == 1
    for g, x in enumerate(rows):
        row = sub + (8 * g + rank)
        before = jnp.concatenate([x[7:], x[:7]], axis=0)
        over = jnp.sum(jnp.where(lane == row - 1, before, 0.0), axis=1, keepdims=True)
        off = jnp.sum(jnp.where(lane == row - 1, x, 0.0), axis=1, keepdims=True)
        x = jnp.where(odd, x - (off / jnp.where(odd[:, :1], over, 1.0)) * before, x)
        diag = jnp.sum(jnp.where(lane == row, x, 0.0), axis=1, keepdims=True)
        out.append(x / jnp.sqrt(diag))
    return jnp.concatenate(out, axis=0)


def far_first(i, n):
    return n // 2 + ((i + 1) // 2) * (1 - 2 * (i % 2))


def each(count, step):
    def body(i, carry):
        step(i)
        return carry

    lax.fori_loop(0, count, body, 0)


def wrap(value, n):
    return jnp.where(value >= n, value - n, value)


A1, TG, A2, A3, G1, G2, G3, GRAM, XX, C4, C5, PAIR = range(12)


def main_kernel(
    n, nx, workers, hist_scale,
    tb_hbm, sw_hbm, head_hbm, weight_hbm, cot_hbm, err_hbm, right_hbm, gate_hbm, loss_hbm, bins_hbm,
    right_o, basis_o, gate_o, hist_o, grad_o,
    tb_ref, sw_ref, head, weight, cot, right, gate, loss, bins, load_sem,
    both_g, head_t, rstack, scale, left_v, stack_v, merged, own_s, sib_s,
    l_src, l_in, l_mid, l_all,
    g_src, g_in, g_mid, g_all,
    s_src, s_in, s_x, s_xin, s_mid, s_all,
    t_src, t_in, gram, chol,
    ssem, rsem,
):
    rank = right.shape[0]
    tokens, feats = head.shape
    width = cot.shape[1]
    latents, per = loss.shape
    nbins = gate.shape[0]
    share = width // nx
    half = rank // 2
    piece = half // n
    pairs = 2 * n
    FIRST = PAIR + nx

    index = lax.axis_index("dp")
    x = lax.axis_index("tensor")
    c = lax.rem(index, 2)
    y = lax.rem(index // 2, n)
    z = index // (2 * n)

    def at_z(j, core):
        return ((j * n + y) * 2 + core, x)

    def at_y(j, core):
        return ((z * n + j) * 2 + core, x)

    a = jnp.where(c == 0, z, y)
    b = jnp.where(c == 0, y, z)

    a_step = jnp.where(c == 0, 2 * n, 2)
    a_base = jnp.where(c == 0, 2 * y, 2 * n * z)
    b_step = jnp.where(c == 0, 2, 2 * n)
    b_base = jnp.where(c == 0, 2 * n * z, 2 * y) + c

    def at_a(j, core):
        return (j * a_step + a_base + core, x)

    def at_b(j):
        return (j * b_step + b_base, x)

    sibling = (index + 1 - 2 * c, x)

    barrier = pltpu.get_barrier_semaphore()

    def greet(device):
        pl.semaphore_signal(barrier, inc=1, device_id=device, device_id_type=MESH)

    @functools.partial(each, n - 1)
    def _(i):
        k = far_first(i, n)
        jz = wrap(z + k, n)
        jy = wrap(y + k, n)
        for core in (0, 1):
            greet(at_z(jz, core))
            greet(at_y(jy, core))

    greet(sibling)

    @functools.partial(each, nx - 1)
    def _(i):
        greet((index, wrap(x + far_first(i, nx), nx)))

    wanted = [(right_hbm, right), (tb_hbm, tb_ref), (sw_hbm, sw_ref), (gate_hbm, gate)]
    for i in range(feats // 128):
        rows = pl.ds(i * 128, 128)
        wanted.append((err_hbm.at[0, rows], both_g.at[rows]))
    for l in range(latents):
        rows = pl.ds(l * per, per)
        wanted.append((cot_hbm.at[rows], cot.at[rows]))
    wanted += [(head_hbm, head), (loss_hbm, loss), (bins_hbm, bins), (weight_hbm, weight)]
    loads = []
    for k, (src, dst) in enumerate(wanted):
        loads.append(pltpu.make_async_copy(src, dst, load_sem.at[k]))
        loads[-1].start()
    e_load = 4
    c_load = e_load + feats // 128
    h_load = c_load + latents

    def remote(src, dst, phase, device):
        return pltpu.make_async_remote_copy(
            src_ref=src, dst_ref=dst, send_sem=ssem.at[phase], recv_sem=rsem.at[phase],
            device_id=device, device_id_type=MESH,
        )

    def scatter_send(src, dst, phase):
        @functools.partial(each, n - 1)
        def _(i):
            k = far_first(i, n)
            jz = wrap(z + k, n)
            jy = wrap(y + k, n)
            remote(src.at[jz], dst.at[z * 2 + c], phase, at_z(jz, 0)).start()
            remote(src.at[n + jy], dst.at[y * 2 + c], phase, at_y(jy, 1)).start()

        @pl.when(c == 1)
        def _():
            remote(src.at[z], dst.at[z * 2 + 1], phase, sibling).start()

        @pl.when(c == 0)
        def _():
            remote(src.at[n + y], dst.at[y * 2], phase, sibling).start()

        dst[a * 2 + c] = src[c * n + a]

    def wait_many(ref, count, phase, recv=True):
        part = ref.at[pl.ds(0, count)]
        copy = remote(part, part, phase, sibling)
        if recv:
            copy.wait_recv()
        else:
            copy.wait_send()

    def sum_slots(ref, count):
        out = ref[0]
        for k in range(1, count):
            out = out + ref[k]
        return out

    def ring_send(ref, phase):
        @functools.partial(each, n - 1)
        def _(i):
            remote(ref.at[b], ref.at[b], phase, at_b(wrap(b + far_first(i, n), n))).start()

    def gather_send(ref, phase):
        mine = c * n + a

        @functools.partial(each, n - 1)
        def _(i):
            j = wrap(a + far_first(i, n), n)
            for core in (0, 1):
                remote(ref.at[mine], ref.at[mine], phase, at_a(j, core)).start()

        remote(ref.at[mine], ref.at[mine], phase, sibling).start()

    loads[0].wait()
    rstack[...] = split(right[...])

    @functools.partial(each, feats // 128)
    def _(i):
        rows = pl.ds(pl.multiple_of(i * 128, 128), 128)
        pltpu.make_async_copy(err_hbm.at[0, rows], both_g.at[rows], load_sem.at[e_load + i]).wait()
        term = lax.dot_general(both_g[rows, :], rstack[...], NT, preferred_element_type=F32)
        left_v[:, rows] = fold(term.T)

    for k in (1, 2, 3):
        loads[k].wait()
    bin_of = lax.broadcasted_iota(jnp.int32, (8, nbins), 1)
    row_of = lax.broadcasted_iota(jnp.int32, (8, nbins), 0)
    onehot = jnp.zeros((8, nbins), F32)
    weights = []
    for l in range(latents):
        tb = tb_ref[l]
        weights.append(sw_ref[tb])
        onehot = jnp.where((row_of == l) & (bin_of == tb), 1.0, onehot)
    gates = lax.dot_general(onehot.astype(BF16), gate[...], NN, preferred_element_type=F32)
    row8 = lax.broadcasted_iota(jnp.int32, (8, width), 0)
    lat8 = jnp.zeros((8, width), F32)
    for l in range(latents):
        lat8 = jnp.where(row8 == l, weights[l], lat8)
    scale[...] = gates * lat8
    loads[h_load].wait()

    @functools.partial(each, latents)
    def _(l):
        rows = pl.ds(pl.multiple_of(l * per, per), per)
        pltpu.make_async_copy(cot_hbm.at[rows], cot.at[rows], load_sem.at[c_load + l]).wait()
        part = (cot[rows, :].astype(F32) * scale[pl.ds(l, 1), :]).astype(BF16)
        both_g[pl.ds(pl.multiple_of(feats + l * per, per), per), :] = part
        mixed = fold(lax.dot_general(part, rstack[...], NT, preferred_element_type=F32).T)
        left_v[...] += fold(lax.dot_general(split(mixed), head[rows, :], NN, preferred_element_type=F32))

    left = left_v[...]
    for k in range(pairs):
        l_src[k] = left[k * piece : (k + 1) * piece]

    pl.semaphore_wait(barrier, 4 * (n - 1) + 1 + (nx - 1))
    scatter_send(l_src, l_in, A1)

    loads[h_load + 3].wait()
    row_s = lax.broadcasted_iota(jnp.int32, (8, share), 0)

    @functools.partial(each, nx)
    def _(t):
        cols = pl.ds(pl.multiple_of(t * share, 128), share)
        out = jnp.zeros((8, share), F32)
        for l in range(latents):
            rows = pl.ds(l * per, per)
            branch = lax.dot_general(head[rows, :], weight[:, cols], NN, preferred_element_type=F32)
            row = jnp.sum(branch * cot[rows, cols].astype(F32), axis=0, keepdims=True) * weights[l]
            out = jnp.where(row_s == l, row, out)
        t_src[t] = out

    stack_v[rank:, feats:] = jnp.zeros((rank, feats), BF16)
    t_in[x] = t_src[x]

    @functools.partial(each, nx - 1)
    def _(i):
        j = wrap(x + far_first(i, nx), nx)
        remote(t_src.at[j], t_in.at[x], TG, (index, j)).start()

    wait_many(l_in, pairs - 1, A1)
    l_mid[b] = sum_slots(l_in, pairs)
    ring_send(l_mid, A2)

    head_t[...] = head[...].T

    @functools.partial(each, nx)
    def _(t):
        cols = pl.ds(pl.multiple_of(t * share, 128), share)
        for i in range(feats // 128):
            rows = pl.ds(i * 128, 128)
            whole = lax.dot_general(head_t[rows, :], both_g[feats:, cols], NN, preferred_element_type=F32)
            whole = whole + both_g[rows, cols].astype(F32)
            high = whole.astype(BF16)
            merged[rows, cols] = high
            merged[pl.ds(feats + i * 128, 128), cols] = (whole - high.astype(F32)).astype(BF16)

    loads[h_load + 1].wait()
    loads[h_load + 2].wait()
    bin_row = lax.broadcasted_iota(jnp.int32, (nbins, per), 0)
    hist = jnp.zeros((nbins, per), F32)
    for l in range(latents):
        hist = hist + jnp.where(bin_row == bins[l : l + 1, :], weights[l] * loss[l : l + 1, :], 0.0)
    wait_many(t_in, nx - 1, TG)
    lat_sum = sum_slots(t_in, nx)
    bin_s = lax.broadcasted_iota(jnp.int32, (nbins, share), 0)
    spread = jnp.zeros((nbins, share), F32)
    for l in range(latents):
        spread = spread + jnp.where(bin_s == tb_ref[l], lat_sum[l : l + 1, :], 0.0)
    for k in range(pairs):
        g_src[k, :, share:] = hist[k * piece : (k + 1) * piece]
        g_src[k, :, :share] = spread[k * piece : (k + 1) * piece]
    scatter_send(g_src, g_in, G1)

    wait_many(l_mid, n - 1, A2)
    l_all[c * n + a] = sum_slots(l_mid, n) * (1.0 / workers)
    gather_send(l_all, A3)

    @functools.partial(each, latents)
    def _(l):
        grad_o[pl.ds(pl.multiple_of(l * per, per), per), :] = lax.dot_general(
            both_g[pl.ds(pl.multiple_of(feats + l * per, per), per), :], weight[...], NT, preferred_element_type=F32
        ).astype(BF16)

    wait_many(g_in, pairs - 1, G1)
    g_mid[b] = sum_slots(g_in, pairs)
    ring_send(g_mid, G2)

    wait_many(l_all, pairs - 1, A3)
    left = jnp.concatenate([l_all[k] for k in range(pairs)], axis=0)
    high = left.astype(BF16)
    low = (left - high.astype(F32)).astype(BF16)
    stack_v[:rank, :feats] = high
    stack_v[:rank, feats:] = high
    stack_v[rank:, :feats] = low

    def target(i):
        return wrap(x + far_first(i, nx), nx)

    def part_start(i):
        cols = pl.ds(pl.multiple_of(target(i) * share, 128), share)
        term = fold(lax.dot_general(stack_v[...], merged[:, cols], NN, preferred_element_type=F32))
        own_s[i, 0] = term[:half]
        own_s[i, 1] = term[half:]
        remote(own_s.at[i, 1 - c], sib_s.at[i], PAIR + i, sibling).start()

    def part_scatter(i):
        remote(sib_s.at[i], sib_s.at[i], PAIR + i, sibling).wait_recv()
        total = own_s[i, c] + sib_s[i]
        for k in range(n):
            s_src[i, k] = total[k * piece : (k + 1) * piece]
        s_in[i, a] = s_src[i, a]

        @functools.partial(each, n - 1)
        def _(k):
            j = wrap(a + far_first(k, n), n)
            remote(s_src.at[i, j], s_in.at[i, a], FIRST + i, at_a(j, c)).start()

    def part_sum(i):
        wait_many(s_in.at[i], n - 1, FIRST + i)
        total = s_in[i, 0]
        for k in range(1, n):
            total = total + s_in[i, k]
        return total

    lead = min(nx, 2)

    @functools.partial(each, nx + lead)
    def _(i):
        @pl.when(i < nx)
        def _():
            part_start(i)

        @pl.when(i >= lead)
        def _():
            part_scatter(i - lead)

    padded = jnp.concatenate([left, jnp.zeros((128 - rank, share), F32)], axis=0)
    gram[x] = lax.dot_general(left, padded, NT, precision=HIGHEST, preferred_element_type=F32)

    @functools.partial(each, nx - 1)
    def _(i):
        remote(gram.at[x], gram.at[x], GRAM, (index, target(i))).start()

    wait_many(g_mid, n - 1, G2)
    g_all[c * n + a] = sum_slots(g_mid, n)
    gather_send(g_all, G3)

    @functools.partial(each, nx - 1)
    def _(i):
        s_x[i] = part_sum(i)
        remote(s_x.at[i], s_xin.at[x], XX, (index, target(i))).start()

    groups = rank // 8
    wait_many(gram, nx - 1, GRAM)
    whole = sum_slots(gram, nx)
    eye_r = lax.broadcasted_iota(jnp.int32, (rank, 128), 0)
    eye_c = lax.broadcasted_iota(jnp.int32, (rank, 128), 1)
    whole = jnp.where(eye_c == eye_r + rank, 1.0, whole)
    for g in range(groups):
        chol[g] = whole[8 * g : 8 * g + 8]
    eliminate(chol, 0, groups // 4)
    s_xin[x] = part_sum(nx - 1)

    wait_many(s_xin, nx - 1, XX)
    s_mid[b] = sum_slots(s_xin, nx)
    ring_send(s_mid, C4)

    eliminate(chol, groups // 4, 5 * groups // 8)

    wait_many(s_mid, n - 1, C4)
    s_all[c * n + a] = sum_slots(s_mid, n)
    gather_send(s_all, C5)
    eliminate(chol, 5 * groups // 8, groups)
    inverse = unscaled_to_inverse([chol[g] for g in range(groups)], rank)[:, :rank]
    basis_o[...] = lax.dot_general(inverse, left, NN, precision=HIGHEST, preferred_element_type=F32)
    wait_many(g_all, pairs - 1, G3)
    gates = jnp.concatenate([g_all[k] for k in range(pairs)], axis=0)
    gate_o[...] = gates[:, :share]
    hist_o[...] = jnp.sum(gates[:, share:], axis=1, keepdims=True).T * hist_scale
    inv_high = inverse.astype(BF16)
    inv_low = (inverse - inv_high.astype(F32)).astype(BF16)
    inv_stack = jnp.concatenate([inv_high, inv_high, inv_low], axis=1)

    wait_many(l_src, pairs - 1, A1, False)
    wait_many(t_src, nx - 1, TG, False)
    wait_many(l_mid, n - 1, A2, False)
    wait_many(l_all, pairs - 1, A3, False)
    wait_many(g_src, pairs - 1, G1, False)

    @functools.partial(each, nx)
    def _(i):
        remote(sib_s.at[i], sib_s.at[i], PAIR + i, sibling).wait_send()
        wait_many(s_src.at[i], n - 1, FIRST + i, False)

    wait_many(gram, nx - 1, GRAM, False)
    wait_many(g_mid, n - 1, G2, False)
    wait_many(s_x, nx - 1, XX, False)
    wait_many(s_mid, n - 1, C4, False)
    wait_many(g_all, pairs - 1, G3, False)

    wait_many(s_all, pairs - 1, C5)
    s_whole = jnp.concatenate([s_all[k] for k in range(pairs)], axis=0)
    s_high = s_whole.astype(BF16)
    s_low = (s_whole - s_high.astype(F32)).astype(BF16)
    right_o[...] = lax.dot_general(
        inv_stack, jnp.concatenate([s_high, s_low, s_high], axis=0), NN, preferred_element_type=F32
    ) * (1.0 / workers)
    wait_many(s_all, pairs - 1, C5, False)


def end_kernel(*refs):
    count = len(refs) // 2
    sem = refs[-1]
    copies = [pltpu.make_async_copy(refs[k], refs[count + k], sem.at[k]) for k in range(count)]
    for copy in copies:
        copy.start()
    for copy in copies:
        copy.wait()


def per_device(n, nx, head, weight, cot, err, right, gate, sample, tbins, loss, lbins):
    workers = 2 * n * n
    rank = right.shape[1]
    tokens, feats = head.shape
    width = cot.shape[1]
    latents = tbins.shape[0]
    per = tokens // latents
    nbins = gate.shape[0]
    share = width // nx
    half = rank // 2
    piece = half // n
    pairs = 2 * n
    gwidth = share + per
    vmem = pl.BlockSpec(memory_space=pltpu.VMEM)
    hbm = pl.BlockSpec(memory_space=pltpu.HBM)
    V = pltpu.VMEM
    DMA = pltpu.SemaphoreType.DMA
    out = jax.ShapeDtypeStruct
    operands = (
        tbins, sample, head, weight, cot, err, right.T, gate,
        loss.reshape(latents, per), lbins.reshape(latents, per),
    )
    kinds = (
        ((rank, share), F32),
        ((rank, share), F32),
        ((nbins, share), F32),
        ((1, nbins), F32),
        ((tokens, feats), BF16),
    )
    results = pl.pallas_call(
        functools.partial(main_kernel, n, nx, workers, nbins / (tokens * workers)),
        out_shape=tuple(V(shape, dtype) for shape, dtype in kinds),
        in_specs=[hbm] * 10,
        out_specs=(vmem,) * 5,
        scratch_shapes=[
            pltpu.SMEM(tbins.shape, jnp.int32),
            pltpu.SMEM(sample.shape, F32),
            V(head.shape, BF16),
            V(weight.shape, BF16),
            V(cot.shape, BF16),
            V((rank, width), F32),
            V(gate.shape, BF16),
            V((latents, per), F32),
            V((latents, per), jnp.int32),
            DMA((8 + feats // 128 + latents,)),
            V((feats + tokens, width), BF16),
            V((feats, tokens), BF16),
            V((2 * rank, width), BF16),
            V((8, width), F32),
            V((rank, share), F32),
            V((2 * rank, 2 * feats), BF16),
            V((2 * feats, width), BF16),
            V((nx, 2, half, share), F32),
            V((nx, half, share), F32),
            V((pairs, piece, share), F32),
            V((pairs, piece, share), F32),
            V((n, piece, share), F32),
            V((pairs, piece, share), F32),
            V((pairs, piece, gwidth), F32),
            V((pairs, piece, gwidth), F32),
            V((n, piece, gwidth), F32),
            V((pairs, piece, gwidth), F32),
            V((nx, n, piece, share), F32),
            V((nx, n, piece, share), F32),
            V((nx, piece, share), F32),
            V((nx, piece, share), F32),
            V((n, piece, share), F32),
            V((pairs, piece, share), F32),
            V((nx, 8, share), F32),
            V((nx, 8, share), F32),
            V((nx, rank, 128), F32),
            V((rank // 8, 8, 128), F32),
            DMA((PAIR + 2 * nx,)),
            DMA((PAIR + 2 * nx,)),
        ],
        compiler_params=pltpu.CompilerParams(
            collective_id=0, has_side_effects=True, vmem_limit_bytes=32 * 1024 * 1024
        ),
        name="main",
    )(*[pltpu.with_memory_space_constraint(v, pltpu.HBM) for v in operands])
    new_right, basis, gate_grad, hist, grad = pl.pallas_call(
        end_kernel,
        out_shape=tuple(out(shape, dtype) for shape, dtype in kinds),
        in_specs=[vmem] * 5,
        out_specs=(hbm,) * 5,
        scratch_shapes=[DMA((5,))],
        compiler_params=pltpu.CompilerParams(vmem_limit_bytes=8 * 1024 * 1024),
        name="finish",
    )(*results)
    return grad, basis.T, new_right.T, gate_grad, hist.reshape(nbins)


def solution(mesh):
    n = math.isqrt(mesh.shape["dp"] // 2)
    assert 2 * n * n == mesh.shape["dp"]
    placed = (
        P("dp", "tensor"),
        P("tensor", None),
        P("dp", None),
        P("dp", "tensor", None),
        P(),
        P(),
        P(),
        P("dp"),
        P("dp"),
        P("dp"),
    )
    return jax.shard_map(
        functools.partial(per_device, n, mesh.shape["tensor"]),
        mesh=mesh,
        in_specs=placed,
        out_specs=(P("dp", "tensor"), P("tensor", None), P("tensor", None), P(None, "tensor"), P()),
        check_vma=False,
    )
```

```python
import functools
import math

import jax
import jax.numpy as jnp
from jax import lax
from jax.experimental import pallas as pl
from jax.experimental.pallas import tpu as pltpu
from jax.sharding import PartitionSpec as P

MESH = pl.DeviceIdType.MESH
F32 = jnp.float32
BF16 = jnp.bfloat16
HIGHEST = lax.Precision.HIGHEST
NN = (((1,), (0,)), ((), ()))
NT = (((1,), (1,)), ((), ()))


def split(x):
    high = x.astype(BF16)
    low = (x - high.astype(F32)).astype(BF16)
    return jnp.concatenate([high, low], axis=0)


def fold(x):
    half = x.shape[0] // 2
    return x[:half] + x[half:]


def eliminate(ref, begin, end):
    groups, _, width = ref.shape
    sub = lax.broadcasted_iota(jnp.int32, (8, width), 0)

    def wide(x, j):
        return jnp.broadcast_to(x[:, j : j + 1], (8, width))

    def block(k, carry):
        own = ref[k]
        rows = [ref[g] for g in range(groups)]
        for r in range(0, 8, 2):
            first, second = wide(own, r), wide(own, r + 1)
            aa = first[r : r + 1]
            ab = first[r + 1 : r + 2]
            bb = second[r + 1 : r + 2]
            inverse = 1.0 / (aa * bb - ab * ab)
            top = own[r : r + 1]
            low = own[r + 1 : r + 2]
            one = jnp.broadcast_to((bb * inverse) * top - (ab * inverse) * low, (8, width))
            two = jnp.broadcast_to((aa * inverse) * low - (ab * inverse) * top, (8, width))
            if r < 6:
                own = own - jnp.where(sub > r + 1, first * one + second * two, 0.0)
            for g in range(groups):
                change = wide(rows[g], r) * one + wide(rows[g], r + 1) * two
                rows[g] = rows[g] - jnp.where(g > k, change, 0.0)
        for g in range(groups):
            ref[g] = pltpu.roll(jnp.where(g == k, own, rows[g]), width - 8, 1)
        return carry

    lax.fori_loop(begin, end, block, 0)


def unscaled_to_inverse(rows, rank):
    out = []
    width = rows[0].shape[1]
    lane = lax.broadcasted_iota(jnp.int32, (8, width), 1)
    sub = lax.broadcasted_iota(jnp.int32, (8, width), 0)
    odd = lax.rem(sub, 2) == 1
    for g, x in enumerate(rows):
        row = sub + (8 * g + rank)
        before = jnp.concatenate([x[7:], x[:7]], axis=0)
        over = jnp.sum(jnp.where(lane == row - 1, before, 0.0), axis=1, keepdims=True)
        off = jnp.sum(jnp.where(lane == row - 1, x, 0.0), axis=1, keepdims=True)
        x = jnp.where(odd, x - (off / jnp.where(odd[:, :1], over, 1.0)) * before, x)
        diag = jnp.sum(jnp.where(lane == row, x, 0.0), axis=1, keepdims=True)
        out.append(x / jnp.sqrt(diag))
    return jnp.concatenate(out, axis=0)


def far_first(i, n):
    return n // 2 + ((i + 1) // 2) * (1 - 2 * (i % 2))


def each(count, step):
    def body(i, carry):
        step(i)
        return carry

    lax.fori_loop(0, count, body, 0)


def wrap(value, n):
    return jnp.where(value >= n, value - n, value)


A1, TG, A2, A3, G1, G2, G3, GRAM, XX, C5, PAIR = range(11)


def main_kernel(
    n, nx, workers, hist_scale,
    tb_hbm, sw_hbm, head_hbm, weight_hbm, cot_hbm, err_hbm, right_hbm, gate_hbm, loss_hbm, bins_hbm,
    right_o, basis_o, gate_o, hist_o, grad_o,
    tb_ref, sw_ref, head, weight, cot, right, gate, loss, bins, load_sem,
    both_g, head_t, rstack, scale, left_v, stack_v, merged, own_s, sib_s,
    l_src, l_in, l_mid, l_all,
    g_src, g_in, g_mid, g_all,
    s_src, s_in, s_x, s_xin, s_all,
    t_src, t_in, gram, chol,
    ssem, rsem,
):
    rank = right.shape[0]
    tokens, feats = head.shape
    width = cot.shape[1]
    latents, per = loss.shape
    nbins = gate.shape[0]
    share = width // nx
    half = rank // 2
    piece = half // n
    pairs = 2 * n
    FIRST = PAIR + nx

    index = lax.axis_index("dp")
    x = lax.axis_index("tensor")
    c = lax.rem(index, 2)
    y = lax.rem(index // 2, n)
    z = index // (2 * n)

    def at_z(j, core):
        return ((j * n + y) * 2 + core, x)

    def at_y(j, core):
        return ((z * n + j) * 2 + core, x)

    a = jnp.where(c == 0, z, y)
    b = jnp.where(c == 0, y, z)

    a_step = jnp.where(c == 0, 2 * n, 2)
    a_base = jnp.where(c == 0, 2 * y, 2 * n * z)
    b_step = jnp.where(c == 0, 2, 2 * n)
    b_base = jnp.where(c == 0, 2 * n * z, 2 * y) + c

    def at_a(j, core):
        return (j * a_step + a_base + core, x)

    def at_b(j, t=x):
        return (j * b_step + b_base, t)

    sibling = (index + 1 - 2 * c, x)

    barrier = pltpu.get_barrier_semaphore()

    def greet(device):
        pl.semaphore_signal(barrier, inc=1, device_id=device, device_id_type=MESH)

    @functools.partial(each, n - 1)
    def _(i):
        k = far_first(i, n)
        jz = wrap(z + k, n)
        jy = wrap(y + k, n)
        for core in (0, 1):
            greet(at_z(jz, core))
            greet(at_y(jy, core))

    greet(sibling)

    @functools.partial(each, nx - 1)
    def _(i):
        greet((index, wrap(x + far_first(i, nx), nx)))

    wanted = [(right_hbm, right), (tb_hbm, tb_ref), (sw_hbm, sw_ref), (gate_hbm, gate)]
    for i in range(feats // 128):
        rows = pl.ds(i * 128, 128)
        wanted.append((err_hbm.at[0, rows], both_g.at[rows]))
    for l in range(latents):
        rows = pl.ds(l * per, per)
        wanted.append((cot_hbm.at[rows], cot.at[rows]))
    wanted += [(head_hbm, head), (loss_hbm, loss), (bins_hbm, bins), (weight_hbm, weight)]
    loads = []
    for k, (src, dst) in enumerate(wanted):
        loads.append(pltpu.make_async_copy(src, dst, load_sem.at[k]))
        loads[-1].start()
    e_load = 4
    c_load = e_load + feats // 128
    h_load = c_load + latents

    def remote(src, dst, phase, device):
        return pltpu.make_async_remote_copy(
            src_ref=src, dst_ref=dst, send_sem=ssem.at[phase], recv_sem=rsem.at[phase],
            device_id=device, device_id_type=MESH,
        )

    def scatter_send(src, dst, phase):
        @functools.partial(each, n - 1)
        def _(i):
            k = far_first(i, n)
            jz = wrap(z + k, n)
            jy = wrap(y + k, n)
            remote(src.at[jz], dst.at[z * 2 + c], phase, at_z(jz, 0)).start()
            remote(src.at[n + jy], dst.at[y * 2 + c], phase, at_y(jy, 1)).start()

        @pl.when(c == 1)
        def _():
            remote(src.at[z], dst.at[z * 2 + 1], phase, sibling).start()

        @pl.when(c == 0)
        def _():
            remote(src.at[n + y], dst.at[y * 2], phase, sibling).start()

        dst[a * 2 + c] = src[c * n + a]

    def wait_many(ref, count, phase, recv=True):
        part = ref.at[pl.ds(0, count)]
        copy = remote(part, part, phase, sibling)
        if recv:
            copy.wait_recv()
        else:
            copy.wait_send()

    def sum_slots(ref, count):
        out = ref[0]
        for k in range(1, count):
            out = out + ref[k]
        return out

    def ring_send(ref, phase):
        @functools.partial(each, n - 1)
        def _(i):
            remote(ref.at[b], ref.at[b], phase, at_b(wrap(b + far_first(i, n), n))).start()

    def gather_send(ref, phase):
        mine = c * n + a

        @functools.partial(each, n - 1)
        def _(i):
            j = wrap(a + far_first(i, n), n)
            for core in (0, 1):
                remote(ref.at[mine], ref.at[mine], phase, at_a(j, core)).start()

        remote(ref.at[mine], ref.at[mine], phase, sibling).start()

    loads[0].wait()
    rstack[...] = split(right[...])

    @functools.partial(each, feats // 128)
    def _(i):
        rows = pl.ds(pl.multiple_of(i * 128, 128), 128)
        pltpu.make_async_copy(err_hbm.at[0, rows], both_g.at[rows], load_sem.at[e_load + i]).wait()
        term = lax.dot_general(both_g[rows, :], rstack[...], NT, preferred_element_type=F32)
        left_v[:, rows] = fold(term.T)

    for k in (1, 2, 3):
        loads[k].wait()
    bin_of = lax.broadcasted_iota(jnp.int32, (8, nbins), 1)
    row_of = lax.broadcasted_iota(jnp.int32, (8, nbins), 0)
    onehot = jnp.zeros((8, nbins), F32)
    weights = []
    for l in range(latents):
        tb = tb_ref[l]
        weights.append(sw_ref[tb])
        onehot = jnp.where((row_of == l) & (bin_of == tb), 1.0, onehot)
    gates = lax.dot_general(onehot.astype(BF16), gate[...], NN, preferred_element_type=F32)
    row8 = lax.broadcasted_iota(jnp.int32, (8, width), 0)
    lat8 = jnp.zeros((8, width), F32)
    for l in range(latents):
        lat8 = jnp.where(row8 == l, weights[l], lat8)
    scale[...] = gates * lat8
    loads[h_load].wait()

    @functools.partial(each, latents)
    def _(l):
        rows = pl.ds(pl.multiple_of(l * per, per), per)
        pltpu.make_async_copy(cot_hbm.at[rows], cot.at[rows], load_sem.at[c_load + l]).wait()
        part = (cot[rows, :].astype(F32) * scale[pl.ds(l, 1), :]).astype(BF16)
        both_g[pl.ds(pl.multiple_of(feats + l * per, per), per), :] = part
        mixed = fold(lax.dot_general(part, rstack[...], NT, preferred_element_type=F32).T)
        left_v[...] += fold(lax.dot_general(split(mixed), head[rows, :], NN, preferred_element_type=F32))

    left = left_v[...]
    for k in range(pairs):
        l_src[k] = left[k * piece : (k + 1) * piece]

    pl.semaphore_wait(barrier, 4 * (n - 1) + 1 + (nx - 1))
    scatter_send(l_src, l_in, A1)

    loads[h_load + 3].wait()
    row_s = lax.broadcasted_iota(jnp.int32, (8, share), 0)

    @functools.partial(each, nx)
    def _(t):
        cols = pl.ds(pl.multiple_of(t * share, 128), share)
        out = jnp.zeros((8, share), F32)
        for l in range(latents):
            rows = pl.ds(l * per, per)
            branch = lax.dot_general(head[rows, :], weight[:, cols], NN, preferred_element_type=F32)
            row = jnp.sum(branch * cot[rows, cols].astype(F32), axis=0, keepdims=True) * weights[l]
            out = jnp.where(row_s == l, row, out)
        t_src[t] = out

    stack_v[rank:, feats:] = jnp.zeros((rank, feats), BF16)
    t_in[x] = t_src[x]

    @functools.partial(each, nx - 1)
    def _(i):
        j = wrap(x + far_first(i, nx), nx)
        remote(t_src.at[j], t_in.at[x], TG, (index, j)).start()

    wait_many(l_in, pairs - 1, A1)
    l_mid[b] = sum_slots(l_in, pairs)
    ring_send(l_mid, A2)

    head_t[...] = head[...].T

    @functools.partial(each, nx)
    def _(t):
        cols = pl.ds(pl.multiple_of(t * share, 128), share)
        for i in range(feats // 128):
            rows = pl.ds(i * 128, 128)
            whole = lax.dot_general(head_t[rows, :], both_g[feats:, cols], NN, preferred_element_type=F32)
            whole = whole + both_g[rows, cols].astype(F32)
            high = whole.astype(BF16)
            merged[rows, cols] = high
            merged[pl.ds(feats + i * 128, 128), cols] = (whole - high.astype(F32)).astype(BF16)

    loads[h_load + 1].wait()
    loads[h_load + 2].wait()
    bin_row = lax.broadcasted_iota(jnp.int32, (nbins, per), 0)
    hist = jnp.zeros((nbins, per), F32)
    for l in range(latents):
        hist = hist + jnp.where(bin_row == bins[l : l + 1, :], weights[l] * loss[l : l + 1, :], 0.0)
    wait_many(t_in, nx - 1, TG)
    lat_sum = sum_slots(t_in, nx)
    bin_s = lax.broadcasted_iota(jnp.int32, (nbins, share), 0)
    spread = jnp.zeros((nbins, share), F32)
    for l in range(latents):
        spread = spread + jnp.where(bin_s == tb_ref[l], lat_sum[l : l + 1, :], 0.0)
    for k in range(pairs):
        g_src[k, :, share:] = hist[k * piece : (k + 1) * piece]
        g_src[k, :, :share] = spread[k * piece : (k + 1) * piece]
    scatter_send(g_src, g_in, G1)

    wait_many(l_mid, n - 1, A2)
    l_all[c * n + a] = sum_slots(l_mid, n) * (1.0 / workers)
    gather_send(l_all, A3)

    @functools.partial(each, latents)
    def _(l):
        grad_o[pl.ds(pl.multiple_of(l * per, per), per), :] = lax.dot_general(
            both_g[pl.ds(pl.multiple_of(feats + l * per, per), per), :], weight[...], NT, preferred_element_type=F32
        ).astype(BF16)

    wait_many(g_in, pairs - 1, G1)
    g_mid[b] = sum_slots(g_in, pairs)
    ring_send(g_mid, G2)

    wait_many(l_all, pairs - 1, A3)
    left = jnp.concatenate([l_all[k] for k in range(pairs)], axis=0)
    high = left.astype(BF16)
    low = (left - high.astype(F32)).astype(BF16)
    stack_v[:rank, :feats] = high
    stack_v[:rank, feats:] = high
    stack_v[rank:, :feats] = low

    def target(i):
        return wrap(x + far_first(i, nx), nx)

    def part_start(i):
        cols = pl.ds(pl.multiple_of(target(i) * share, 128), share)
        term = fold(lax.dot_general(stack_v[...], merged[:, cols], NN, preferred_element_type=F32))
        own_s[i, 0] = term[:half]
        own_s[i, 1] = term[half:]
        remote(own_s.at[i, 1 - c], sib_s.at[i], PAIR + i, sibling).start()

    def part_scatter(i):
        remote(sib_s.at[i], sib_s.at[i], PAIR + i, sibling).wait_recv()
        total = own_s[i, c] + sib_s[i]
        for k in range(n):
            s_src[i, k] = total[k * piece : (k + 1) * piece]
        s_in[i, a] = s_src[i, a]

        @functools.partial(each, n - 1)
        def _(k):
            j = wrap(a + far_first(k, n), n)
            remote(s_src.at[i, j], s_in.at[i, a], FIRST + i, at_a(j, c)).start()

    def part_sum(i):
        wait_many(s_in.at[i], n - 1, FIRST + i)
        total = s_in[i, 0]
        for k in range(1, n):
            total = total + s_in[i, k]
        return total

    lead = min(nx, 2)

    @functools.partial(each, nx + lead)
    def _(i):
        @pl.when(i < nx)
        def _():
            part_start(i)

        @pl.when(i >= lead)
        def _():
            part_scatter(i - lead)

    padded = jnp.concatenate([left, jnp.zeros((128 - rank, share), F32)], axis=0)
    gram[x] = lax.dot_general(left, padded, NT, precision=HIGHEST, preferred_element_type=F32)

    @functools.partial(each, nx - 1)
    def _(i):
        remote(gram.at[x], gram.at[x], GRAM, (index, target(i))).start()

    wait_many(g_mid, n - 1, G2)
    g_all[c * n + a] = sum_slots(g_mid, n)
    gather_send(g_all, G3)

    @functools.partial(each, nx - 1)
    def _(i):
        s_x[i] = part_sum(i)

        @functools.partial(each, n)
        def _(k):
            j = wrap(b + far_first(k, n), n)
            remote(s_x.at[i], s_xin.at[x * n + b], XX, at_b(j, target(i))).start()

    groups = rank // 8
    wait_many(gram, nx - 1, GRAM)
    whole = sum_slots(gram, nx)
    eye_r = lax.broadcasted_iota(jnp.int32, (rank, 128), 0)
    eye_c = lax.broadcasted_iota(jnp.int32, (rank, 128), 1)
    whole = jnp.where(eye_c == eye_r + rank, 1.0, whole)
    for g in range(groups):
        chol[g] = whole[8 * g : 8 * g + 8]
    eliminate(chol, 0, groups // 4)
    s_x[nx - 1] = part_sum(nx - 1)
    s_xin[x * n + b] = s_x[nx - 1]

    @functools.partial(each, n - 1)
    def _(k):
        j = wrap(b + far_first(k, n), n)
        remote(s_x.at[nx - 1], s_xin.at[x * n + b], XX, at_b(j)).start()

    eliminate(chol, groups // 4, 5 * groups // 8)

    wait_many(s_xin, nx * n - 1, XX)
    s_all[c * n + a] = sum_slots(s_xin, nx * n)
    gather_send(s_all, C5)
    eliminate(chol, 5 * groups // 8, groups)
    inverse = unscaled_to_inverse([chol[g] for g in range(groups)], rank)[:, :rank]
    basis_o[...] = lax.dot_general(inverse, left, NN, precision=HIGHEST, preferred_element_type=F32)
    wait_many(g_all, pairs - 1, G3)
    gates = jnp.concatenate([g_all[k] for k in range(pairs)], axis=0)
    gate_o[...] = gates[:, :share]
    hist_o[...] = jnp.sum(gates[:, share:], axis=1, keepdims=True).T * hist_scale
    inv_high = inverse.astype(BF16)
    inv_low = (inverse - inv_high.astype(F32)).astype(BF16)
    inv_stack = jnp.concatenate([inv_high, inv_high, inv_low], axis=1)

    wait_many(l_src, pairs - 1, A1, False)
    wait_many(t_src, nx - 1, TG, False)
    wait_many(l_mid, n - 1, A2, False)
    wait_many(l_all, pairs - 1, A3, False)
    wait_many(g_src, pairs - 1, G1, False)

    @functools.partial(each, nx)
    def _(i):
        remote(sib_s.at[i], sib_s.at[i], PAIR + i, sibling).wait_send()
        wait_many(s_src.at[i], n - 1, FIRST + i, False)

    wait_many(gram, nx - 1, GRAM, False)
    wait_many(g_mid, n - 1, G2, False)
    wait_many(s_xin, nx * n - 1, XX, False)
    wait_many(g_all, pairs - 1, G3, False)

    wait_many(s_all, pairs - 1, C5)
    s_whole = jnp.concatenate([s_all[k] for k in range(pairs)], axis=0)
    s_high = s_whole.astype(BF16)
    s_low = (s_whole - s_high.astype(F32)).astype(BF16)
    right_o[...] = lax.dot_general(
        inv_stack, jnp.concatenate([s_high, s_low, s_high], axis=0), NN, preferred_element_type=F32
    ) * (1.0 / workers)
    wait_many(s_all, pairs - 1, C5, False)


def end_kernel(*refs):
    count = len(refs) // 2
    sem = refs[-1]
    copies = [pltpu.make_async_copy(refs[k], refs[count + k], sem.at[k]) for k in range(count)]
    for copy in copies:
        copy.start()
    for copy in copies:
        copy.wait()


def per_device(n, nx, head, weight, cot, err, right, gate, sample, tbins, loss, lbins):
    workers = 2 * n * n
    rank = right.shape[1]
    tokens, feats = head.shape
    width = cot.shape[1]
    latents = tbins.shape[0]
    per = tokens // latents
    nbins = gate.shape[0]
    share = width // nx
    half = rank // 2
    piece = half // n
    pairs = 2 * n
    gwidth = share + per
    vmem = pl.BlockSpec(memory_space=pltpu.VMEM)
    hbm = pl.BlockSpec(memory_space=pltpu.HBM)
    V = pltpu.VMEM
    DMA = pltpu.SemaphoreType.DMA
    out = jax.ShapeDtypeStruct
    operands = (
        tbins, sample, head, weight, cot, err, right.T, gate,
        loss.reshape(latents, per), lbins.reshape(latents, per),
    )
    kinds = (
        ((rank, share), F32),
        ((rank, share), F32),
        ((nbins, share), F32),
        ((1, nbins), F32),
        ((tokens, feats), BF16),
    )
    results = pl.pallas_call(
        functools.partial(main_kernel, n, nx, workers, nbins / (tokens * workers)),
        out_shape=tuple(V(shape, dtype) for shape, dtype in kinds),
        in_specs=[hbm] * 10,
        out_specs=(vmem,) * 5,
        scratch_shapes=[
            pltpu.SMEM(tbins.shape, jnp.int32),
            pltpu.SMEM(sample.shape, F32),
            V(head.shape, BF16),
            V(weight.shape, BF16),
            V(cot.shape, BF16),
            V((rank, width), F32),
            V(gate.shape, BF16),
            V((latents, per), F32),
            V((latents, per), jnp.int32),
            DMA((8 + feats // 128 + latents,)),
            V((feats + tokens, width), BF16),
            V((feats, tokens), BF16),
            V((2 * rank, width), BF16),
            V((8, width), F32),
            V((rank, share), F32),
            V((2 * rank, 2 * feats), BF16),
            V((2 * feats, width), BF16),
            V((nx, 2, half, share), F32),
            V((nx, half, share), F32),
            V((pairs, piece, share), F32),
            V((pairs, piece, share), F32),
            V((n, piece, share), F32),
            V((pairs, piece, share), F32),
            V((pairs, piece, gwidth), F32),
            V((pairs, piece, gwidth), F32),
            V((n, piece, gwidth), F32),
            V((pairs, piece, gwidth), F32),
            V((nx, n, piece, share), F32),
            V((nx, n, piece, share), F32),
            V((nx, piece, share), F32),
            V((nx * n, piece, share), F32),
            V((pairs, piece, share), F32),
            V((nx, 8, share), F32),
            V((nx, 8, share), F32),
            V((nx, rank, 128), F32),
            V((rank // 8, 8, 128), F32),
            DMA((PAIR + 2 * nx,)),
            DMA((PAIR + 2 * nx,)),
        ],
        compiler_params=pltpu.CompilerParams(
            collective_id=0, has_side_effects=True, vmem_limit_bytes=32 * 1024 * 1024
        ),
        name="main",
    )(*[pltpu.with_memory_space_constraint(v, pltpu.HBM) for v in operands])
    new_right, basis, gate_grad, hist, grad = pl.pallas_call(
        end_kernel,
        out_shape=tuple(out(shape, dtype) for shape, dtype in kinds),
        in_specs=[vmem] * 5,
        out_specs=(hbm,) * 5,
        scratch_shapes=[DMA((5,))],
        compiler_params=pltpu.CompilerParams(vmem_limit_bytes=8 * 1024 * 1024),
        name="finish",
    )(*results)
    return grad, basis.T, new_right.T, gate_grad, hist.reshape(nbins)


def solution(mesh):
    n = math.isqrt(mesh.shape["dp"] // 2)
    assert 2 * n * n == mesh.shape["dp"]
    placed = (
        P("dp", "tensor"),
        P("tensor", None),
        P("dp", None),
        P("dp", "tensor", None),
        P(),
        P(),
        P(),
        P("dp"),
        P("dp"),
        P("dp"),
    )
    return jax.shard_map(
        functools.partial(per_device, n, mesh.shape["tensor"]),
        mesh=mesh,
        in_specs=placed,
        out_specs=(P("dp", "tensor"), P("tensor", None), P("tensor", None), P(None, "tensor"), P()),
        check_vma=False,
    )
```

```python
import functools
import math

import jax
import jax.numpy as jnp
from jax import lax
from jax.experimental import pallas as pl
from jax.experimental.pallas import tpu as pltpu
from jax.sharding import PartitionSpec as P

MESH = pl.DeviceIdType.MESH
F32 = jnp.float32
BF16 = jnp.bfloat16
HIGHEST = lax.Precision.HIGHEST
NN = (((1,), (0,)), ((), ()))
NT = (((1,), (1,)), ((), ()))


def split(x):
    high = x.astype(BF16)
    low = (x - high.astype(F32)).astype(BF16)
    return jnp.concatenate([high, low], axis=0)


def fold(x):
    half = x.shape[0] // 2
    return x[:half] + x[half:]


def eliminate(ref, begin, end):
    groups, _, width = ref.shape
    sub = lax.broadcasted_iota(jnp.int32, (8, width), 0)

    def wide(x, j):
        return jnp.broadcast_to(x[:, j : j + 1], (8, width))

    def block(k, carry):
        own = ref[k]
        rows = [ref[g] for g in range(groups)]
        for r in range(0, 8, 2):
            first, second = wide(own, r), wide(own, r + 1)
            aa = first[r : r + 1]
            ab = first[r + 1 : r + 2]
            bb = second[r + 1 : r + 2]
            inverse = 1.0 / (aa * bb - ab * ab)
            top = own[r : r + 1]
            low = own[r + 1 : r + 2]
            one = jnp.broadcast_to((bb * inverse) * top - (ab * inverse) * low, (8, width))
            two = jnp.broadcast_to((aa * inverse) * low - (ab * inverse) * top, (8, width))
            if r < 6:
                own = own - jnp.where(sub > r + 1, first * one + second * two, 0.0)
            for g in range(groups):
                change = wide(rows[g], r) * one + wide(rows[g], r + 1) * two
                rows[g] = rows[g] - jnp.where(g > k, change, 0.0)
        for g in range(groups):
            ref[g] = pltpu.roll(jnp.where(g == k, own, rows[g]), width - 8, 1)
        return carry

    lax.fori_loop(begin, end, block, 0)


def unscaled_to_inverse(rows, rank):
    out = []
    width = rows[0].shape[1]
    lane = lax.broadcasted_iota(jnp.int32, (8, width), 1)
    sub = lax.broadcasted_iota(jnp.int32, (8, width), 0)
    odd = lax.rem(sub, 2) == 1
    for g, x in enumerate(rows):
        row = sub + (8 * g + rank)
        before = jnp.concatenate([x[7:], x[:7]], axis=0)
        over = jnp.sum(jnp.where(lane == row - 1, before, 0.0), axis=1, keepdims=True)
        off = jnp.sum(jnp.where(lane == row - 1, x, 0.0), axis=1, keepdims=True)
        x = jnp.where(odd, x - (off / jnp.where(odd[:, :1], over, 1.0)) * before, x)
        diag = jnp.sum(jnp.where(lane == row, x, 0.0), axis=1, keepdims=True)
        out.append(x / jnp.sqrt(diag))
    return jnp.concatenate(out, axis=0)


def far_first(i, n):
    return n // 2 + ((i + 1) // 2) * (1 - 2 * (i % 2))


def each(count, step):
    def body(i, carry):
        step(i)
        return carry

    lax.fori_loop(0, count, body, 0)


def wrap(value, n):
    return jnp.where(value >= n, value - n, value)


A1, TG, A2, A3, G1, G2, G3, GRAM, XX, C5, FIRST = range(11)


def main_kernel(
    n, nx, workers, hist_scale,
    tb_hbm, sw_hbm, head_hbm, weight_hbm, cot_hbm, err_hbm, right_hbm, gate_hbm, loss_hbm, bins_hbm,
    right_o, basis_o, gate_o, hist_o, grad_o,
    tb_ref, sw_ref, head, weight, cot, right, gate, loss, bins, load_sem,
    both_g, head_t, rstack, scale, left_v, stack_v, merged,
    l_src, l_in, l_mid, l_all,
    g_src, g_in, g_mid, g_all,
    s_src, s_in, s_x, s_xin, s_all,
    t_src, t_in, gram, chol,
    ssem, rsem,
):
    rank = right.shape[0]
    tokens, feats = head.shape
    width = cot.shape[1]
    latents, per = loss.shape
    nbins = gate.shape[0]
    share = width // nx
    half = rank // 2
    piece = half // n
    pairs = 2 * n

    index = lax.axis_index("dp")
    x = lax.axis_index("tensor")
    c = lax.rem(index, 2)
    y = lax.rem(index // 2, n)
    z = index // (2 * n)

    def at_z(j, core):
        return ((j * n + y) * 2 + core, x)

    def at_y(j, core):
        return ((z * n + j) * 2 + core, x)

    a = jnp.where(c == 0, z, y)
    b = jnp.where(c == 0, y, z)

    a_step = jnp.where(c == 0, 2 * n, 2)
    a_base = jnp.where(c == 0, 2 * y, 2 * n * z)
    b_step = jnp.where(c == 0, 2, 2 * n)
    b_base = jnp.where(c == 0, 2 * n * z, 2 * y) + c

    def at_a(j, core):
        return (j * a_step + a_base + core, x)

    def at_b(j, t=x):
        return (j * b_step + b_base, t)

    sibling = (index + 1 - 2 * c, x)

    barrier = pltpu.get_barrier_semaphore()

    def greet(device):
        pl.semaphore_signal(barrier, inc=1, device_id=device, device_id_type=MESH)

    @functools.partial(each, n - 1)
    def _(i):
        k = far_first(i, n)
        jz = wrap(z + k, n)
        jy = wrap(y + k, n)
        for core in (0, 1):
            greet(at_z(jz, core))
            greet(at_y(jy, core))

    greet(sibling)

    @functools.partial(each, nx - 1)
    def _(i):
        greet((index, wrap(x + far_first(i, nx), nx)))

    wanted = [(right_hbm, right), (tb_hbm, tb_ref), (sw_hbm, sw_ref), (gate_hbm, gate)]
    for i in range(feats // 128):
        rows = pl.ds(i * 128, 128)
        wanted.append((err_hbm.at[0, rows], both_g.at[rows]))
    for l in range(latents):
        rows = pl.ds(l * per, per)
        wanted.append((cot_hbm.at[rows], cot.at[rows]))
    wanted += [(head_hbm, head), (loss_hbm, loss), (bins_hbm, bins), (weight_hbm, weight)]
    loads = []
    for k, (src, dst) in enumerate(wanted):
        loads.append(pltpu.make_async_copy(src, dst, load_sem.at[k]))
        loads[-1].start()
    e_load = 4
    c_load = e_load + feats // 128
    h_load = c_load + latents

    def remote(src, dst, phase, device):
        return pltpu.make_async_remote_copy(
            src_ref=src, dst_ref=dst, send_sem=ssem.at[phase], recv_sem=rsem.at[phase],
            device_id=device, device_id_type=MESH,
        )

    def scatter_send(src, dst, phase):
        @functools.partial(each, n - 1)
        def _(i):
            k = far_first(i, n)
            jz = wrap(z + k, n)
            jy = wrap(y + k, n)
            remote(src.at[jz], dst.at[z * 2 + c], phase, at_z(jz, 0)).start()
            remote(src.at[n + jy], dst.at[y * 2 + c], phase, at_y(jy, 1)).start()

        @pl.when(c == 1)
        def _():
            remote(src.at[z], dst.at[z * 2 + 1], phase, sibling).start()

        @pl.when(c == 0)
        def _():
            remote(src.at[n + y], dst.at[y * 2], phase, sibling).start()

        dst[a * 2 + c] = src[c * n + a]

    def wait_many(ref, count, phase, recv=True):
        part = ref.at[pl.ds(0, count)]
        copy = remote(part, part, phase, sibling)
        if recv:
            copy.wait_recv()
        else:
            copy.wait_send()

    def sum_slots(ref, count):
        out = ref[0]
        for k in range(1, count):
            out = out + ref[k]
        return out

    def ring_send(ref, phase):
        @functools.partial(each, n - 1)
        def _(i):
            remote(ref.at[b], ref.at[b], phase, at_b(wrap(b + far_first(i, n), n))).start()

    def gather_send(ref, phase):
        mine = c * n + a

        @functools.partial(each, n - 1)
        def _(i):
            j = wrap(a + far_first(i, n), n)
            for core in (0, 1):
                remote(ref.at[mine], ref.at[mine], phase, at_a(j, core)).start()

        remote(ref.at[mine], ref.at[mine], phase, sibling).start()

    loads[0].wait()
    rstack[...] = split(right[...])

    @functools.partial(each, feats // 128)
    def _(i):
        rows = pl.ds(pl.multiple_of(i * 128, 128), 128)
        pltpu.make_async_copy(err_hbm.at[0, rows], both_g.at[rows], load_sem.at[e_load + i]).wait()
        term = lax.dot_general(both_g[rows, :], rstack[...], NT, preferred_element_type=F32)
        left_v[:, rows] = fold(term.T)

    for k in (1, 2, 3):
        loads[k].wait()
    bin_of = lax.broadcasted_iota(jnp.int32, (8, nbins), 1)
    row_of = lax.broadcasted_iota(jnp.int32, (8, nbins), 0)
    onehot = jnp.zeros((8, nbins), F32)
    weights = []
    for l in range(latents):
        tb = tb_ref[l]
        weights.append(sw_ref[tb])
        onehot = jnp.where((row_of == l) & (bin_of == tb), 1.0, onehot)
    gates = lax.dot_general(onehot.astype(BF16), gate[...], NN, preferred_element_type=F32)
    row8 = lax.broadcasted_iota(jnp.int32, (8, width), 0)
    lat8 = jnp.zeros((8, width), F32)
    for l in range(latents):
        lat8 = jnp.where(row8 == l, weights[l], lat8)
    scale[...] = gates * lat8
    loads[h_load].wait()

    @functools.partial(each, latents)
    def _(l):
        rows = pl.ds(pl.multiple_of(l * per, per), per)
        pltpu.make_async_copy(cot_hbm.at[rows], cot.at[rows], load_sem.at[c_load + l]).wait()
        part = (cot[rows, :].astype(F32) * scale[pl.ds(l, 1), :]).astype(BF16)
        both_g[pl.ds(pl.multiple_of(feats + l * per, per), per), :] = part
        mixed = fold(lax.dot_general(part, rstack[...], NT, preferred_element_type=F32).T)
        left_v[...] += fold(lax.dot_general(split(mixed), head[rows, :], NN, preferred_element_type=F32))

    left = left_v[...]
    for k in range(pairs):
        l_src[k] = left[k * piece : (k + 1) * piece]

    pl.semaphore_wait(barrier, 4 * (n - 1) + 1 + (nx - 1))
    scatter_send(l_src, l_in, A1)

    loads[h_load + 3].wait()
    row_s = lax.broadcasted_iota(jnp.int32, (8, share), 0)

    @functools.partial(each, nx)
    def _(t):
        cols = pl.ds(pl.multiple_of(t * share, 128), share)
        out = jnp.zeros((8, share), F32)
        for l in range(latents):
            rows = pl.ds(l * per, per)
            branch = lax.dot_general(head[rows, :], weight[:, cols], NN, preferred_element_type=F32)
            row = jnp.sum(branch * cot[rows, cols].astype(F32), axis=0, keepdims=True) * weights[l]
            out = jnp.where(row_s == l, row, out)
        t_src[t] = out

    stack_v[rank:, feats:] = jnp.zeros((rank, feats), BF16)
    t_in[x] = t_src[x]

    @functools.partial(each, nx - 1)
    def _(i):
        j = wrap(x + far_first(i, nx), nx)
        remote(t_src.at[j], t_in.at[x], TG, (index, j)).start()

    wait_many(l_in, pairs - 1, A1)
    l_mid[b] = sum_slots(l_in, pairs)
    ring_send(l_mid, A2)

    head_t[...] = head[...].T

    @functools.partial(each, nx)
    def _(t):
        cols = pl.ds(pl.multiple_of(t * share, 128), share)
        for i in range(feats // 128):
            rows = pl.ds(i * 128, 128)
            whole = lax.dot_general(head_t[rows, :], both_g[feats:, cols], NN, preferred_element_type=F32)
            whole = whole + both_g[rows, cols].astype(F32)
            high = whole.astype(BF16)
            merged[rows, cols] = high
            merged[pl.ds(feats + i * 128, 128), cols] = (whole - high.astype(F32)).astype(BF16)

    loads[h_load + 1].wait()
    loads[h_load + 2].wait()
    bin_row = lax.broadcasted_iota(jnp.int32, (nbins, per), 0)
    hist = jnp.zeros((nbins, per), F32)
    for l in range(latents):
        hist = hist + jnp.where(bin_row == bins[l : l + 1, :], weights[l] * loss[l : l + 1, :], 0.0)
    wait_many(t_in, nx - 1, TG)
    lat_sum = sum_slots(t_in, nx)
    bin_s = lax.broadcasted_iota(jnp.int32, (nbins, share), 0)
    spread = jnp.zeros((nbins, share), F32)
    for l in range(latents):
        spread = spread + jnp.where(bin_s == tb_ref[l], lat_sum[l : l + 1, :], 0.0)
    for k in range(pairs):
        g_src[k, :, share:] = hist[k * piece : (k + 1) * piece]
        g_src[k, :, :share] = spread[k * piece : (k + 1) * piece]
    scatter_send(g_src, g_in, G1)

    wait_many(l_mid, n - 1, A2)
    l_all[c * n + a] = sum_slots(l_mid, n) * (1.0 / workers)
    gather_send(l_all, A3)

    @functools.partial(each, latents)
    def _(l):
        grad_o[pl.ds(pl.multiple_of(l * per, per), per), :] = lax.dot_general(
            both_g[pl.ds(pl.multiple_of(feats + l * per, per), per), :], weight[...], NT, preferred_element_type=F32
        ).astype(BF16)

    wait_many(g_in, pairs - 1, G1)
    g_mid[b] = sum_slots(g_in, pairs)
    ring_send(g_mid, G2)

    wait_many(l_all, pairs - 1, A3)
    left = jnp.concatenate([l_all[k] for k in range(pairs)], axis=0)
    high = left.astype(BF16)
    low = (left - high.astype(F32)).astype(BF16)
    stack_v[:rank, :feats] = high
    stack_v[:rank, feats:] = high
    stack_v[rank:, :feats] = low

    def target(i):
        return wrap(x + far_first(i, nx), nx)

    @functools.partial(each, nx)
    def _(i):
        cols = pl.ds(pl.multiple_of(target(i) * share, 128), share)
        term = fold(lax.dot_general(stack_v[...], merged[:, cols], NN, preferred_element_type=F32))
        for k in range(pairs):
            s_src[i, k] = term[k * piece : (k + 1) * piece]
        scatter_send(s_src.at[i], s_in.at[i], FIRST + i)

    def part_sum(i):
        wait_many(s_in.at[i], pairs - 1, FIRST + i)
        total = s_in[i, 0]
        for k in range(1, pairs):
            total = total + s_in[i, k]
        return total

    padded = jnp.concatenate([left, jnp.zeros((128 - rank, share), F32)], axis=0)
    gram[x] = lax.dot_general(left, padded, NT, precision=HIGHEST, preferred_element_type=F32)

    @functools.partial(each, nx - 1)
    def _(i):
        remote(gram.at[x], gram.at[x], GRAM, (index, target(i))).start()

    wait_many(g_mid, n - 1, G2)
    g_all[c * n + a] = sum_slots(g_mid, n)
    gather_send(g_all, G3)

    @functools.partial(each, nx - 1)
    def _(i):
        s_x[i] = part_sum(i)

        @functools.partial(each, n)
        def _(k):
            j = wrap(b + far_first(k, n), n)
            remote(s_x.at[i], s_xin.at[x * n + b], XX, at_b(j, target(i))).start()

    groups = rank // 8
    wait_many(gram, nx - 1, GRAM)
    whole = sum_slots(gram, nx)
    eye_r = lax.broadcasted_iota(jnp.int32, (rank, 128), 0)
    eye_c = lax.broadcasted_iota(jnp.int32, (rank, 128), 1)
    whole = jnp.where(eye_c == eye_r + rank, 1.0, whole)
    for g in range(groups):
        chol[g] = whole[8 * g : 8 * g + 8]
    eliminate(chol, 0, groups // 4)
    s_x[nx - 1] = part_sum(nx - 1)
    s_xin[x * n + b] = s_x[nx - 1]

    @functools.partial(each, n - 1)
    def _(k):
        j = wrap(b + far_first(k, n), n)
        remote(s_x.at[nx - 1], s_xin.at[x * n + b], XX, at_b(j)).start()

    eliminate(chol, groups // 4, 5 * groups // 8)

    wait_many(s_xin, nx * n - 1, XX)
    s_all[c * n + a] = sum_slots(s_xin, nx * n)
    gather_send(s_all, C5)
    eliminate(chol, 5 * groups // 8, groups)
    inverse = unscaled_to_inverse([chol[g] for g in range(groups)], rank)[:, :rank]
    basis_o[...] = lax.dot_general(inverse, left, NN, precision=HIGHEST, preferred_element_type=F32)
    wait_many(g_all, pairs - 1, G3)
    gates = jnp.concatenate([g_all[k] for k in range(pairs)], axis=0)
    gate_o[...] = gates[:, :share]
    hist_o[...] = jnp.sum(gates[:, share:], axis=1, keepdims=True).T * hist_scale
    inv_high = inverse.astype(BF16)
    inv_low = (inverse - inv_high.astype(F32)).astype(BF16)
    inv_stack = jnp.concatenate([inv_high, inv_high, inv_low], axis=1)

    wait_many(l_src, pairs - 1, A1, False)
    wait_many(t_src, nx - 1, TG, False)
    wait_many(l_mid, n - 1, A2, False)
    wait_many(l_all, pairs - 1, A3, False)
    wait_many(g_src, pairs - 1, G1, False)

    @functools.partial(each, nx)
    def _(i):
        wait_many(s_src.at[i], pairs - 1, FIRST + i, False)

    wait_many(gram, nx - 1, GRAM, False)
    wait_many(g_mid, n - 1, G2, False)
    wait_many(s_xin, nx * n - 1, XX, False)
    wait_many(g_all, pairs - 1, G3, False)

    wait_many(s_all, pairs - 1, C5)
    s_whole = jnp.concatenate([s_all[k] for k in range(pairs)], axis=0)
    s_high = s_whole.astype(BF16)
    s_low = (s_whole - s_high.astype(F32)).astype(BF16)
    right_o[...] = lax.dot_general(
        inv_stack, jnp.concatenate([s_high, s_low, s_high], axis=0), NN, preferred_element_type=F32
    ) * (1.0 / workers)
    wait_many(s_all, pairs - 1, C5, False)


def end_kernel(*refs):
    count = len(refs) // 2
    sem = refs[-1]
    copies = [pltpu.make_async_copy(refs[k], refs[count + k], sem.at[k]) for k in range(count)]
    for copy in copies:
        copy.start()
    for copy in copies:
        copy.wait()


def per_device(n, nx, head, weight, cot, err, right, gate, sample, tbins, loss, lbins):
    workers = 2 * n * n
    rank = right.shape[1]
    tokens, feats = head.shape
    width = cot.shape[1]
    latents = tbins.shape[0]
    per = tokens // latents
    nbins = gate.shape[0]
    share = width // nx
    half = rank // 2
    piece = half // n
    pairs = 2 * n
    gwidth = share + per
    vmem = pl.BlockSpec(memory_space=pltpu.VMEM)
    hbm = pl.BlockSpec(memory_space=pltpu.HBM)
    V = pltpu.VMEM
    DMA = pltpu.SemaphoreType.DMA
    out = jax.ShapeDtypeStruct
    operands = (
        tbins, sample, head, weight, cot, err, right.T, gate,
        loss.reshape(latents, per), lbins.reshape(latents, per),
    )
    kinds = (
        ((rank, share), F32),
        ((rank, share), F32),
        ((nbins, share), F32),
        ((1, nbins), F32),
        ((tokens, feats), BF16),
    )
    results = pl.pallas_call(
        functools.partial(main_kernel, n, nx, workers, nbins / (tokens * workers)),
        out_shape=tuple(V(shape, dtype) for shape, dtype in kinds),
        in_specs=[hbm] * 10,
        out_specs=(vmem,) * 5,
        scratch_shapes=[
            pltpu.SMEM(tbins.shape, jnp.int32),
            pltpu.SMEM(sample.shape, F32),
            V(head.shape, BF16),
            V(weight.shape, BF16),
            V(cot.shape, BF16),
            V((rank, width), F32),
            V(gate.shape, BF16),
            V((latents, per), F32),
            V((latents, per), jnp.int32),
            DMA((8 + feats // 128 + latents,)),
            V((feats + tokens, width), BF16),
            V((feats, tokens), BF16),
            V((2 * rank, width), BF16),
            V((8, width), F32),
            V((rank, share), F32),
            V((2 * rank, 2 * feats), BF16),
            V((2 * feats, width), BF16),
            V((pairs, piece, share), F32),
            V((pairs, piece, share), F32),
            V((n, piece, share), F32),
            V((pairs, piece, share), F32),
            V((pairs, piece, gwidth), F32),
            V((pairs, piece, gwidth), F32),
            V((n, piece, gwidth), F32),
            V((pairs, piece, gwidth), F32),
            V((nx, pairs, piece, share), F32),
            V((nx, pairs, piece, share), F32),
            V((nx, piece, share), F32),
            V((nx * n, piece, share), F32),
            V((pairs, piece, share), F32),
            V((nx, 8, share), F32),
            V((nx, 8, share), F32),
            V((nx, rank, 128), F32),
            V((rank // 8, 8, 128), F32),
            DMA((FIRST + nx,)),
            DMA((FIRST + nx,)),
        ],
        compiler_params=pltpu.CompilerParams(
            collective_id=0, has_side_effects=True, vmem_limit_bytes=32 * 1024 * 1024
        ),
        name="main",
    )(*[pltpu.with_memory_space_constraint(v, pltpu.HBM) for v in operands])
    new_right, basis, gate_grad, hist, grad = pl.pallas_call(
        end_kernel,
        out_shape=tuple(out(shape, dtype) for shape, dtype in kinds),
        in_specs=[vmem] * 5,
        out_specs=(hbm,) * 5,
        scratch_shapes=[DMA((5,))],
        compiler_params=pltpu.CompilerParams(vmem_limit_bytes=8 * 1024 * 1024),
        name="finish",
    )(*results)
    return grad, basis.T, new_right.T, gate_grad, hist.reshape(nbins)


def solution(mesh):
    n = math.isqrt(mesh.shape["dp"] // 2)
    assert 2 * n * n == mesh.shape["dp"]
    placed = (
        P("dp", "tensor"),
        P("tensor", None),
        P("dp", None),
        P("dp", "tensor", None),
        P(),
        P(),
        P(),
        P("dp"),
        P("dp"),
        P("dp"),
    )
    return jax.shard_map(
        functools.partial(per_device, n, mesh.shape["tensor"]),
        mesh=mesh,
        in_specs=placed,
        out_specs=(P("dp", "tensor"), P("tensor", None), P("tensor", None), P(None, "tensor"), P()),
        check_vma=False,
    )
```

```python
import functools
import math

import jax
import jax.numpy as jnp
from jax import lax
from jax.experimental import pallas as pl
from jax.experimental.pallas import tpu as pltpu
from jax.sharding import PartitionSpec as P

MESH = pl.DeviceIdType.MESH
F32 = jnp.float32
BF16 = jnp.bfloat16
HIGHEST = lax.Precision.HIGHEST
NN = (((1,), (0,)), ((), ()))
NT = (((1,), (1,)), ((), ()))


def split(x):
    high = x.astype(BF16)
    low = (x - high.astype(F32)).astype(BF16)
    return jnp.concatenate([high, low], axis=0)


def fold(x):
    half = x.shape[0] // 2
    return x[:half] + x[half:]


def eliminate(ref, begin, end):
    groups, _, width = ref.shape
    sub = lax.broadcasted_iota(jnp.int32, (8, width), 0)

    def wide(x, j):
        return jnp.broadcast_to(x[:, j : j + 1], (8, width))

    def block(k, carry):
        own = ref[k]
        rows = [ref[g] for g in range(groups)]
        for r in range(0, 8, 2):
            first, second = wide(own, r), wide(own, r + 1)
            aa = first[r : r + 1]
            ab = first[r + 1 : r + 2]
            bb = second[r + 1 : r + 2]
            inverse = 1.0 / (aa * bb - ab * ab)
            top = own[r : r + 1]
            low = own[r + 1 : r + 2]
            one = jnp.broadcast_to((bb * inverse) * top - (ab * inverse) * low, (8, width))
            two = jnp.broadcast_to((aa * inverse) * low - (ab * inverse) * top, (8, width))
            if r < 6:
                own = own - jnp.where(sub > r + 1, first * one + second * two, 0.0)
            for g in range(groups):
                change = wide(rows[g], r) * one + wide(rows[g], r + 1) * two
                rows[g] = rows[g] - jnp.where(g > k, change, 0.0)
        for g in range(groups):
            ref[g] = pltpu.roll(jnp.where(g == k, own, rows[g]), width - 8, 1)
        return carry

    lax.fori_loop(begin, end, block, 0)


def unscaled_to_inverse(rows, rank):
    out = []
    width = rows[0].shape[1]
    lane = lax.broadcasted_iota(jnp.int32, (8, width), 1)
    sub = lax.broadcasted_iota(jnp.int32, (8, width), 0)
    odd = lax.rem(sub, 2) == 1
    for g, x in enumerate(rows):
        row = sub + (8 * g + rank)
        before = jnp.concatenate([x[7:], x[:7]], axis=0)
        over = jnp.sum(jnp.where(lane == row - 1, before, 0.0), axis=1, keepdims=True)
        off = jnp.sum(jnp.where(lane == row - 1, x, 0.0), axis=1, keepdims=True)
        x = jnp.where(odd, x - (off / jnp.where(odd[:, :1], over, 1.0)) * before, x)
        diag = jnp.sum(jnp.where(lane == row, x, 0.0), axis=1, keepdims=True)
        out.append(x / jnp.sqrt(diag))
    return jnp.concatenate(out, axis=0)


def far_first(i, n):
    return n // 2 + ((i + 1) // 2) * (1 - 2 * (i % 2))


def each(count, step):
    def body(i, carry):
        step(i)
        return carry

    lax.fori_loop(0, count, body, 0)


def wrap(value, n):
    return jnp.where(value >= n, value - n, value)


A1, TG, A2, A3, G1, G2, G3, GRAM, XX, C5, PAIR = range(11)


def main_kernel(
    n, nx, workers, hist_scale,
    tb_hbm, sw_hbm, head_hbm, weight_hbm, cot_hbm, err_hbm, right_hbm, gate_hbm, loss_hbm, bins_hbm,
    right_o, basis_o, gate_o, hist_o, grad_o,
    tb_ref, sw_ref, head, weight, cot, right, gate, loss, bins, load_sem,
    both_g, head_t, rstack, scale, left_v, stack_v, merged, own_s, sib_s,
    l_src, l_in, l_mid, l_all,
    g_src, g_in, g_mid, g_all,
    s_src, s_in, s_x, s_xin, s_all,
    t_src, t_in, gram, chol,
    ssem, rsem,
):
    rank = right.shape[0]
    tokens, feats = head.shape
    width = cot.shape[1]
    latents, per = loss.shape
    nbins = gate.shape[0]
    share = width // nx
    half = rank // 2
    piece = half // n
    pairs = 2 * n
    FIRST = PAIR + nx

    index = lax.axis_index("dp")
    x = lax.axis_index("tensor")
    c = lax.rem(index, 2)
    y = lax.rem(index // 2, n)
    z = index // (2 * n)

    def at_z(j, core):
        return ((j * n + y) * 2 + core, x)

    def at_y(j, core):
        return ((z * n + j) * 2 + core, x)

    a = jnp.where(c == 0, z, y)
    b = jnp.where(c == 0, y, z)

    a_step = jnp.where(c == 0, 2 * n, 2)
    a_base = jnp.where(c == 0, 2 * y, 2 * n * z)
    b_step = jnp.where(c == 0, 2, 2 * n)
    b_base = jnp.where(c == 0, 2 * n * z, 2 * y) + c

    def at_a(j, core):
        return (j * a_step + a_base + core, x)

    def at_b(j, t=x):
        return (j * b_step + b_base, t)

    sibling = (index + 1 - 2 * c, x)

    barrier = pltpu.get_barrier_semaphore()

    def greet(device):
        pl.semaphore_signal(barrier, inc=1, device_id=device, device_id_type=MESH)

    @functools.partial(each, n - 1)
    def _(i):
        k = far_first(i, n)
        jz = wrap(z + k, n)
        jy = wrap(y + k, n)
        for core in (0, 1):
            greet(at_z(jz, core))
            greet(at_y(jy, core))

    greet(sibling)

    @functools.partial(each, nx - 1)
    def _(i):
        greet((index, wrap(x + far_first(i, nx), nx)))

    wanted = [(right_hbm, right), (tb_hbm, tb_ref), (sw_hbm, sw_ref), (gate_hbm, gate)]
    for i in range(feats // 128):
        rows = pl.ds(i * 128, 128)
        wanted.append((err_hbm.at[0, rows], both_g.at[rows]))
    for l in range(latents):
        rows = pl.ds(l * per, per)
        wanted.append((cot_hbm.at[rows], cot.at[rows]))
    wanted += [(head_hbm, head), (loss_hbm, loss), (bins_hbm, bins), (weight_hbm, weight)]
    loads = []
    for k, (src, dst) in enumerate(wanted):
        loads.append(pltpu.make_async_copy(src, dst, load_sem.at[k]))
        loads[-1].start()
    e_load = 4
    c_load = e_load + feats // 128
    h_load = c_load + latents

    def remote(src, dst, phase, device):
        return pltpu.make_async_remote_copy(
            src_ref=src, dst_ref=dst, send_sem=ssem.at[phase], recv_sem=rsem.at[phase],
            device_id=device, device_id_type=MESH,
        )

    def scatter_send(src, dst, phase):
        @functools.partial(each, n - 1)
        def _(i):
            k = far_first(i, n)
            jz = wrap(z + k, n)
            jy = wrap(y + k, n)
            remote(src.at[jz], dst.at[z * 2 + c], phase, at_z(jz, 0)).start()
            remote(src.at[n + jy], dst.at[y * 2 + c], phase, at_y(jy, 1)).start()

        @pl.when(c == 1)
        def _():
            remote(src.at[z], dst.at[z * 2 + 1], phase, sibling).start()

        @pl.when(c == 0)
        def _():
            remote(src.at[n + y], dst.at[y * 2], phase, sibling).start()

        dst[a * 2 + c] = src[c * n + a]

    def wait_many(ref, count, phase, recv=True):
        part = ref.at[pl.ds(0, count)]
        copy = remote(part, part, phase, sibling)
        if recv:
            copy.wait_recv()
        else:
            copy.wait_send()

    def sum_slots(ref, count):
        out = ref[0]
        for k in range(1, count):
            out = out + ref[k]
        return out

    def ring_send(ref, phase):
        @functools.partial(each, n - 1)
        def _(i):
            remote(ref.at[b], ref.at[b], phase, at_b(wrap(b + far_first(i, n), n))).start()

    def gather_send(ref, phase):
        mine = c * n + a

        @functools.partial(each, n - 1)
        def _(i):
            j = wrap(a + far_first(i, n), n)
            for core in (0, 1):
                remote(ref.at[mine], ref.at[mine], phase, at_a(j, core)).start()

        remote(ref.at[mine], ref.at[mine], phase, sibling).start()

    loads[0].wait()
    rstack[...] = split(right[...])

    @functools.partial(each, feats // 128)
    def _(i):
        rows = pl.ds(pl.multiple_of(i * 128, 128), 128)
        pltpu.make_async_copy(err_hbm.at[0, rows], both_g.at[rows], load_sem.at[e_load + i]).wait()
        term = lax.dot_general(both_g[rows, :], rstack[...], NT, preferred_element_type=F32)
        left_v[:, rows] = fold(term.T)

    for k in (1, 2, 3):
        loads[k].wait()
    bin_of = lax.broadcasted_iota(jnp.int32, (8, nbins), 1)
    row_of = lax.broadcasted_iota(jnp.int32, (8, nbins), 0)
    onehot = jnp.zeros((8, nbins), F32)
    weights = []
    for l in range(latents):
        tb = tb_ref[l]
        weights.append(sw_ref[tb])
        onehot = jnp.where((row_of == l) & (bin_of == tb), 1.0, onehot)
    gates = lax.dot_general(onehot.astype(BF16), gate[...], NN, preferred_element_type=F32)
    row8 = lax.broadcasted_iota(jnp.int32, (8, width), 0)
    lat8 = jnp.zeros((8, width), F32)
    for l in range(latents):
        lat8 = jnp.where(row8 == l, weights[l], lat8)
    scale[...] = gates * lat8
    loads[h_load].wait()

    @functools.partial(each, latents)
    def _(l):
        rows = pl.ds(pl.multiple_of(l * per, per), per)
        pltpu.make_async_copy(cot_hbm.at[rows], cot.at[rows], load_sem.at[c_load + l]).wait()
        part = (cot[rows, :].astype(F32) * scale[pl.ds(l, 1), :]).astype(BF16)
        both_g[pl.ds(pl.multiple_of(feats + l * per, per), per), :] = part
        mixed = fold(lax.dot_general(part, rstack[...], NT, preferred_element_type=F32).T)
        left_v[...] += fold(lax.dot_general(split(mixed), head[rows, :], NN, preferred_element_type=F32))

    left = left_v[...]
    for k in range(pairs):
        l_src[k] = left[k * piece : (k + 1) * piece]

    pl.semaphore_wait(barrier, 4 * (n - 1) + 1 + (nx - 1))
    scatter_send(l_src, l_in, A1)

    loads[h_load + 3].wait()
    row_s = lax.broadcasted_iota(jnp.int32, (8, share), 0)

    @functools.partial(each, nx)
    def _(t):
        cols = pl.ds(pl.multiple_of(t * share, 128), share)
        out = jnp.zeros((8, share), F32)
        for l in range(latents):
            rows = pl.ds(l * per, per)
            branch = lax.dot_general(head[rows, :], weight[:, cols], NN, preferred_element_type=F32)
            row = jnp.sum(branch * cot[rows, cols].astype(F32), axis=0, keepdims=True) * weights[l]
            out = jnp.where(row_s == l, row, out)
        t_src[t] = out

    stack_v[rank:, feats:] = jnp.zeros((rank, feats), BF16)
    t_in[x] = t_src[x]

    @functools.partial(each, nx - 1)
    def _(i):
        j = wrap(x + far_first(i, nx), nx)
        remote(t_src.at[j], t_in.at[x], TG, (index, j)).start()

    wait_many(l_in, pairs - 1, A1)
    l_mid[b] = sum_slots(l_in, pairs)
    ring_send(l_mid, A2)

    head_t[...] = head[...].T

    @functools.partial(each, nx)
    def _(t):
        cols = pl.ds(pl.multiple_of(t * share, 128), share)
        for i in range(feats // 128):
            rows = pl.ds(i * 128, 128)
            whole = lax.dot_general(head_t[rows, :], both_g[feats:, cols], NN, preferred_element_type=F32)
            whole = whole + both_g[rows, cols].astype(F32)
            high = whole.astype(BF16)
            merged[rows, cols] = high
            merged[pl.ds(feats + i * 128, 128), cols] = (whole - high.astype(F32)).astype(BF16)

    loads[h_load + 1].wait()
    loads[h_load + 2].wait()
    bin_row = lax.broadcasted_iota(jnp.int32, (nbins, per), 0)
    hist = jnp.zeros((nbins, per), F32)
    for l in range(latents):
        hist = hist + jnp.where(bin_row == bins[l : l + 1, :], weights[l] * loss[l : l + 1, :], 0.0)
    wait_many(t_in, nx - 1, TG)
    lat_sum = sum_slots(t_in, nx)
    bin_s = lax.broadcasted_iota(jnp.int32, (nbins, share), 0)
    spread = jnp.zeros((nbins, share), F32)
    for l in range(latents):
        spread = spread + jnp.where(bin_s == tb_ref[l], lat_sum[l : l + 1, :], 0.0)
    for k in range(pairs):
        g_src[k, :, share:] = hist[k * piece : (k + 1) * piece]
        g_src[k, :, :share] = spread[k * piece : (k + 1) * piece]
    scatter_send(g_src, g_in, G1)

    wait_many(l_mid, n - 1, A2)
    l_all[c * n + a] = sum_slots(l_mid, n) * (1.0 / workers)
    gather_send(l_all, A3)

    @functools.partial(each, latents)
    def _(l):
        grad_o[pl.ds(pl.multiple_of(l * per, per), per), :] = lax.dot_general(
            both_g[pl.ds(pl.multiple_of(feats + l * per, per), per), :], weight[...], NT, preferred_element_type=F32
        ).astype(BF16)

    wait_many(g_in, pairs - 1, G1)
    g_mid[b] = sum_slots(g_in, pairs)
    ring_send(g_mid, G2)

    wait_many(l_all, pairs - 1, A3)
    left = jnp.concatenate([l_all[k] for k in range(pairs)], axis=0)
    high = left.astype(BF16)
    low = (left - high.astype(F32)).astype(BF16)
    stack_v[:rank, :feats] = high
    stack_v[:rank, feats:] = high
    stack_v[rank:, :feats] = low

    def target(i):
        return wrap(x + far_first(i, nx), nx)

    def part_start(i):
        cols = pl.ds(pl.multiple_of(target(i) * share, 128), share)
        term = fold(lax.dot_general(stack_v[...], merged[:, cols], NN, preferred_element_type=F32))
        own_s[i, 0] = term[:half]
        own_s[i, 1] = term[half:]
        remote(own_s.at[i, 1 - c], sib_s.at[i], PAIR + i, sibling).start()

    def part_scatter(i):
        remote(sib_s.at[i], sib_s.at[i], PAIR + i, sibling).wait_recv()
        total = own_s[i, c] + sib_s[i]
        for k in range(n):
            s_src[i, k] = total[k * piece : (k + 1) * piece]
        s_in[i, a] = s_src[i, a]

        @functools.partial(each, n - 1)
        def _(k):
            j = wrap(a + far_first(k, n), n)
            remote(s_src.at[i, j], s_in.at[i, a], FIRST + i, at_a(j, c)).start()

    def part_sum(i):
        wait_many(s_in.at[i], n - 1, FIRST + i)
        total = s_in[i, 0]
        for k in range(1, n):
            total = total + s_in[i, k]
        return total

    each(nx, part_start)
    padded = jnp.concatenate([left, jnp.zeros((128 - rank, share), F32)], axis=0)
    gram[x] = lax.dot_general(left, padded, NT, precision=HIGHEST, preferred_element_type=F32)

    @functools.partial(each, nx - 1)
    def _(i):
        remote(gram.at[x], gram.at[x], GRAM, (index, target(i))).start()

    each(nx, part_scatter)


    @functools.partial(each, nx - 1)
    def _(i):
        s_x[i] = part_sum(i)

        @functools.partial(each, n)
        def _(k):
            j = wrap(b + far_first(k, n), n)
            remote(s_x.at[i], s_xin.at[x * n + b], XX, at_b(j, target(i))).start()

    groups = rank // 8
    wait_many(gram, nx - 1, GRAM)
    whole = sum_slots(gram, nx)
    eye_r = lax.broadcasted_iota(jnp.int32, (rank, 128), 0)
    eye_c = lax.broadcasted_iota(jnp.int32, (rank, 128), 1)
    whole = jnp.where(eye_c == eye_r + rank, 1.0, whole)
    for g in range(groups):
        chol[g] = whole[8 * g : 8 * g + 8]
    eliminate(chol, 0, groups // 4)
    s_x[nx - 1] = part_sum(nx - 1)
    s_xin[x * n + b] = s_x[nx - 1]

    @functools.partial(each, n - 1)
    def _(k):
        j = wrap(b + far_first(k, n), n)
        remote(s_x.at[nx - 1], s_xin.at[x * n + b], XX, at_b(j)).start()

    wait_many(g_mid, n - 1, G2)
    g_all[c * n + a] = sum_slots(g_mid, n)
    gather_send(g_all, G3)
    eliminate(chol, groups // 4, 5 * groups // 8)

    wait_many(s_xin, nx * n - 1, XX)
    s_all[c * n + a] = sum_slots(s_xin, nx * n)
    gather_send(s_all, C5)
    eliminate(chol, 5 * groups // 8, groups)
    inverse = unscaled_to_inverse([chol[g] for g in range(groups)], rank)[:, :rank]
    basis_o[...] = lax.dot_general(inverse, left, NN, precision=HIGHEST, preferred_element_type=F32)
    wait_many(g_all, pairs - 1, G3)
    gates = jnp.concatenate([g_all[k] for k in range(pairs)], axis=0)
    gate_o[...] = gates[:, :share]
    hist_o[...] = jnp.sum(gates[:, share:], axis=1, keepdims=True).T * hist_scale
    inv_high = inverse.astype(BF16)
    inv_low = (inverse - inv_high.astype(F32)).astype(BF16)
    inv_stack = jnp.concatenate([inv_high, inv_high, inv_low], axis=1)

    wait_many(l_src, pairs - 1, A1, False)
    wait_many(t_src, nx - 1, TG, False)
    wait_many(l_mid, n - 1, A2, False)
    wait_many(l_all, pairs - 1, A3, False)
    wait_many(g_src, pairs - 1, G1, False)

    @functools.partial(each, nx)
    def _(i):
        remote(sib_s.at[i], sib_s.at[i], PAIR + i, sibling).wait_send()
        wait_many(s_src.at[i], n - 1, FIRST + i, False)

    wait_many(gram, nx - 1, GRAM, False)
    wait_many(g_mid, n - 1, G2, False)
    wait_many(s_xin, nx * n - 1, XX, False)
    wait_many(g_all, pairs - 1, G3, False)

    wait_many(s_all, pairs - 1, C5)
    s_whole = jnp.concatenate([s_all[k] for k in range(pairs)], axis=0)
    s_high = s_whole.astype(BF16)
    s_low = (s_whole - s_high.astype(F32)).astype(BF16)
    right_o[...] = lax.dot_general(
        inv_stack, jnp.concatenate([s_high, s_low, s_high], axis=0), NN, preferred_element_type=F32
    ) * (1.0 / workers)
    wait_many(s_all, pairs - 1, C5, False)


def end_kernel(*refs):
    count = len(refs) // 2
    sem = refs[-1]
    copies = [pltpu.make_async_copy(refs[k], refs[count + k], sem.at[k]) for k in range(count)]
    for copy in copies:
        copy.start()
    for copy in copies:
        copy.wait()


def per_device(n, nx, head, weight, cot, err, right, gate, sample, tbins, loss, lbins):
    workers = 2 * n * n
    rank = right.shape[1]
    tokens, feats = head.shape
    width = cot.shape[1]
    latents = tbins.shape[0]
    per = tokens // latents
    nbins = gate.shape[0]
    share = width // nx
    half = rank // 2
    piece = half // n
    pairs = 2 * n
    gwidth = share + per
    vmem = pl.BlockSpec(memory_space=pltpu.VMEM)
    hbm = pl.BlockSpec(memory_space=pltpu.HBM)
    V = pltpu.VMEM
    DMA = pltpu.SemaphoreType.DMA
    out = jax.ShapeDtypeStruct
    operands = (
        tbins, sample, head, weight, cot, err, right.T, gate,
        loss.reshape(latents, per), lbins.reshape(latents, per),
    )
    kinds = (
        ((rank, share), F32),
        ((rank, share), F32),
        ((nbins, share), F32),
        ((1, nbins), F32),
        ((tokens, feats), BF16),
    )
    results = pl.pallas_call(
        functools.partial(main_kernel, n, nx, workers, nbins / (tokens * workers)),
        out_shape=tuple(V(shape, dtype) for shape, dtype in kinds),
        in_specs=[hbm] * 10,
        out_specs=(vmem,) * 5,
        scratch_shapes=[
            pltpu.SMEM(tbins.shape, jnp.int32),
            pltpu.SMEM(sample.shape, F32),
            V(head.shape, BF16),
            V(weight.shape, BF16),
            V(cot.shape, BF16),
            V((rank, width), F32),
            V(gate.shape, BF16),
            V((latents, per), F32),
            V((latents, per), jnp.int32),
            DMA((8 + feats // 128 + latents,)),
            V((feats + tokens, width), BF16),
            V((feats, tokens), BF16),
            V((2 * rank, width), BF16),
            V((8, width), F32),
            V((rank, share), F32),
            V((2 * rank, 2 * feats), BF16),
            V((2 * feats, width), BF16),
            V((nx, 2, half, share), F32),
            V((nx, half, share), F32),
            V((pairs, piece, share), F32),
            V((pairs, piece, share), F32),
            V((n, piece, share), F32),
            V((pairs, piece, share), F32),
            V((pairs, piece, gwidth), F32),
            V((pairs, piece, gwidth), F32),
            V((n, piece, gwidth), F32),
            V((pairs, piece, gwidth), F32),
            V((nx, n, piece, share), F32),
            V((nx, n, piece, share), F32),
            V((nx, piece, share), F32),
            V((nx * n, piece, share), F32),
            V((pairs, piece, share), F32),
            V((nx, 8, share), F32),
            V((nx, 8, share), F32),
            V((nx, rank, 128), F32),
            V((rank // 8, 8, 128), F32),
            DMA((PAIR + 2 * nx,)),
            DMA((PAIR + 2 * nx,)),
        ],
        compiler_params=pltpu.CompilerParams(
            collective_id=0, has_side_effects=True, vmem_limit_bytes=32 * 1024 * 1024
        ),
        name="main",
    )(*[pltpu.with_memory_space_constraint(v, pltpu.HBM) for v in operands])
    new_right, basis, gate_grad, hist, grad = pl.pallas_call(
        end_kernel,
        out_shape=tuple(out(shape, dtype) for shape, dtype in kinds),
        in_specs=[vmem] * 5,
        out_specs=(hbm,) * 5,
        scratch_shapes=[DMA((5,))],
        compiler_params=pltpu.CompilerParams(vmem_limit_bytes=8 * 1024 * 1024),
        name="finish",
    )(*results)
    return grad, basis.T, new_right.T, gate_grad, hist.reshape(nbins)


def solution(mesh):
    n = math.isqrt(mesh.shape["dp"] // 2)
    assert 2 * n * n == mesh.shape["dp"]
    placed = (
        P("dp", "tensor"),
        P("tensor", None),
        P("dp", None),
        P("dp", "tensor", None),
        P(),
        P(),
        P(),
        P("dp"),
        P("dp"),
        P("dp"),
    )
    return jax.shard_map(
        functools.partial(per_device, n, mesh.shape["tensor"]),
        mesh=mesh,
        in_specs=placed,
        out_specs=(P("dp", "tensor"), P("tensor", None), P("tensor", None), P(None, "tensor"), P()),
        check_vma=False,
    )
```

```python
import functools
import math

import jax
import jax.numpy as jnp
from jax import lax
from jax.experimental import pallas as pl
from jax.experimental.pallas import tpu as pltpu
from jax.sharding import PartitionSpec as P

MESH = pl.DeviceIdType.MESH
F32 = jnp.float32
BF16 = jnp.bfloat16
HIGHEST = lax.Precision.HIGHEST
NN = (((1,), (0,)), ((), ()))
NT = (((1,), (1,)), ((), ()))


def split(x):
    high = x.astype(BF16)
    low = (x - high.astype(F32)).astype(BF16)
    return jnp.concatenate([high, low], axis=0)


def fold(x):
    half = x.shape[0] // 2
    return x[:half] + x[half:]


def eliminate(ref, begin, end, low_group):
    groups, _, width = ref.shape
    active = range(low_group, groups)
    sub = lax.broadcasted_iota(jnp.int32, (8, width), 0)

    def wide(x, j):
        return jnp.broadcast_to(x[:, j : j + 1], (8, width))

    def block(k, carry):
        own = ref[k]
        rows = {g: ref[g] for g in active}
        for r in range(0, 8, 2):
            first, second = wide(own, r), wide(own, r + 1)
            aa = first[r : r + 1]
            ab = first[r + 1 : r + 2]
            bb = second[r + 1 : r + 2]
            inverse = 1.0 / (aa * bb - ab * ab)
            top = own[r : r + 1]
            low = own[r + 1 : r + 2]
            one = jnp.broadcast_to((bb * inverse) * top - (ab * inverse) * low, (8, width))
            two = jnp.broadcast_to((aa * inverse) * low - (ab * inverse) * top, (8, width))
            if r < 6:
                own = own - jnp.where(sub > r + 1, first * one + second * two, 0.0)
            for g in active:
                change = wide(rows[g], r) * one + wide(rows[g], r + 1) * two
                rows[g] = rows[g] - jnp.where(g > k, change, 0.0)
        for g in active:
            ref[g] = pltpu.roll(jnp.where(g == k, own, rows[g]), width - 8, 1)
        return carry

    lax.fori_loop(begin, end, block, 0)


def unscaled_to_inverse(rows, rank):
    out = []
    width = rows[0].shape[1]
    lane = lax.broadcasted_iota(jnp.int32, (8, width), 1)
    sub = lax.broadcasted_iota(jnp.int32, (8, width), 0)
    odd = lax.rem(sub, 2) == 1
    for g, x in enumerate(rows):
        row = sub + (8 * g + rank)
        before = jnp.concatenate([x[7:], x[:7]], axis=0)
        over = jnp.sum(jnp.where(lane == row - 1, before, 0.0), axis=1, keepdims=True)
        off = jnp.sum(jnp.where(lane == row - 1, x, 0.0), axis=1, keepdims=True)
        x = jnp.where(odd, x - (off / jnp.where(odd[:, :1], over, 1.0)) * before, x)
        diag = jnp.sum(jnp.where(lane == row, x, 0.0), axis=1, keepdims=True)
        out.append(x / jnp.sqrt(diag))
    return jnp.concatenate(out, axis=0)


def far_first(i, n):
    return n // 2 + ((i + 1) // 2) * (1 - 2 * (i % 2))


def each(count, step):
    def body(i, carry):
        step(i)
        return carry

    lax.fori_loop(0, count, body, 0)


def wrap(value, n):
    return jnp.where(value >= n, value - n, value)


A1, TG, A2, A3, G1, G2, G3, GRAM, XX, C5, PAIR = range(11)


def main_kernel(
    n, nx, workers, hist_scale,
    tb_hbm, sw_hbm, head_hbm, weight_hbm, cot_hbm, err_hbm, right_hbm, gate_hbm, loss_hbm, bins_hbm,
    right_o, basis_o, gate_o, hist_o, grad_o,
    tb_ref, sw_ref, head, weight, cot, right, gate, loss, bins, load_sem,
    both_g, head_t, rstack, scale, left_v, stack_v, merged, own_s, sib_s,
    l_src, l_in, l_mid, l_all,
    g_src, g_in, g_mid, g_all,
    s_src, s_in, s_x, s_xin, s_all,
    t_src, t_in, gram, chol,
    ssem, rsem,
):
    rank = right.shape[0]
    tokens, feats = head.shape
    width = cot.shape[1]
    latents, per = loss.shape
    nbins = gate.shape[0]
    share = width // nx
    half = rank // 2
    piece = half // n
    pairs = 2 * n
    FIRST = PAIR + nx

    index = lax.axis_index("dp")
    x = lax.axis_index("tensor")
    c = lax.rem(index, 2)
    y = lax.rem(index // 2, n)
    z = index // (2 * n)

    def at_z(j, core):
        return ((j * n + y) * 2 + core, x)

    def at_y(j, core):
        return ((z * n + j) * 2 + core, x)

    a = jnp.where(c == 0, z, y)
    b = jnp.where(c == 0, y, z)

    a_step = jnp.where(c == 0, 2 * n, 2)
    a_base = jnp.where(c == 0, 2 * y, 2 * n * z)
    b_step = jnp.where(c == 0, 2, 2 * n)
    b_base = jnp.where(c == 0, 2 * n * z, 2 * y) + c

    def at_a(j, core):
        return (j * a_step + a_base + core, x)

    def at_b(j, t=x):
        return (j * b_step + b_base, t)

    sibling = (index + 1 - 2 * c, x)

    barrier = pltpu.get_barrier_semaphore()

    def greet(device):
        pl.semaphore_signal(barrier, inc=1, device_id=device, device_id_type=MESH)

    @functools.partial(each, n - 1)
    def _(i):
        k = far_first(i, n)
        jz = wrap(z + k, n)
        jy = wrap(y + k, n)
        for core in (0, 1):
            greet(at_z(jz, core))
            greet(at_y(jy, core))

    greet(sibling)

    @functools.partial(each, nx - 1)
    def _(i):
        greet((index, wrap(x + far_first(i, nx), nx)))

    wanted = [(right_hbm, right), (tb_hbm, tb_ref), (sw_hbm, sw_ref), (gate_hbm, gate)]
    for i in range(feats // 128):
        rows = pl.ds(i * 128, 128)
        wanted.append((err_hbm.at[0, rows], both_g.at[rows]))
    for l in range(latents):
        rows = pl.ds(l * per, per)
        wanted.append((cot_hbm.at[rows], cot.at[rows]))
    wanted += [(head_hbm, head), (loss_hbm, loss), (bins_hbm, bins), (weight_hbm, weight)]
    loads = []
    for k, (src, dst) in enumerate(wanted):
        loads.append(pltpu.make_async_copy(src, dst, load_sem.at[k]))
        loads[-1].start()
    e_load = 4
    c_load = e_load + feats // 128
    h_load = c_load + latents

    def remote(src, dst, phase, device):
        return pltpu.make_async_remote_copy(
            src_ref=src, dst_ref=dst, send_sem=ssem.at[phase], recv_sem=rsem.at[phase],
            device_id=device, device_id_type=MESH,
        )

    def scatter_send(src, dst, phase):
        @functools.partial(each, n - 1)
        def _(i):
            k = far_first(i, n)
            jz = wrap(z + k, n)
            jy = wrap(y + k, n)
            remote(src.at[jz], dst.at[z * 2 + c], phase, at_z(jz, 0)).start()
            remote(src.at[n + jy], dst.at[y * 2 + c], phase, at_y(jy, 1)).start()

        @pl.when(c == 1)
        def _():
            remote(src.at[z], dst.at[z * 2 + 1], phase, sibling).start()

        @pl.when(c == 0)
        def _():
            remote(src.at[n + y], dst.at[y * 2], phase, sibling).start()

        dst[a * 2 + c] = src[c * n + a]

    def wait_many(ref, count, phase, recv=True):
        part = ref.at[pl.ds(0, count)]
        copy = remote(part, part, phase, sibling)
        if recv:
            copy.wait_recv()
        else:
            copy.wait_send()

    def sum_slots(ref, count):
        out = ref[0]
        for k in range(1, count):
            out = out + ref[k]
        return out

    def ring_send(ref, phase):
        @functools.partial(each, n - 1)
        def _(i):
            remote(ref.at[b], ref.at[b], phase, at_b(wrap(b + far_first(i, n), n))).start()

    def gather_send(ref, phase):
        mine = c * n + a

        @functools.partial(each, n - 1)
        def _(i):
            j = wrap(a + far_first(i, n), n)
            for core in (0, 1):
                remote(ref.at[mine], ref.at[mine], phase, at_a(j, core)).start()

        remote(ref.at[mine], ref.at[mine], phase, sibling).start()

    loads[0].wait()
    rstack[...] = split(right[...])

    @functools.partial(each, feats // 128)
    def _(i):
        rows = pl.ds(pl.multiple_of(i * 128, 128), 128)
        pltpu.make_async_copy(err_hbm.at[0, rows], both_g.at[rows], load_sem.at[e_load + i]).wait()
        term = lax.dot_general(both_g[rows, :], rstack[...], NT, preferred_element_type=F32)
        left_v[:, rows] = fold(term.T)

    for k in (1, 2, 3):
        loads[k].wait()
    bin_of = lax.broadcasted_iota(jnp.int32, (8, nbins), 1)
    row_of = lax.broadcasted_iota(jnp.int32, (8, nbins), 0)
    onehot = jnp.zeros((8, nbins), F32)
    weights = []
    for l in range(latents):
        tb = tb_ref[l]
        weights.append(sw_ref[tb])
        onehot = jnp.where((row_of == l) & (bin_of == tb), 1.0, onehot)
    gates = lax.dot_general(onehot.astype(BF16), gate[...], NN, preferred_element_type=F32)
    row8 = lax.broadcasted_iota(jnp.int32, (8, width), 0)
    lat8 = jnp.zeros((8, width), F32)
    for l in range(latents):
        lat8 = jnp.where(row8 == l, weights[l], lat8)
    scale[...] = gates * lat8
    loads[h_load].wait()

    @functools.partial(each, latents)
    def _(l):
        rows = pl.ds(pl.multiple_of(l * per, per), per)
        pltpu.make_async_copy(cot_hbm.at[rows], cot.at[rows], load_sem.at[c_load + l]).wait()
        part = (cot[rows, :].astype(F32) * scale[pl.ds(l, 1), :]).astype(BF16)
        both_g[pl.ds(pl.multiple_of(feats + l * per, per), per), :] = part
        mixed = fold(lax.dot_general(part, rstack[...], NT, preferred_element_type=F32).T)
        left_v[...] += fold(lax.dot_general(split(mixed), head[rows, :], NN, preferred_element_type=F32))

    left = left_v[...]
    for k in range(pairs):
        l_src[k] = left[k * piece : (k + 1) * piece]

    pl.semaphore_wait(barrier, 4 * (n - 1) + 1 + (nx - 1))
    scatter_send(l_src, l_in, A1)

    loads[h_load + 3].wait()
    row_s = lax.broadcasted_iota(jnp.int32, (8, share), 0)

    @functools.partial(each, nx)
    def _(t):
        cols = pl.ds(pl.multiple_of(t * share, 128), share)
        out = jnp.zeros((8, share), F32)
        for l in range(latents):
            rows = pl.ds(l * per, per)
            branch = lax.dot_general(head[rows, :], weight[:, cols], NN, preferred_element_type=F32)
            row = jnp.sum(branch * cot[rows, cols].astype(F32), axis=0, keepdims=True) * weights[l]
            out = jnp.where(row_s == l, row, out)
        t_src[t] = out

    stack_v[rank:, feats:] = jnp.zeros((rank, feats), BF16)
    t_in[x] = t_src[x]

    @functools.partial(each, nx - 1)
    def _(i):
        j = wrap(x + far_first(i, nx), nx)
        remote(t_src.at[j], t_in.at[x], TG, (index, j)).start()

    wait_many(l_in, pairs - 1, A1)
    l_mid[b] = sum_slots(l_in, pairs)
    ring_send(l_mid, A2)

    head_t[...] = head[...].T

    @functools.partial(each, nx)
    def _(t):
        cols = pl.ds(pl.multiple_of(t * share, 128), share)
        for i in range(feats // 128):
            rows = pl.ds(i * 128, 128)
            whole = lax.dot_general(head_t[rows, :], both_g[feats:, cols], NN, preferred_element_type=F32)
            whole = whole + both_g[rows, cols].astype(F32)
            high = whole.astype(BF16)
            merged[rows, cols] = high
            merged[pl.ds(feats + i * 128, 128), cols] = (whole - high.astype(F32)).astype(BF16)

    loads[h_load + 1].wait()
    loads[h_load + 2].wait()
    bin_row = lax.broadcasted_iota(jnp.int32, (nbins, per), 0)
    hist = jnp.zeros((nbins, per), F32)
    for l in range(latents):
        hist = hist + jnp.where(bin_row == bins[l : l + 1, :], weights[l] * loss[l : l + 1, :], 0.0)
    wait_many(t_in, nx - 1, TG)
    lat_sum = sum_slots(t_in, nx)
    bin_s = lax.broadcasted_iota(jnp.int32, (nbins, share), 0)
    spread = jnp.zeros((nbins, share), F32)
    for l in range(latents):
        spread = spread + jnp.where(bin_s == tb_ref[l], lat_sum[l : l + 1, :], 0.0)
    for k in range(pairs):
        g_src[k, :, share:] = hist[k * piece : (k + 1) * piece]
        g_src[k, :, :share] = spread[k * piece : (k + 1) * piece]
    scatter_send(g_src, g_in, G1)

    wait_many(l_mid, n - 1, A2)
    l_all[c * n + a] = sum_slots(l_mid, n) * (1.0 / workers)
    gather_send(l_all, A3)

    @functools.partial(each, latents)
    def _(l):
        grad_o[pl.ds(pl.multiple_of(l * per, per), per), :] = lax.dot_general(
            both_g[pl.ds(pl.multiple_of(feats + l * per, per), per), :], weight[...], NT, preferred_element_type=F32
        ).astype(BF16)

    wait_many(g_in, pairs - 1, G1)
    g_mid[b] = sum_slots(g_in, pairs)
    ring_send(g_mid, G2)

    wait_many(l_all, pairs - 1, A3)
    left = jnp.concatenate([l_all[k] for k in range(pairs)], axis=0)
    high = left.astype(BF16)
    low = (left - high.astype(F32)).astype(BF16)
    stack_v[:rank, :feats] = high
    stack_v[:rank, feats:] = high
    stack_v[rank:, :feats] = low

    def target(i):
        return wrap(x + far_first(i, nx), nx)

    def part_start(i):
        cols = pl.ds(pl.multiple_of(target(i) * share, 128), share)
        term = fold(lax.dot_general(stack_v[...], merged[:, cols], NN, preferred_element_type=F32))
        own_s[i, 0] = term[:half]
        own_s[i, 1] = term[half:]
        remote(own_s.at[i, 1 - c], sib_s.at[i], PAIR + i, sibling).start()

    def part_scatter(i):
        remote(sib_s.at[i], sib_s.at[i], PAIR + i, sibling).wait_recv()
        total = own_s[i, c] + sib_s[i]
        for k in range(n):
            s_src[i, k] = total[k * piece : (k + 1) * piece]
        s_in[i, a] = s_src[i, a]

        @functools.partial(each, n - 1)
        def _(k):
            j = wrap(a + far_first(k, n), n)
            remote(s_src.at[i, j], s_in.at[i, a], FIRST + i, at_a(j, c)).start()

    def part_sum(i):
        wait_many(s_in.at[i], n - 1, FIRST + i)
        total = s_in[i, 0]
        for k in range(1, n):
            total = total + s_in[i, k]
        return total

    each(nx, part_start)
    padded = jnp.concatenate([left, jnp.zeros((128 - rank, share), F32)], axis=0)
    gram[x] = lax.dot_general(left, padded, NT, precision=HIGHEST, preferred_element_type=F32)

    @functools.partial(each, nx - 1)
    def _(i):
        remote(gram.at[x], gram.at[x], GRAM, (index, target(i))).start()

    each(nx, part_scatter)


    @functools.partial(each, nx - 1)
    def _(i):
        s_x[i] = part_sum(i)

        @functools.partial(each, n)
        def _(k):
            j = wrap(b + far_first(k, n), n)
            remote(s_x.at[i], s_xin.at[x * n + b], XX, at_b(j, target(i))).start()

    s_x[nx - 1] = part_sum(nx - 1)
    s_xin[x * n + b] = s_x[nx - 1]

    @functools.partial(each, n - 1)
    def _(k):
        j = wrap(b + far_first(k, n), n)
        remote(s_x.at[nx - 1], s_xin.at[x * n + b], XX, at_b(j)).start()

    wait_many(g_mid, n - 1, G2)
    g_all[c * n + a] = sum_slots(g_mid, n)
    gather_send(g_all, G3)
    groups = rank // 8
    wait_many(gram, nx - 1, GRAM)
    whole = sum_slots(gram, nx)
    eye_r = lax.broadcasted_iota(jnp.int32, (rank, 128), 0)
    eye_c = lax.broadcasted_iota(jnp.int32, (rank, 128), 1)
    whole = jnp.where(eye_c == eye_r + rank, 1.0, whole)
    for g in range(groups):
        chol[g] = whole[8 * g : 8 * g + 8]
    eliminate(chol, 0, groups // 2, 0)
    eliminate(chol, groups // 2, 5 * groups // 8, groups // 2)

    wait_many(s_xin, nx * n - 1, XX)
    s_all[c * n + a] = sum_slots(s_xin, nx * n)
    gather_send(s_all, C5)
    eliminate(chol, 5 * groups // 8, groups, groups // 2)
    turned = [pltpu.roll(chol[g], 128 - rank // 2, 1) for g in range(groups // 2)]
    turned += [chol[g] for g in range(groups // 2, groups)]
    inverse = unscaled_to_inverse(turned, rank)[:, :rank]
    inv_high = inverse.astype(BF16)
    inv_low = (inverse - inv_high.astype(F32)).astype(BF16)
    inv_stack = jnp.concatenate([inv_high, inv_high, inv_low], axis=1)
    basis_o[...] = lax.dot_general(
        inv_stack, jnp.concatenate([high, low, high], axis=0), NN, preferred_element_type=F32
    )
    wait_many(g_all, pairs - 1, G3)
    gates = jnp.concatenate([g_all[k] for k in range(pairs)], axis=0)
    gate_o[...] = gates[:, :share]
    hist_o[...] = jnp.sum(gates[:, share:], axis=1, keepdims=True).T * hist_scale
    wait_many(l_src, pairs - 1, A1, False)
    wait_many(t_src, nx - 1, TG, False)
    wait_many(l_mid, n - 1, A2, False)
    wait_many(l_all, pairs - 1, A3, False)
    wait_many(g_src, pairs - 1, G1, False)

    @functools.partial(each, nx)
    def _(i):
        remote(sib_s.at[i], sib_s.at[i], PAIR + i, sibling).wait_send()
        wait_many(s_src.at[i], n - 1, FIRST + i, False)

    wait_many(gram, nx - 1, GRAM, False)
    wait_many(g_mid, n - 1, G2, False)
    wait_many(s_xin, nx * n - 1, XX, False)
    wait_many(g_all, pairs - 1, G3, False)

    wait_many(s_all, pairs - 1, C5)
    s_whole = jnp.concatenate([s_all[k] for k in range(pairs)], axis=0)
    s_high = s_whole.astype(BF16)
    s_low = (s_whole - s_high.astype(F32)).astype(BF16)
    right_o[...] = lax.dot_general(
        inv_stack, jnp.concatenate([s_high, s_low, s_high], axis=0), NN, preferred_element_type=F32
    ) * (1.0 / workers)
    wait_many(s_all, pairs - 1, C5, False)


def end_kernel(*refs):
    count = len(refs) // 2
    sem = refs[-1]
    copies = [pltpu.make_async_copy(refs[k], refs[count + k], sem.at[k]) for k in range(count)]
    for copy in copies:
        copy.start()
    for copy in copies:
        copy.wait()


def per_device(n, nx, head, weight, cot, err, right, gate, sample, tbins, loss, lbins):
    workers = 2 * n * n
    rank = right.shape[1]
    tokens, feats = head.shape
    width = cot.shape[1]
    latents = tbins.shape[0]
    per = tokens // latents
    nbins = gate.shape[0]
    share = width // nx
    half = rank // 2
    piece = half // n
    pairs = 2 * n
    gwidth = share + per
    vmem = pl.BlockSpec(memory_space=pltpu.VMEM)
    hbm = pl.BlockSpec(memory_space=pltpu.HBM)
    V = pltpu.VMEM
    DMA = pltpu.SemaphoreType.DMA
    out = jax.ShapeDtypeStruct
    operands = (
        tbins, sample, head, weight, cot, err, right.T, gate,
        loss.reshape(latents, per), lbins.reshape(latents, per),
    )
    kinds = (
        ((rank, share), F32),
        ((rank, share), F32),
        ((nbins, share), F32),
        ((1, nbins), F32),
        ((tokens, feats), BF16),
    )
    results = pl.pallas_call(
        functools.partial(main_kernel, n, nx, workers, nbins / (tokens * workers)),
        out_shape=tuple(V(shape, dtype) for shape, dtype in kinds),
        in_specs=[hbm] * 10,
        out_specs=(vmem,) * 5,
        scratch_shapes=[
            pltpu.SMEM(tbins.shape, jnp.int32),
            pltpu.SMEM(sample.shape, F32),
            V(head.shape, BF16),
            V(weight.shape, BF16),
            V(cot.shape, BF16),
            V((rank, width), F32),
            V(gate.shape, BF16),
            V((latents, per), F32),
            V((latents, per), jnp.int32),
            DMA((8 + feats // 128 + latents,)),
            V((feats + tokens, width), BF16),
            V((feats, tokens), BF16),
            V((2 * rank, width), BF16),
            V((8, width), F32),
            V((rank, share), F32),
            V((2 * rank, 2 * feats), BF16),
            V((2 * feats, width), BF16),
            V((nx, 2, half, share), F32),
            V((nx, half, share), F32),
            V((pairs, piece, share), F32),
            V((pairs, piece, share), F32),
            V((n, piece, share), F32),
            V((pairs, piece, share), F32),
            V((pairs, piece, gwidth), F32),
            V((pairs, piece, gwidth), F32),
            V((n, piece, gwidth), F32),
            V((pairs, piece, gwidth), F32),
            V((nx, n, piece, share), F32),
            V((nx, n, piece, share), F32),
            V((nx, piece, share), F32),
            V((nx * n, piece, share), F32),
            V((pairs, piece, share), F32),
            V((nx, 8, share), F32),
            V((nx, 8, share), F32),
            V((nx, rank, 128), F32),
            V((rank // 8, 8, 128), F32),
            DMA((PAIR + 2 * nx,)),
            DMA((PAIR + 2 * nx,)),
        ],
        compiler_params=pltpu.CompilerParams(
            collective_id=0, has_side_effects=True, vmem_limit_bytes=32 * 1024 * 1024
        ),
        name="main",
    )(*[pltpu.with_memory_space_constraint(v, pltpu.HBM) for v in operands])
    new_right, basis, gate_grad, hist, grad = pl.pallas_call(
        end_kernel,
        out_shape=tuple(out(shape, dtype) for shape, dtype in kinds),
        in_specs=[vmem] * 5,
        out_specs=(hbm,) * 5,
        scratch_shapes=[DMA((5,))],
        compiler_params=pltpu.CompilerParams(vmem_limit_bytes=8 * 1024 * 1024),
        name="finish",
    )(*results)
    return grad, basis.T, new_right.T, gate_grad, hist.reshape(nbins)


def solution(mesh):
    n = math.isqrt(mesh.shape["dp"] // 2)
    assert 2 * n * n == mesh.shape["dp"]
    placed = (
        P("dp", "tensor"),
        P("tensor", None),
        P("dp", None),
        P("dp", "tensor", None),
        P(),
        P(),
        P(),
        P("dp"),
        P("dp"),
        P("dp"),
    )
    return jax.shard_map(
        functools.partial(per_device, n, mesh.shape["tensor"]),
        mesh=mesh,
        in_specs=placed,
        out_specs=(P("dp", "tensor"), P("tensor", None), P("tensor", None), P(None, "tensor"), P()),
        check_vma=False,
    )
```

```python
import functools
import math

import jax
import jax.numpy as jnp
from jax import lax
from jax.experimental import pallas as pl
from jax.experimental.pallas import tpu as pltpu
from jax.sharding import PartitionSpec as P

MESH = pl.DeviceIdType.MESH
F32 = jnp.float32
BF16 = jnp.bfloat16
HIGHEST = lax.Precision.HIGHEST
NN = (((1,), (0,)), ((), ()))
NT = (((1,), (1,)), ((), ()))


def split(x):
    high = x.astype(BF16)
    low = (x - high.astype(F32)).astype(BF16)
    return jnp.concatenate([high, low], axis=0)


def fold(x):
    half = x.shape[0] // 2
    return x[:half] + x[half:]


def eliminate(ref, begin, end, low_group):
    groups, _, width = ref.shape
    active = range(low_group, groups)
    sub = lax.broadcasted_iota(jnp.int32, (8, width), 0)

    def wide(x, j):
        return jnp.broadcast_to(x[:, j : j + 1], (8, width))

    def block(k, carry):
        own = ref[k]
        rows = {g: ref[g] for g in active}
        for r in range(0, 8, 2):
            first, second = wide(own, r), wide(own, r + 1)
            aa = first[r : r + 1]
            ab = first[r + 1 : r + 2]
            bb = second[r + 1 : r + 2]
            inverse = 1.0 / (aa * bb - ab * ab)
            top = own[r : r + 1]
            low = own[r + 1 : r + 2]
            one = jnp.broadcast_to((bb * inverse) * top - (ab * inverse) * low, (8, width))
            two = jnp.broadcast_to((aa * inverse) * low - (ab * inverse) * top, (8, width))
            if r < 6:
                own = own - jnp.where(sub > r + 1, first * one + second * two, 0.0)
            for g in active:
                change = wide(rows[g], r) * one + wide(rows[g], r + 1) * two
                rows[g] = rows[g] - jnp.where(g > k, change, 0.0)
        for g in active:
            ref[g] = pltpu.roll(jnp.where(g == k, own, rows[g]), width - 8, 1)
        return carry

    lax.fori_loop(begin, end, block, 0)


def unscaled_to_inverse(rows, rank):
    out = []
    width = rows[0].shape[1]
    lane = lax.broadcasted_iota(jnp.int32, (8, width), 1)
    sub = lax.broadcasted_iota(jnp.int32, (8, width), 0)
    odd = lax.rem(sub, 2) == 1
    for g, x in enumerate(rows):
        row = sub + (8 * g + rank)
        before = jnp.concatenate([x[7:], x[:7]], axis=0)
        over = jnp.sum(jnp.where(lane == row - 1, before, 0.0), axis=1, keepdims=True)
        off = jnp.sum(jnp.where(lane == row - 1, x, 0.0), axis=1, keepdims=True)
        x = jnp.where(odd, x - (off / jnp.where(odd[:, :1], over, 1.0)) * before, x)
        diag = jnp.sum(jnp.where(lane == row, x, 0.0), axis=1, keepdims=True)
        out.append(x / jnp.sqrt(diag))
    return jnp.concatenate(out, axis=0)


def far_first(i, n):
    return n // 2 + ((i + 1) // 2) * (1 - 2 * (i % 2))


def each(count, step):
    def body(i, carry):
        step(i)
        return carry

    lax.fori_loop(0, count, body, 0)


def wrap(value, n):
    return jnp.where(value >= n, value - n, value)


A1, TG, A2, A3, G1, G2, G3, GRAM, XX, C5, PAIR = range(11)


def main_kernel(
    n, nx, workers, hist_scale,
    tb_hbm, sw_hbm, head_hbm, weight_hbm, cot_hbm, err_hbm, right_hbm, gate_hbm, loss_hbm, bins_hbm,
    right_o, basis_o, gate_o, hist_o, grad_o,
    tb_ref, sw_ref, head, weight, cot, right, gate, loss, bins, load_sem,
    both_g, head_t, rstack, scale, left_v, stack_v, merged, own_s, sib_s,
    l_src, l_in, l_mid, l_all,
    g_src, g_in, g_mid, g_all,
    s_src, s_in, s_x, s_xin, s_all,
    t_src, t_in, gram, chol,
    ssem, rsem,
):
    rank = right.shape[0]
    tokens, feats = head.shape
    width = cot.shape[1]
    latents, per = loss.shape
    nbins = gate.shape[0]
    share = width // nx
    half = rank // 2
    piece = half // n
    pairs = 2 * n
    FIRST = PAIR + nx

    index = lax.axis_index("dp")
    x = lax.axis_index("tensor")
    c = lax.rem(index, 2)
    y = lax.rem(index // 2, n)
    z = index // (2 * n)

    def at_z(j, core):
        return ((j * n + y) * 2 + core, x)

    def at_y(j, core):
        return ((z * n + j) * 2 + core, x)

    a = jnp.where(c == 0, z, y)
    b = jnp.where(c == 0, y, z)

    a_step = jnp.where(c == 0, 2 * n, 2)
    a_base = jnp.where(c == 0, 2 * y, 2 * n * z)
    b_step = jnp.where(c == 0, 2, 2 * n)
    b_base = jnp.where(c == 0, 2 * n * z, 2 * y) + c

    def at_a(j, core):
        return (j * a_step + a_base + core, x)

    def at_b(j, t=x):
        return (j * b_step + b_base, t)

    sibling = (index + 1 - 2 * c, x)

    barrier = pltpu.get_barrier_semaphore()

    def greet(device):
        pl.semaphore_signal(barrier, inc=1, device_id=device, device_id_type=MESH)

    @functools.partial(each, n - 1)
    def _(i):
        k = far_first(i, n)
        jz = wrap(z + k, n)
        jy = wrap(y + k, n)
        for core in (0, 1):
            greet(at_z(jz, core))
            greet(at_y(jy, core))

    greet(sibling)

    @functools.partial(each, nx - 1)
    def _(i):
        greet((index, wrap(x + far_first(i, nx), nx)))

    wanted = [(right_hbm, right), (tb_hbm, tb_ref), (sw_hbm, sw_ref), (gate_hbm, gate)]
    for i in range(feats // 128):
        rows = pl.ds(i * 128, 128)
        wanted.append((err_hbm.at[0, rows], both_g.at[rows]))
    for l in range(latents):
        rows = pl.ds(l * per, per)
        wanted.append((cot_hbm.at[rows], cot.at[rows]))
    wanted += [(head_hbm, head), (loss_hbm, loss), (bins_hbm, bins), (weight_hbm, weight)]
    loads = []
    for k, (src, dst) in enumerate(wanted):
        loads.append(pltpu.make_async_copy(src, dst, load_sem.at[k]))
        loads[-1].start()
    e_load = 4
    c_load = e_load + feats // 128
    h_load = c_load + latents

    def remote(src, dst, phase, device):
        return pltpu.make_async_remote_copy(
            src_ref=src, dst_ref=dst, send_sem=ssem.at[phase], recv_sem=rsem.at[phase],
            device_id=device, device_id_type=MESH,
        )

    def scatter_send(src, dst, phase):
        @functools.partial(each, n - 1)
        def _(i):
            k = far_first(i, n)
            jz = wrap(z + k, n)
            jy = wrap(y + k, n)
            remote(src.at[jz], dst.at[z * 2 + c], phase, at_z(jz, 0)).start()
            remote(src.at[n + jy], dst.at[y * 2 + c], phase, at_y(jy, 1)).start()

        @pl.when(c == 1)
        def _():
            remote(src.at[z], dst.at[z * 2 + 1], phase, sibling).start()

        @pl.when(c == 0)
        def _():
            remote(src.at[n + y], dst.at[y * 2], phase, sibling).start()

        dst[a * 2 + c] = src[c * n + a]

    def wait_many(ref, count, phase, recv=True):
        part = ref.at[pl.ds(0, count)]
        copy = remote(part, part, phase, sibling)
        if recv:
            copy.wait_recv()
        else:
            copy.wait_send()

    def sum_slots(ref, count):
        out = ref[0]
        for k in range(1, count):
            out = out + ref[k]
        return out

    def ring_send(ref, phase):
        @functools.partial(each, n - 1)
        def _(i):
            remote(ref.at[b], ref.at[b], phase, at_b(wrap(b + far_first(i, n), n))).start()

    def gather_send(ref, phase):
        mine = c * n + a

        @functools.partial(each, n - 1)
        def _(i):
            j = wrap(a + far_first(i, n), n)
            for core in (0, 1):
                remote(ref.at[mine], ref.at[mine], phase, at_a(j, core)).start()

        remote(ref.at[mine], ref.at[mine], phase, sibling).start()

    loads[0].wait()
    rstack[...] = split(right[...])

    @functools.partial(each, feats // 128)
    def _(i):
        rows = pl.ds(pl.multiple_of(i * 128, 128), 128)
        pltpu.make_async_copy(err_hbm.at[0, rows], both_g.at[rows], load_sem.at[e_load + i]).wait()
        term = lax.dot_general(both_g[rows, :], rstack[...], NT, preferred_element_type=F32)
        left_v[:, rows] = fold(term.T)

    for k in (1, 2, 3):
        loads[k].wait()
    bin_of = lax.broadcasted_iota(jnp.int32, (8, nbins), 1)
    row_of = lax.broadcasted_iota(jnp.int32, (8, nbins), 0)
    onehot = jnp.zeros((8, nbins), F32)
    weights = []
    for l in range(latents):
        tb = tb_ref[l]
        weights.append(sw_ref[tb])
        onehot = jnp.where((row_of == l) & (bin_of == tb), 1.0, onehot)
    gates = lax.dot_general(onehot.astype(BF16), gate[...], NN, preferred_element_type=F32)
    row8 = lax.broadcasted_iota(jnp.int32, (8, width), 0)
    lat8 = jnp.zeros((8, width), F32)
    for l in range(latents):
        lat8 = jnp.where(row8 == l, weights[l], lat8)
    scale[...] = gates * lat8
    loads[h_load].wait()

    @functools.partial(each, latents)
    def _(l):
        rows = pl.ds(pl.multiple_of(l * per, per), per)
        pltpu.make_async_copy(cot_hbm.at[rows], cot.at[rows], load_sem.at[c_load + l]).wait()
        part = (cot[rows, :].astype(F32) * scale[pl.ds(l, 1), :]).astype(BF16)
        both_g[pl.ds(pl.multiple_of(feats + l * per, per), per), :] = part
        mixed = fold(lax.dot_general(part, rstack[...], NT, preferred_element_type=F32).T)
        left_v[...] += fold(lax.dot_general(split(mixed), head[rows, :], NN, preferred_element_type=F32))

    left = left_v[...]
    for k in range(pairs):
        l_src[k] = left[k * piece : (k + 1) * piece]

    pl.semaphore_wait(barrier, 4 * (n - 1) + 1 + (nx - 1))
    scatter_send(l_src, l_in, A1)

    loads[h_load + 3].wait()
    row_s = lax.broadcasted_iota(jnp.int32, (8, share), 0)

    @functools.partial(each, nx)
    def _(t):
        cols = pl.ds(pl.multiple_of(t * share, 128), share)
        out = jnp.zeros((8, share), F32)
        for l in range(latents):
            rows = pl.ds(l * per, per)
            branch = lax.dot_general(head[rows, :], weight[:, cols], NN, preferred_element_type=F32)
            row = jnp.sum(branch * cot[rows, cols].astype(F32), axis=0, keepdims=True) * weights[l]
            out = jnp.where(row_s == l, row, out)
        t_src[t] = out

    stack_v[rank:, feats:] = jnp.zeros((rank, feats), BF16)
    t_in[x] = t_src[x]

    @functools.partial(each, nx - 1)
    def _(i):
        j = wrap(x + far_first(i, nx), nx)
        remote(t_src.at[j], t_in.at[x], TG, (index, j)).start()

    wait_many(l_in, pairs - 1, A1)
    l_mid[b] = sum_slots(l_in, pairs)
    ring_send(l_mid, A2)

    head_t[...] = head[...].T

    @functools.partial(each, nx)
    def _(t):
        cols = pl.ds(pl.multiple_of(t * share, 128), share)
        for i in range(feats // 128):
            rows = pl.ds(i * 128, 128)
            whole = lax.dot_general(head_t[rows, :], both_g[feats:, cols], NN, preferred_element_type=F32)
            whole = whole + both_g[rows, cols].astype(F32)
            high = whole.astype(BF16)
            merged[rows, cols] = high
            merged[pl.ds(feats + i * 128, 128), cols] = (whole - high.astype(F32)).astype(BF16)

    loads[h_load + 1].wait()
    loads[h_load + 2].wait()
    bin_row = lax.broadcasted_iota(jnp.int32, (nbins, per), 0)
    hist = jnp.zeros((nbins, per), F32)
    for l in range(latents):
        hist = hist + jnp.where(bin_row == bins[l : l + 1, :], weights[l] * loss[l : l + 1, :], 0.0)
    wait_many(t_in, nx - 1, TG)
    lat_sum = sum_slots(t_in, nx)
    bin_s = lax.broadcasted_iota(jnp.int32, (nbins, share), 0)
    spread = jnp.zeros((nbins, share), F32)
    for l in range(latents):
        spread = spread + jnp.where(bin_s == tb_ref[l], lat_sum[l : l + 1, :], 0.0)
    for k in range(pairs):
        g_src[k, :, share:] = hist[k * piece : (k + 1) * piece]
        g_src[k, :, :share] = spread[k * piece : (k + 1) * piece]
    scatter_send(g_src, g_in, G1)

    wait_many(l_mid, n - 1, A2)
    l_all[c * n + a] = sum_slots(l_mid, n) * (1.0 / workers)
    gather_send(l_all, A3)

    @functools.partial(each, latents)
    def _(l):
        grad_o[pl.ds(pl.multiple_of(l * per, per), per), :] = lax.dot_general(
            both_g[pl.ds(pl.multiple_of(feats + l * per, per), per), :], weight[...], NT, preferred_element_type=F32
        ).astype(BF16)

    wait_many(g_in, pairs - 1, G1)
    g_mid[b] = sum_slots(g_in, pairs)
    ring_send(g_mid, G2)

    wait_many(l_all, pairs - 1, A3)
    left = jnp.concatenate([l_all[k] for k in range(pairs)], axis=0)
    high = left.astype(BF16)
    low = (left - high.astype(F32)).astype(BF16)
    stack_v[:rank, :feats] = high
    stack_v[:rank, feats:] = high
    stack_v[rank:, :feats] = low

    def target(i):
        return wrap(x + far_first(i, nx), nx)

    def part_start(i):
        cols = pl.ds(pl.multiple_of(target(i) * share, 128), share)
        term = fold(lax.dot_general(stack_v[...], merged[:, cols], NN, preferred_element_type=F32))
        own_s[i, 0] = term[:half]
        own_s[i, 1] = term[half:]
        remote(own_s.at[i, 1 - c], sib_s.at[i], PAIR + i, sibling).start()

    def part_scatter(i):
        remote(sib_s.at[i], sib_s.at[i], PAIR + i, sibling).wait_recv()
        total = own_s[i, c] + sib_s[i]
        for k in range(n):
            s_src[i, k] = total[k * piece : (k + 1) * piece]
        s_in[i, a] = s_src[i, a]

        @functools.partial(each, n - 1)
        def _(k):
            j = wrap(a + far_first(k, n), n)
            remote(s_src.at[i, j], s_in.at[i, a], FIRST + i, at_a(j, c)).start()

    def part_sum(i):
        wait_many(s_in.at[i], n - 1, FIRST + i)
        total = s_in[i, 0]
        for k in range(1, n):
            total = total + s_in[i, k]
        return total

    each(nx, part_start)
    padded = jnp.concatenate([left, jnp.zeros((128 - rank, share), F32)], axis=0)
    gram[x] = lax.dot_general(left, padded, NT, precision=HIGHEST, preferred_element_type=F32)

    @functools.partial(each, nx - 1)
    def _(i):
        remote(gram.at[x], gram.at[x], GRAM, (index, target(i))).start()

    each(nx, part_scatter)
    groups = rank // 8
    wait_many(gram, nx - 1, GRAM)
    whole = sum_slots(gram, nx)
    eye_r = lax.broadcasted_iota(jnp.int32, (rank, 128), 0)
    eye_c = lax.broadcasted_iota(jnp.int32, (rank, 128), 1)
    whole = jnp.where(eye_c == eye_r + rank, 1.0, whole)
    for g in range(groups):
        chol[g] = whole[8 * g : 8 * g + 8]
    eliminate(chol, 0, groups // 4, 0)

    @functools.partial(each, nx - 1)
    def _(i):
        s_x[i] = part_sum(i)

        @functools.partial(each, n)
        def _(k):
            j = wrap(b + far_first(k, n), n)
            remote(s_x.at[i], s_xin.at[x * n + b], XX, at_b(j, target(i))).start()

    s_x[nx - 1] = part_sum(nx - 1)
    s_xin[x * n + b] = s_x[nx - 1]

    @functools.partial(each, n - 1)
    def _(k):
        j = wrap(b + far_first(k, n), n)
        remote(s_x.at[nx - 1], s_xin.at[x * n + b], XX, at_b(j)).start()

    wait_many(g_mid, n - 1, G2)
    g_all[c * n + a] = sum_slots(g_mid, n)
    gather_send(g_all, G3)
    eliminate(chol, groups // 4, groups // 2, 0)
    eliminate(chol, groups // 2, 5 * groups // 8, groups // 2)

    wait_many(s_xin, nx * n - 1, XX)
    s_all[c * n + a] = sum_slots(s_xin, nx * n)
    gather_send(s_all, C5)
    eliminate(chol, 5 * groups // 8, groups, groups // 2)
    turned = [pltpu.roll(chol[g], 128 - rank // 2, 1) for g in range(groups // 2)]
    turned += [chol[g] for g in range(groups // 2, groups)]
    inverse = unscaled_to_inverse(turned, rank)[:, :rank]
    inv_high = inverse.astype(BF16)
    inv_low = (inverse - inv_high.astype(F32)).astype(BF16)
    inv_stack = jnp.concatenate([inv_high, inv_high, inv_low], axis=1)
    basis_o[...] = lax.dot_general(
        inv_stack, jnp.concatenate([high, low, high], axis=0), NN, preferred_element_type=F32
    )
    wait_many(g_all, pairs - 1, G3)
    gates = jnp.concatenate([g_all[k] for k in range(pairs)], axis=0)
    gate_o[...] = gates[:, :share]
    hist_o[...] = jnp.sum(gates[:, share:], axis=1, keepdims=True).T * hist_scale
    wait_many(l_src, pairs - 1, A1, False)
    wait_many(t_src, nx - 1, TG, False)
    wait_many(l_mid, n - 1, A2, False)
    wait_many(l_all, pairs - 1, A3, False)
    wait_many(g_src, pairs - 1, G1, False)

    @functools.partial(each, nx)
    def _(i):
        remote(sib_s.at[i], sib_s.at[i], PAIR + i, sibling).wait_send()
        wait_many(s_src.at[i], n - 1, FIRST + i, False)

    wait_many(gram, nx - 1, GRAM, False)
    wait_many(g_mid, n - 1, G2, False)
    wait_many(s_xin, nx * n - 1, XX, False)
    wait_many(g_all, pairs - 1, G3, False)

    wait_many(s_all, pairs - 1, C5)
    s_whole = jnp.concatenate([s_all[k] for k in range(pairs)], axis=0)
    s_high = s_whole.astype(BF16)
    s_low = (s_whole - s_high.astype(F32)).astype(BF16)
    right_o[...] = lax.dot_general(
        inv_stack, jnp.concatenate([s_high, s_low, s_high], axis=0), NN, preferred_element_type=F32
    ) * (1.0 / workers)
    wait_many(s_all, pairs - 1, C5, False)


def end_kernel(*refs):
    count = len(refs) // 2
    sem = refs[-1]
    copies = [pltpu.make_async_copy(refs[k], refs[count + k], sem.at[k]) for k in range(count)]
    for copy in copies:
        copy.start()
    for copy in copies:
        copy.wait()


def per_device(n, nx, head, weight, cot, err, right, gate, sample, tbins, loss, lbins):
    workers = 2 * n * n
    rank = right.shape[1]
    tokens, feats = head.shape
    width = cot.shape[1]
    latents = tbins.shape[0]
    per = tokens // latents
    nbins = gate.shape[0]
    share = width // nx
    half = rank // 2
    piece = half // n
    pairs = 2 * n
    gwidth = share + per
    vmem = pl.BlockSpec(memory_space=pltpu.VMEM)
    hbm = pl.BlockSpec(memory_space=pltpu.HBM)
    V = pltpu.VMEM
    DMA = pltpu.SemaphoreType.DMA
    out = jax.ShapeDtypeStruct
    operands = (
        tbins, sample, head, weight, cot, err, right.T, gate,
        loss.reshape(latents, per), lbins.reshape(latents, per),
    )
    kinds = (
        ((rank, share), F32),
        ((rank, share), F32),
        ((nbins, share), F32),
        ((1, nbins), F32),
        ((tokens, feats), BF16),
    )
    results = pl.pallas_call(
        functools.partial(main_kernel, n, nx, workers, nbins / (tokens * workers)),
        out_shape=tuple(V(shape, dtype) for shape, dtype in kinds),
        in_specs=[hbm] * 10,
        out_specs=(vmem,) * 5,
        scratch_shapes=[
            pltpu.SMEM(tbins.shape, jnp.int32),
            pltpu.SMEM(sample.shape, F32),
            V(head.shape, BF16),
            V(weight.shape, BF16),
            V(cot.shape, BF16),
            V((rank, width), F32),
            V(gate.shape, BF16),
            V((latents, per), F32),
            V((latents, per), jnp.int32),
            DMA((8 + feats // 128 + latents,)),
            V((feats + tokens, width), BF16),
            V((feats, tokens), BF16),
            V((2 * rank, width), BF16),
            V((8, width), F32),
            V((rank, share), F32),
            V((2 * rank, 2 * feats), BF16),
            V((2 * feats, width), BF16),
            V((nx, 2, half, share), F32),
            V((nx, half, share), F32),
            V((pairs, piece, share), F32),
            V((pairs, piece, share), F32),
            V((n, piece, share), F32),
            V((pairs, piece, share), F32),
            V((pairs, piece, gwidth), F32),
            V((pairs, piece, gwidth), F32),
            V((n, piece, gwidth), F32),
            V((pairs, piece, gwidth), F32),
            V((nx, n, piece, share), F32),
            V((nx, n, piece, share), F32),
            V((nx, piece, share), F32),
            V((nx * n, piece, share), F32),
            V((pairs, piece, share), F32),
            V((nx, 8, share), F32),
            V((nx, 8, share), F32),
            V((nx, rank, 128), F32),
            V((rank // 8, 8, 128), F32),
            DMA((PAIR + 2 * nx,)),
            DMA((PAIR + 2 * nx,)),
        ],
        compiler_params=pltpu.CompilerParams(
            collective_id=0, has_side_effects=True, vmem_limit_bytes=32 * 1024 * 1024
        ),
        name="main",
    )(*[pltpu.with_memory_space_constraint(v, pltpu.HBM) for v in operands])
    new_right, basis, gate_grad, hist, grad = pl.pallas_call(
        end_kernel,
        out_shape=tuple(out(shape, dtype) for shape, dtype in kinds),
        in_specs=[vmem] * 5,
        out_specs=(hbm,) * 5,
        scratch_shapes=[DMA((5,))],
        compiler_params=pltpu.CompilerParams(vmem_limit_bytes=8 * 1024 * 1024),
        name="finish",
    )(*results)
    return grad, basis.T, new_right.T, gate_grad, hist.reshape(nbins)


def solution(mesh):
    n = math.isqrt(mesh.shape["dp"] // 2)
    assert 2 * n * n == mesh.shape["dp"]
    placed = (
        P("dp", "tensor"),
        P("tensor", None),
        P("dp", None),
        P("dp", "tensor", None),
        P(),
        P(),
        P(),
        P("dp"),
        P("dp"),
        P("dp"),
    )
    return jax.shard_map(
        functools.partial(per_device, n, mesh.shape["tensor"]),
        mesh=mesh,
        in_specs=placed,
        out_specs=(P("dp", "tensor"), P("tensor", None), P("tensor", None), P(None, "tensor"), P()),
        check_vma=False,
    )
```
